32 devices in a mesh: groups: 2 (over y), row: 4 (over z), col: 2 (over x), sub: 2 (over core).
Axes of the slice: x: 2, y: 2, z: 4, core: 2. Of those that a mesh axis runs over, the one named last changes fastest.
Arguments:
- query_acts: bfloat16 [64, 128, 4096], P(('groups', 'col', 'sub'), None, 'row'), parts along dimension 0, may hold values from -6 to 6
- query_grads: bfloat16 [64, 128, 4096], P(('groups', 'col', 'sub'), None, 'row'), parts along dimension 0, may hold values from -0.5390625 to 0.5390625
- proj_in: bfloat16 [4096, 128], P('row'), may hold values from -0.09375 to 0.09375
- proj_out: bfloat16 [4096, 128], P('row'), may hold values from -0.09375 to 0.09375
- inverse_gram: float32 [16384, 16384], P('row', ('col', 'sub')), may hold values from -0.01 to 2.01, as said below
- store_slab: bfloat16 [2048, 16384], P(('groups', 'col'), ('row', 'sub')), parts along dimension 0, may hold values from -0.046875 to 0.046875
Outputs:
- scores: float32 [64, 1024], P('groups', 'col'), parts along dimension 0
The draws below stay inside these ranges and needn't reach their ends.
There are 2 independent parts, one for each index of `groups`. The reference program is written for one: setup_inputs(seed, part) draws one part's arguments, and reference() takes and returns one part's arrays. A program takes and returns all parts, laid end to end along the dimension named above; an argument that names none is the same for every part. Nothing has to cross between parts.
Inputs may be any that keep to these rules, and one draw needn't show every extreme that they name: inverse_gram is symmetric.
All inputs are finite; a program needn't handle non-finite values.
Results may differ from the reference program's by a relative error of at most 0.0029.
Values may be sent and summed in bfloat16 or wider, within the bound.
No kernel may reach another device: no remote copies, remote signals or barrier semaphores. Data moves between devices by JAX's collectives and lax.ppermute only.
A program may use at most 128 MiB of HBM per device.

```python
import math
import jax
import jax.numpy as jnp
from jax import lax

D = 4096
K_IN = 128
K_OUT = 128
Q = 32
S = 128
F = 16384
E = 1024


def draw_inverse_gram(key, part):
    feature_count = K_IN * K_OUT
    first_key, second_key = jax.random.split(jax.random.fold_in(key, 11))
    noise = jax.random.uniform(first_key, (feature_count, feature_count), jnp.float32, -1.0, 1.0)
    symmetric = (noise + noise.T) * 0.005
    diagonal = jnp.exp(jax.random.uniform(second_key, (feature_count,), jnp.float32, math.log(0.5), math.log(2.0)))
    positions = jnp.arange(feature_count)
    return symmetric.at[positions, positions].add(diagonal)


def block_levels(own_key, extent, cuts, low, top_value):
    gain = 1.0
    for position, shards_of in cuts:
        steps = jax.random.uniform(jax.random.fold_in(jax.random.fold_in(own_key, 6), position), (shards_of,), jnp.float32, low / len(cuts), top_value / len(cuts))
        gain = gain * jnp.repeat(jnp.exp(steps), extent[position] // shards_of).reshape((-1,) + (1,) * (len(extent) - 1 - position))
    return gain


def bell_draw(key, dims, deviation, reach, pieces=(), kind=jnp.bfloat16):
    gain = block_levels(key, dims, pieces, -0.22, 0.18) if pieces else 1.0
    entries = jax.random.normal(key, dims, jnp.float32) * deviation * gain
    return jnp.minimum(jnp.maximum(entries, -reach), reach).astype(kind)


def setup_inputs(seed: int = 0, part: int = 0) -> dict:
    key_of = jax.random.split(jax.random.key(seed), 7)
    part_splits = jax.random.split(jax.random.fold_in(key_of[6], part), 7)
    return {
        "query_acts": bell_draw(part_splits[0], (Q, S, D), 1.0, 6.0, ((0, 4), (2, 4))),
        "query_grads": bell_draw(part_splits[1], (Q, S, D), 0.09, 0.5390625, ((0, 4), (2, 4))),
        "proj_in": bell_draw(key_of[2], (D, K_IN), D ** -0.5, 0.09375, ((0, 4),)),
        "proj_out": bell_draw(key_of[3], (D, K_OUT), D ** -0.5, 0.09375, ((0, 4),)),
        "inverse_gram": draw_inverse_gram(jax.random.fold_in(key_of[6], 71), part),
        "store_slab": bell_draw(part_splits[5], (E, F), F ** -0.5, 0.046875, ((0, 2), (1, 8))),
    }


def reference(query_acts, query_grads, proj_in, proj_out, inverse_gram, store_slab):
    act_proj = jnp.einsum("qtd,dk->qtk", query_acts.astype(jnp.float32), proj_in.astype(jnp.float32), precision=lax.Precision.HIGHEST)
    grad_proj = jnp.einsum("qtd,dk->qtk", query_grads.astype(jnp.float32), proj_out.astype(jnp.float32), precision=lax.Precision.HIGHEST)
    kron_feats = jnp.einsum("qta,qtb->qab", act_proj, grad_proj, precision=lax.Precision.HIGHEST)
    kron_feats = kron_feats.reshape(kron_feats.shape[0], -1)
    precond = jnp.dot(kron_feats, inverse_gram, precision=lax.Precision.HIGHEST)
    precond_b = precond.astype(jnp.bfloat16)
    return jnp.dot(precond_b, store_slab.T, preferred_element_type=jnp.float32)
```

```python
import jax
import jax.numpy as jnp
from jax import lax
from jax.experimental import pallas as pl
from jax.experimental.pallas import tpu as pltpu
from jax.sharding import PartitionSpec as P

HIGHEST = lax.Precision.HIGHEST
CELL = ("row", "col", "sub")


def plain_body(query_acts, query_grads, proj_in, proj_out, inverse_gram, store_slab):
    row_count = lax.axis_size("row")
    row_index = lax.axis_index("row")
    sub_index = lax.axis_index("sub")
    in_width = proj_in.shape[1]
    act_part = jnp.einsum("qtd,dk->qtk", query_acts, proj_in, preferred_element_type=jnp.float32)
    grad_part = jnp.einsum("qtd,dk->qtk", query_grads, proj_out, preferred_element_type=jnp.float32)
    store_width = store_slab.shape[1]
    row_block = in_width // row_count
    act_whole, grad_proj = lax.psum((act_part, grad_part), "row")
    act_proj = lax.dynamic_slice_in_dim(act_whole, row_index * row_block, row_block, 2)
    kron_part = jnp.einsum("qta,qtb->qab", act_proj, grad_proj, precision=HIGHEST)
    kron_feats = lax.all_gather(kron_part, ("col", "sub"), axis=0, tiled=True)
    features_flat = kron_feats.reshape(kron_feats.shape[0], -1)
    precond_part = jnp.dot(features_flat, inverse_gram, precision=HIGHEST)
    precond_block = lax.psum(precond_part, "row").astype(jnp.bfloat16)
    precond_full = lax.all_gather(precond_block, ("col", "sub"), axis=1, tiled=True)
    store_start = (row_index * lax.axis_size("sub") + sub_index) * store_width
    precond_mine = lax.dynamic_slice_in_dim(precond_full, store_start, store_width, 1)
    score_part = lax.dot_general(
        precond_mine, store_slab, (((1,), (1,)), ((), ())), preferred_element_type=jnp.float32
    )
    return lax.psum(score_part, ("row", "sub"))


def gram_kernel(feats_ref, gram_ref, out_ref):
    queries = out_ref.shape[0]
    block = gram_ref[...]
    high = block.astype(jnp.bfloat16)
    low = (block - high.astype(jnp.float32)).astype(jnp.bfloat16)
    feats = feats_ref[...]
    dims = (((1,), (1,)), ((), ()))
    part = lax.dot_general(high, feats, dims, preferred_element_type=jnp.float32)
    part += lax.dot_general(low, feats, dims, preferred_element_type=jnp.float32)
    out_ref[...] = (part[:, :queries] + part[:, queries:]).T


def gram_product(features, inverse_gram, row_tile=256):
    queries, width = features.shape
    rows = inverse_gram.shape[0]
    row_tile = min(row_tile, rows)
    high = features.astype(jnp.bfloat16)
    low = (features - high.astype(jnp.float32)).astype(jnp.bfloat16)
    both = jnp.concatenate([high, low], axis=0)
    return pl.pallas_call(
        gram_kernel,
        grid=(rows // row_tile,),
        in_specs=[
            pl.BlockSpec((2 * queries, width), lambda i: (0, 0)),
            pl.BlockSpec((row_tile, width), lambda i: (i, 0)),
        ],
        out_specs=pl.BlockSpec((queries, row_tile), lambda i: (0, i)),
        out_shape=jax.ShapeDtypeStruct((queries, rows), jnp.float32),
        compiler_params=pltpu.CompilerParams(vmem_limit_bytes=40 * 2**20),
        cost_estimate=pl.CostEstimate(
            flops=8 * queries * rows * width, bytes_accessed=4 * rows * width, transcendentals=0
        ),
        name="gram_product",
    )(both, inverse_gram)


def swap(array, axis):
    size = lax.axis_size(axis)
    return [lax.ppermute(array, axis, [(i, (i + k) % size) for i in range(size)]) for k in range(1, size)]


def body(query_acts, query_grads, proj_in, proj_out, inverse_gram, store_slab):
    row_count = lax.axis_size("row")
    sub_count = lax.axis_size("sub")
    column_count = lax.axis_size("col") * sub_count
    sub_index = lax.axis_index("sub")
    queries, tokens = query_acts.shape[:2]
    own = queries // row_count
    act_part = jnp.einsum("qtd,dk->qtk", query_acts, proj_in, preferred_element_type=jnp.float32)
    grad_part = jnp.einsum("qtd,dk->qtk", query_grads, proj_out, preferred_element_type=jnp.float32)
    both = jnp.stack([act_part, grad_part], 1).reshape(row_count, own, 2, tokens, -1)
    both = lax.all_to_all(both, "row", 0, 0).sum(0)
    kron = jnp.einsum("qta,qtb->qab", both[:, 0], both[:, 1], precision=HIGHEST)
    in_width = kron.shape[1]
    blocks = kron.reshape(own, column_count, in_width // column_count, -1).swapaxes(0, 1)
    blocks = jnp.broadcast_to(blocks[None], (row_count,) + blocks.shape)
    blocks = blocks.reshape((row_count * column_count,) + blocks.shape[2:])
    feats = lax.all_to_all(blocks, CELL, 0, 0)
    feats = feats.reshape(row_count, column_count, own, -1).swapaxes(0, 1).reshape(queries * column_count, -1)
    part = gram_product(feats, inverse_gram)
    width = store_slab.shape[1]
    part = part.reshape(part.shape[0], sub_count, width).swapaxes(0, 1)
    part = lax.all_to_all(part, "sub", 0, 0).sum(0)
    total = part
    for other in swap(part, "col"):
        total = total + other
    scores = lax.dot_general(
        total.astype(jnp.bfloat16), store_slab, (((1,), (1,)), ((), ())), preferred_element_type=jnp.float32
    )
    ring = ("row", "sub")
    count = row_count * sub_count
    pieces = lax.all_to_all(scores.reshape(count, -1, scores.shape[1]), ring, 0, 0).sum(0)
    whole = lax.all_to_all(jnp.broadcast_to(pieces[None], (count,) + pieces.shape), ring, 0, 0)
    return whole.reshape(scores.shape)


def solution(mesh):
    shape = mesh.shape
    def chosen(query_acts, *rest):
        queries = query_acts.shape[0] // (shape["groups"] * shape["col"] * shape["sub"])
        chosen_body = plain_body if queries % shape["row"] else body
        return jax.shard_map(
            chosen_body,
            mesh=mesh,
            in_specs=(
                P(("groups", "col", "sub"), None, "row"),
                P(("groups", "col", "sub"), None, "row"),
                P("row", None),
                P("row", None),
                P("row", ("col", "sub")),
                P(("groups", "col"), ("row", "sub")),
            ),
            out_specs=P("groups", "col"),
            check_vma=False,
        )(query_acts, *rest)

    return chosen
```

```python
import jax
import jax.numpy as jnp
from jax import lax
from jax.experimental import pallas as pl
from jax.experimental.pallas import tpu as pltpu
from jax.sharding import PartitionSpec as P

HIGHEST = lax.Precision.HIGHEST
CELL = ("row", "col", "sub")


def plain_body(query_acts, query_grads, proj_in, proj_out, inverse_gram, store_slab):
    row_count = lax.axis_size("row")
    row_index = lax.axis_index("row")
    sub_index = lax.axis_index("sub")
    in_width = proj_in.shape[1]
    act_part = jnp.einsum("qtd,dk->qtk", query_acts, proj_in, preferred_element_type=jnp.float32)
    grad_part = jnp.einsum("qtd,dk->qtk", query_grads, proj_out, preferred_element_type=jnp.float32)
    store_width = store_slab.shape[1]
    row_block = in_width // row_count
    act_whole, grad_proj = lax.psum((act_part, grad_part), "row")
    act_proj = lax.dynamic_slice_in_dim(act_whole, row_index * row_block, row_block, 2)
    kron_part = jnp.einsum("qta,qtb->qab", act_proj, grad_proj, precision=HIGHEST)
    kron_feats = lax.all_gather(kron_part, ("col", "sub"), axis=0, tiled=True)
    features_flat = kron_feats.reshape(kron_feats.shape[0], -1)
    precond_part = jnp.dot(features_flat, inverse_gram, precision=HIGHEST)
    precond_block = lax.psum(precond_part, "row").astype(jnp.bfloat16)
    precond_full = lax.all_gather(precond_block, ("col", "sub"), axis=1, tiled=True)
    store_start = (row_index * lax.axis_size("sub") + sub_index) * store_width
    precond_mine = lax.dynamic_slice_in_dim(precond_full, store_start, store_width, 1)
    score_part = lax.dot_general(
        precond_mine, store_slab, (((1,), (1,)), ((), ())), preferred_element_type=jnp.float32
    )
    return lax.psum(score_part, ("row", "sub"))


def gram_kernel(feats_ref, gram_ref, out_ref, terms, total):
    queries = out_ref.shape[0]
    step = pl.program_id(1)
    feats = feats_ref[...]
    high = feats.astype(jnp.bfloat16)
    terms[:queries] = high
    terms[queries:] = (feats - high.astype(jnp.float32)).astype(jnp.bfloat16)
    block = gram_ref[...]
    high = block.astype(jnp.bfloat16)
    low = (block - high.astype(jnp.float32)).astype(jnp.bfloat16)
    dims = (((1,), (1,)), ((), ()))
    part = lax.dot_general(high, terms[...], dims, preferred_element_type=jnp.float32)
    part += lax.dot_general(low, terms[...], dims, preferred_element_type=jnp.float32)

    @pl.when(step == 0)
    def _():
        total[...] = part

    @pl.when(step > 0)
    def _():
        total[...] += part

    @pl.when(step == pl.num_programs(1) - 1)
    def _():
        done = total[...]
        out_ref[...] = (done[:, :queries] + done[:, queries:]).T


def gram_product(features, inverse_gram, row_tile=1024, column_tile=1024):
    queries, width = features.shape
    rows = inverse_gram.shape[0]
    row_tile, column_tile = min(row_tile, rows), min(column_tile, width)
    return pl.pallas_call(
        gram_kernel,
        grid=(rows // row_tile, width // column_tile),
        in_specs=[
            pl.BlockSpec((queries, column_tile), lambda i, j: (0, j)),
            pl.BlockSpec((row_tile, column_tile), lambda i, j: (i, j)),
        ],
        out_specs=pl.BlockSpec((queries, row_tile), lambda i, j: (0, i)),
        out_shape=jax.ShapeDtypeStruct((queries, rows), jnp.float32),
        scratch_shapes=[
            pltpu.VMEM((2 * queries, column_tile), jnp.bfloat16),
            pltpu.VMEM((row_tile, 2 * queries), jnp.float32),
        ],
        compiler_params=pltpu.CompilerParams(vmem_limit_bytes=40 * 2**20),
        cost_estimate=pl.CostEstimate(
            flops=8 * queries * rows * width, bytes_accessed=4 * rows * width, transcendentals=0
        ),
        name="gram_product",
    )(features, inverse_gram)


def others(pick, axis):
    size = lax.axis_size(axis)
    index = lax.axis_index(axis)
    return [lax.ppermute(pick(index ^ k), axis, [(i, i ^ k) for i in range(size)]) for k in range(1, size)]


def tree_sum(terms):
    while len(terms) > 1:
        terms = [terms[i] + terms[i + 1] for i in range(0, len(terms), 2)]
    return terms[0]


def exponent(array):
    return jnp.ceil(jnp.log2(jnp.clip(jnp.max(jnp.abs(array)), 1e-30, 1e30)))


def packed(array, k):
    return (array * jnp.exp2(13.0 - k)).astype(jnp.float16)


def unpacked(array, k):
    return array.astype(jnp.float32) * jnp.exp2(k.astype(jnp.float32) - 13.0)


def body(query_acts, query_grads, proj_in, proj_out, inverse_gram, store_slab):
    row_count = lax.axis_size("row")
    row_index = lax.axis_index("row")
    sub_count = lax.axis_size("sub")
    column_count = lax.axis_size("col") * sub_count
    queries, tokens = query_acts.shape[:2]
    own = queries // row_count
    act_part = jnp.einsum("qtd,dk->qtk", query_acts, proj_in, preferred_element_type=jnp.float32)
    grad_part = jnp.einsum("qtd,dk->qtk", query_grads, proj_out, preferred_element_type=jnp.float32)
    in_width, out_width = act_part.shape[2], grad_part.shape[2]
    act_part = act_part.reshape(row_count, own * tokens, in_width)
    grad_part = grad_part.reshape(row_count, own * tokens, out_width)
    act_k, grad_k = exponent(act_part), exponent(grad_part)

    def share(part, k, d):
        piece = packed(lax.dynamic_index_in_dim(part, d, 0, keepdims=False), k)
        return jnp.concatenate([piece, jnp.full((16, part.shape[2]), k, jnp.float16)], 0)

    def summed(part, k):
        mine = lax.dynamic_index_in_dim(part, row_index, 0, keepdims=False)
        for got in others(lambda d: share(part, k, d), "row"):
            mine = mine + unpacked(got[: own * tokens], got[own * tokens, 0])
        return mine.reshape(own, tokens, -1)

    grad_proj = summed(grad_part, grad_k)
    act_proj = summed(act_part, act_k)
    kron = jnp.einsum("qta,qtb->qab", act_proj, grad_proj, precision=HIGHEST)
    kron_k = exponent(kron)
    height = in_width // column_count
    blocks = packed(kron, kron_k).reshape(own, column_count, height, out_width).swapaxes(0, 1)
    blocks = blocks.reshape(column_count, own * height, out_width)
    blocks = jnp.concatenate([blocks, jnp.full((column_count, 16, out_width), kron_k, jnp.float16)], 1)
    blocks = jnp.broadcast_to(blocks[None], (row_count,) + blocks.shape)
    blocks = blocks.reshape((row_count * column_count,) + blocks.shape[2:])
    got = lax.all_to_all(blocks, CELL, 0, 0)
    feats = unpacked(got[:, : own * height], got[:, own * height :][:, :1, :1])
    feats = feats.reshape(row_count, column_count, own, -1).swapaxes(0, 1).reshape(queries * column_count, -1)
    part = gram_product(feats, inverse_gram)
    width = store_slab.shape[1]
    part = part.reshape(part.shape[0], sub_count, width)
    pick = lambda d: lax.dynamic_index_in_dim(part, d, 1, keepdims=False)
    total = pick(lax.axis_index("sub"))
    for got in others(pick, "sub"):
        total = total + got
    half = total.astype(jnp.bfloat16)
    for got in others(lambda d: half, "col"):
        total = total + got.astype(jnp.float32)
    high = lax.reduce_precision(total, 8, 7)
    terms = jnp.concatenate([high, total - high], 0).astype(jnp.bfloat16)
    scores = lax.dot_general(
        terms, store_slab, (((1,), (1,)), ((), ())), preferred_element_type=jnp.float32
    )
    scores = scores[: total.shape[0]] + scores[total.shape[0] :]
    for axis in ("sub", "row"):
        scores = tree_sum([scores] + others(lambda d, sent=scores: sent, axis))
    return scores


def solution(mesh):
    shape = mesh.shape
    even = all(size & (size - 1) == 0 for size in shape.values())
    def chosen(query_acts, *rest):
        queries = query_acts.shape[0] // (shape["groups"] * shape["col"] * shape["sub"])
        chosen_body = body if even and queries % shape["row"] == 0 else plain_body
        return jax.shard_map(
            chosen_body,
            mesh=mesh,
            in_specs=(
                P(("groups", "col", "sub"), None, "row"),
                P(("groups", "col", "sub"), None, "row"),
                P("row", None),
                P("row", None),
                P("row", ("col", "sub")),
                P(("groups", "col"), ("row", "sub")),
            ),
            out_specs=P("groups", "col"),
            check_vma=False,
        )(query_acts, *rest)

    return chosen
```

```python
import functools

import jax
import jax.numpy as jnp
from jax import lax
from jax.experimental import pallas as pl
from jax.experimental.pallas import tpu as pltpu
from jax.sharding import PartitionSpec as P

HIGHEST = lax.Precision.HIGHEST


def plain_body(query_acts, query_grads, proj_in, proj_out, inverse_gram, store_slab):
    row_count = lax.axis_size("row")
    row_index = lax.axis_index("row")
    sub_index = lax.axis_index("sub")
    in_width = proj_in.shape[1]
    act_part = jnp.einsum("qtd,dk->qtk", query_acts, proj_in, preferred_element_type=jnp.float32)
    grad_part = jnp.einsum("qtd,dk->qtk", query_grads, proj_out, preferred_element_type=jnp.float32)
    store_width = store_slab.shape[1]
    row_block = in_width // row_count
    act_whole, grad_proj = lax.psum((act_part, grad_part), "row")
    act_proj = lax.dynamic_slice_in_dim(act_whole, row_index * row_block, row_block, 2)
    kron_part = jnp.einsum("qta,qtb->qab", act_proj, grad_proj, precision=HIGHEST)
    kron_feats = lax.all_gather(kron_part, ("col", "sub"), axis=0, tiled=True)
    features_flat = kron_feats.reshape(kron_feats.shape[0], -1)
    precond_part = jnp.dot(features_flat, inverse_gram, precision=HIGHEST)
    precond_block = lax.psum(precond_part, "row").astype(jnp.bfloat16)
    precond_full = lax.all_gather(precond_block, ("col", "sub"), axis=1, tiled=True)
    store_start = (row_index * lax.axis_size("sub") + sub_index) * store_width
    precond_mine = lax.dynamic_slice_in_dim(precond_full, store_start, store_width, 1)
    score_part = lax.dot_general(
        precond_mine, store_slab, (((1,), (1,)), ((), ())), preferred_element_type=jnp.float32
    )
    return lax.psum(score_part, ("row", "sub"))


PAD = 8
SHIFT = 13.0
LOG2E = 1.4426950408889634
WHOLE = pl.BlockSpec(memory_space=pltpu.VMEM)
MIB = 2**20


def exponents(part):
    top = jnp.max(jnp.abs(part), axis=0, keepdims=True)
    return jnp.ceil(jnp.log(jnp.clip(top, 1e-30, 1e30)) * LOG2E)


def scaled(part, k):
    return part * jnp.exp2(SHIFT - k)


def restored(part, k):
    return part * jnp.exp2(k - SHIFT)


def project_kernel(row_ref, acts_ref, grads_ref, in_ref, out_proj_ref, out_ref):
    del row_ref
    count = acts_ref.shape[0] * acts_ref.shape[1]
    pairs = ((acts_ref, in_ref), (grads_ref, out_proj_ref))
    for i, (x_ref, w_ref) in enumerate(pairs):
        x = x_ref[...].reshape(count, x_ref.shape[2])
        part = jnp.dot(x, w_ref[...], preferred_element_type=jnp.float32)
        k = exponents(part)
        out_ref[0, i * count : (i + 1) * count] = scaled(part, k)
        out_ref[0, 2 * count + i * PAD : 2 * count + (i + 1) * PAD] = jnp.broadcast_to(k, (PAD, k.shape[1]))


def project(query_acts, query_grads, proj_in, proj_out, row_count, row_index):
    queries, tokens, width = query_acts.shape
    own = queries // row_count
    out_width = proj_in.shape[1]
    height = 2 * own * tokens + 2 * PAD
    pick = lambda k, row: (row[0] ^ k, 0, 0)
    full = lambda k, row: (0, 0)
    return pl.pallas_call(
        project_kernel,
        grid_spec=pltpu.PrefetchScalarGridSpec(
            num_scalar_prefetch=1,
            grid=(row_count,),
            in_specs=[
                pl.BlockSpec((own, tokens, width), pick),
                pl.BlockSpec((own, tokens, width), pick),
                pl.BlockSpec(proj_in.shape, full),
                pl.BlockSpec(proj_out.shape, full),
            ],
            out_specs=pl.BlockSpec((1, height, out_width), lambda k, row: (k, 0, 0)),
        ),
        out_shape=jax.ShapeDtypeStruct((row_count, height, out_width), jnp.float32),
        compiler_params=pltpu.CompilerParams(vmem_limit_bytes=16 * MIB),
        name="project",
    )(row_index.reshape(1), query_acts, query_grads, proj_in, proj_out)


def kron_kernel(place_ref, own_ref, *refs, tokens):
    out_ref = refs[-1]
    count = (own_ref.shape[0] - 2 * PAD) // 2
    sums = []
    for i in range(2):
        total = None
        for ref in (own_ref,) + refs[:-1]:
            k = 2 * count + i * PAD
            part = restored(ref[i * count : (i + 1) * count], ref[k : k + 1])
            total = part if total is None else total + part
        sums.append(total)
    acts, grads = sums
    height = acts.shape[1] // 8
    for j in range(count // tokens):
        rows = slice(j * tokens, (j + 1) * tokens)
        kron = lax.dot_general(
            acts[rows], grads[rows], (((0,), (0,)), ((), ())), precision=HIGHEST, preferred_element_type=jnp.float32
        )
        for c in range(2):
            for s in range(2):
                for g in range(2):
                    start = ((c * 2 + s) * 2 + g) * height
                    out_ref[g ^ place_ref[0], c ^ place_ref[2], s ^ place_ref[3], j * height : (j + 1) * height] = (
                        kron[start : start + height]
                    )


def pack_kernel(kept_ref, got_ref, out_ref):
    lanes = kept_ref.shape[-1]
    parts = jnp.concatenate([kept_ref[...].reshape(-1, lanes), got_ref[...].reshape(-1, lanes)], 0)
    k = exponents(parts)
    out_ref[: parts.shape[0]] = scaled(parts, k)
    out_ref[parts.shape[0] :] = jnp.broadcast_to(k, (PAD, lanes))


def split(block):
    high = block.astype(jnp.bfloat16)
    return high, (block - high.astype(jnp.float32)).astype(jnp.bfloat16)


def gram_split_kernel(place_ref, gram_ref, high_ref, low_ref, buffer, sems):
    slots, tile, width = buffer.shape
    steps = high_ref.shape[0] // tile
    column = pl.multiple_of(place_ref[0] * width, width)

    def copy(i):
        rows = pl.ds(pl.multiple_of(i * tile, tile), tile)
        slot = lax.rem(i, slots)
        return pltpu.make_async_copy(gram_ref.at[rows, pl.ds(column, width)], buffer.at[slot], sems.at[slot])

    for i in range(slots - 1):
        copy(i).start()

    @pl.loop(0, steps)
    def _(i):
        @pl.when(i + slots - 1 < steps)
        def _():
            copy(i + slots - 1).start()

        copy(i).wait()
        rows = pl.ds(pl.multiple_of(i * tile, tile), tile)
        high, low = split(buffer[lax.rem(i, slots)])
        high_ref[rows] = high
        low_ref[rows] = low


def gram_split(inverse_gram, place, tile=256, slots=4):
    rows, width = inverse_gram.shape
    half = width // 2
    tile = min(tile, rows)
    terms = pltpu.VMEM((rows, half), jnp.bfloat16)
    return pl.pallas_call(
        gram_split_kernel,
        in_specs=[pl.BlockSpec(memory_space=pltpu.SMEM), pl.BlockSpec(memory_space=pltpu.HBM)],
        out_specs=[WHOLE, WHOLE],
        out_shape=[terms, terms],
        scratch_shapes=[pltpu.VMEM((slots, tile, half), jnp.float32), pltpu.SemaphoreType.DMA((slots,))],
        compiler_params=pltpu.CompilerParams(vmem_limit_bytes=SPLIT_LIMIT),
        cost_estimate=pl.CostEstimate(flops=0, bytes_accessed=4 * rows * half, transcendentals=0),
        name="gram_split",
    )(place, inverse_gram)


def gram_kernel(place_ref, high_ref, low_ref, *refs, row_count, own):
    sources, (out_ref, natural, terms) = refs[:row_count], refs[row_count:]
    group, row, col, sub = (place_ref[i] for i in range(4))
    height, queries, lanes = natural.shape
    for z in range(row_count):
        count = sources[z].shape[0] - PAD
        piece = restored(sources[z][:count], sources[z][count : count + 1])
        for place in range(8):
            s, c, g = place // 4, place // 2 % 2, place % 2
            first = ((((g ^ group) * 2 + (c ^ col)) * 2 + (s ^ sub)) * row_count + (z ^ row)) * own
            for j in range(own):
                start = (place * own + j) * height
                natural[:, pl.ds(first + j, 1), :] = piece[start : start + height].reshape(height, 1, lanes)
    for a in range(height):
        high, low = split(natural[a])
        terms[:queries, a * lanes : (a + 1) * lanes] = high
        terms[queries:, a * lanes : (a + 1) * lanes] = low
    width = out_ref.shape[3]
    tile = min(TILE, width)
    dims = (((1,), (1,)), ((), ()))

    @pl.loop(0, 2 * width // tile)
    def _(i):
        rows = pl.ds(pl.multiple_of(i * tile, tile), tile)
        part = lax.dot_general(high_ref[rows], terms[...], dims, preferred_element_type=jnp.float32)
        part += lax.dot_general(low_ref[rows], terms[...], dims, preferred_element_type=jnp.float32)
        done = (part[:, :queries] + part[:, queries:]).T
        half = i // (width // tile)
        columns = pl.ds(pl.multiple_of((i - half * (width // tile)) * tile, tile), tile)
        for g in range(2):
            out_ref[half ^ sub, g ^ group, :, columns] = done[g * (queries // 2) : (g + 1) * (queries // 2)]


TILE = 512
SPLIT_LIMIT = 16 * MIB
PRODUCT_LIMIT = 16 * MIB


def gram_product(place, high, low, sources, own, tokens_width):
    rows, half = high.shape
    row_count = len(sources)
    queries = 8 * row_count * own
    return pl.pallas_call(
        functools.partial(gram_kernel, row_count=row_count, own=own),
        in_specs=[pl.BlockSpec(memory_space=pltpu.SMEM)] + [WHOLE] * (2 + row_count),
        out_specs=WHOLE,
        out_shape=jax.ShapeDtypeStruct((2, 2, queries // 2, rows // 2), jnp.float32),
        scratch_shapes=[
            pltpu.VMEM((half // tokens_width, queries, tokens_width), jnp.float32),
            pltpu.VMEM((2 * queries, half), jnp.bfloat16),
        ],
        compiler_params=pltpu.CompilerParams(vmem_limit_bytes=PRODUCT_LIMIT),
        cost_estimate=pl.CostEstimate(flops=8 * queries * rows * half, bytes_accessed=4 * rows * half, transcendentals=0),
        name="gram_product",
    )(place, high, low, *sources)


def others(pick, axis):
    size = lax.axis_size(axis)
    index = lax.axis_index(axis)
    return [lax.ppermute(pick(index ^ k), axis, [(i, i ^ k) for i in range(size)]) for k in range(1, size)]


def tree_sum(terms):
    while len(terms) > 1:
        terms = [terms[i] + terms[i + 1] for i in range(0, len(terms), 2)]
    return terms[0]


def swapped(array, axis):
    return others(lambda d: array, axis)[0]


def call(kernel, shape, name, *args):
    specs = [pl.BlockSpec(memory_space=pltpu.SMEM) if a.dtype == jnp.int32 else WHOLE for a in args]
    return pl.pallas_call(
        kernel,
        in_specs=specs,
        out_specs=WHOLE,
        out_shape=jax.ShapeDtypeStruct(shape, jnp.float32),
        compiler_params=pltpu.CompilerParams(vmem_limit_bytes=16 * MIB),
        name=name,
    )(*args)


def body(query_acts, query_grads, proj_in, proj_out, inverse_gram, store_slab):
    row_count = lax.axis_size("row")
    row_index = lax.axis_index("row")
    place = jnp.stack([lax.axis_index(axis) for axis in ("groups", "row", "col", "sub")])
    queries, tokens = query_acts.shape[:2]
    own = queries // row_count
    in_width, out_width = proj_in.shape[1], proj_out.shape[1]
    parts = project(query_acts, query_grads, proj_in, proj_out, row_count, row_index)
    wire = [parts[k].astype(jnp.float16) for k in range(1, row_count)]
    got = [
        lax.ppermute(wire[k - 1], "row", [(i, i ^ k) for i in range(row_count)]).astype(jnp.float32)
        for k in range(1, row_count)
    ]
    high, low = gram_split(inverse_gram, place)
    height = own * in_width // 8
    kron = call(
        functools.partial(kron_kernel, tokens=tokens), (2, 2, 2, height, out_width), "kron", place, parts[0], *got
    )
    near = jnp.stack([kron[0], swapped(kron[1], "groups")], 2)
    near = jnp.stack([near[0], swapped(near[1], "col")], 1)
    packed = call(pack_kernel, (8 * height + PAD, out_width), "pack", near[0], swapped(near[1], "sub"))
    wire = packed.astype(jnp.float16)
    sources = [packed] + [got.astype(jnp.float32) for got in others(lambda d: wire, "row")]
    part = gram_product(place, high, low, sources, own, out_width)
    total = part[0] + swapped(part[1], "sub")
    total = total[0] + swapped(total[1].astype(jnp.bfloat16), "groups").astype(jnp.float32)
    total = total + swapped(total.astype(jnp.bfloat16), "col").astype(jnp.float32)
    high = lax.reduce_precision(total, 8, 7)
    terms = jnp.concatenate([high, total - high], 0).astype(jnp.bfloat16)
    scores = lax.dot_general(
        terms, store_slab, (((1,), (1,)), ((), ())), preferred_element_type=jnp.float32
    )
    scores = scores[: total.shape[0]] + scores[total.shape[0] :]
    for axis in ("sub", "row"):
        scores = tree_sum([scores] + others(lambda d, sent=scores: sent, axis))
    return scores


def solution(mesh):
    shape = mesh.shape
    rows = shape["row"]
    paired = shape["groups"] == shape["col"] == shape["sub"] == 2 and rows & (rows - 1) == 0

    def chosen(query_acts, query_grads, proj_in, proj_out, *rest):
        queries = query_acts.shape[0] // (shape["groups"] * shape["col"] * shape["sub"])
        square = proj_in.shape[1] == proj_out.shape[1] == 128
        chosen_body = body if paired and square and queries % rows == 0 else plain_body
        return jax.shard_map(
            chosen_body,
            mesh=mesh,
            in_specs=(
                P(("groups", "col", "sub"), None, "row"),
                P(("groups", "col", "sub"), None, "row"),
                P("row", None),
                P("row", None),
                P("row", ("col", "sub")),
                P(("groups", "col"), ("row", "sub")),
            ),
            out_specs=P("groups", "col"),
            check_vma=False,
        )(query_acts, query_grads, proj_in, proj_out, *rest)

    return chosen
```

```python
import functools

import jax
import jax.numpy as jnp
from jax import lax
from jax.experimental import pallas as pl
from jax.experimental.pallas import tpu as pltpu
from jax.sharding import PartitionSpec as P

HIGHEST = lax.Precision.HIGHEST


def plain_body(query_acts, query_grads, proj_in, proj_out, inverse_gram, store_slab):
    row_count = lax.axis_size("row")
    row_index = lax.axis_index("row")
    sub_index = lax.axis_index("sub")
    in_width = proj_in.shape[1]
    act_part = jnp.einsum("qtd,dk->qtk", query_acts, proj_in, preferred_element_type=jnp.float32)
    grad_part = jnp.einsum("qtd,dk->qtk", query_grads, proj_out, preferred_element_type=jnp.float32)
    store_width = store_slab.shape[1]
    row_block = in_width // row_count
    act_whole, grad_proj = lax.psum((act_part, grad_part), "row")
    act_proj = lax.dynamic_slice_in_dim(act_whole, row_index * row_block, row_block, 2)
    kron_part = jnp.einsum("qta,qtb->qab", act_proj, grad_proj, precision=HIGHEST)
    kron_feats = lax.all_gather(kron_part, ("col", "sub"), axis=0, tiled=True)
    features_flat = kron_feats.reshape(kron_feats.shape[0], -1)
    precond_part = jnp.dot(features_flat, inverse_gram, precision=HIGHEST)
    precond_block = lax.psum(precond_part, "row").astype(jnp.bfloat16)
    precond_full = lax.all_gather(precond_block, ("col", "sub"), axis=1, tiled=True)
    store_start = (row_index * lax.axis_size("sub") + sub_index) * store_width
    precond_mine = lax.dynamic_slice_in_dim(precond_full, store_start, store_width, 1)
    score_part = lax.dot_general(
        precond_mine, store_slab, (((1,), (1,)), ((), ())), preferred_element_type=jnp.float32
    )
    return lax.psum(score_part, ("row", "sub"))


PAD = 8
SHIFT = 13.0
LOG2E = 1.4426950408889634
WHOLE = pl.BlockSpec(memory_space=pltpu.VMEM)
MIB = 2**20


def exponents(part):
    top = jnp.max(jnp.abs(part), axis=0, keepdims=True)
    return jnp.ceil(jnp.log(jnp.clip(top, 1e-30, 1e30)) * LOG2E)


def scaled(part, k):
    return part * jnp.exp2(SHIFT - k)


def restored(part, k):
    return part * jnp.exp2(k - SHIFT)


def project_kernel(place_ref, *refs):
    inputs, outs, (inputs_buf, weights_buf, sems, weights_sems) = refs[:4], refs[4:-4], refs[-4:]
    own, tokens, width = inputs_buf.shape[2:]
    count = own * tokens
    row = place_ref[1]
    weights = [pltpu.make_async_copy(inputs[2 + i], weights_buf.at[i], weights_sems.at[i]) for i in range(2)]
    order = [k for k in range(len(outs))][::-1]
    copies = {}
    for k in order:
        for i in range(2):
            if k == order[0]:
                weights[i].start()
            rows = pl.ds((row ^ k) * own, own)
            copies[k, i] = pltpu.make_async_copy(inputs[i].at[rows], inputs_buf.at[i, k], sems.at[i, k])
            copies[k, i].start()
    for k in order:
        for i in range(2):
            if k == order[0]:
                weights[i].wait()
            copies[k, i].wait()
            x = inputs_buf[i, k].reshape(count, width)
            part = jnp.dot(x, weights_buf[i], preferred_element_type=jnp.float32)
            e = exponents(part)
            outs[k][i * count : (i + 1) * count] = scaled(part, e)
            outs[k][2 * count + i * PAD : 2 * count + (i + 1) * PAD] = jnp.broadcast_to(e, (PAD, e.shape[1]))


def project(place, query_acts, query_grads, proj_in, proj_out, row_count):
    queries, tokens, width = query_acts.shape
    own = queries // row_count
    out_width = proj_in.shape[1]
    height = 2 * own * tokens + 2 * PAD
    far = pl.BlockSpec(memory_space=pltpu.HBM)
    return pl.pallas_call(
        project_kernel,
        in_specs=[pl.BlockSpec(memory_space=pltpu.SMEM)] + [far] * 4,
        out_specs=[WHOLE] * row_count,
        out_shape=[jax.ShapeDtypeStruct((height, out_width), jnp.float32)] * row_count,
        scratch_shapes=[
            pltpu.VMEM((2, row_count, own, tokens, width), query_acts.dtype),
            pltpu.VMEM((2,) + proj_in.shape, proj_in.dtype),
            pltpu.SemaphoreType.DMA((2, row_count)),
            pltpu.SemaphoreType.DMA((2,)),
        ],
        compiler_params=pltpu.CompilerParams(vmem_limit_bytes=8 * MIB),
        name="project",
    )(place, *[pltpu.with_memory_space_constraint(x, pltpu.HBM) for x in (query_acts, query_grads, proj_in, proj_out)])


def kron_kernel(place_ref, after_ref, own_ref, *refs, tokens):
    del after_ref
    refs, outs, scratch = refs[:-5], refs[-5:-1], refs[-1]
    count = (own_ref.shape[0] - 2 * PAD) // 2
    sums = []
    for i in range(2):
        total = None
        for ref in (own_ref,) + refs:
            k = 2 * count + i * PAD
            part = restored(ref[i * count : (i + 1) * count], ref[k : k + 1])
            total = part if total is None else total + part
        sums.append(total)
    acts, grads = sums
    height = acts.shape[1] // 8
    group, col, sub = place_ref[0], place_ref[2], place_ref[3]
    for j in range(count // tokens):
        rows = slice(j * tokens, (j + 1) * tokens)
        scratch[j] = lax.dot_general(
            acts[rows], grads[rows], (((0,), (0,)), ((), ())), precision=HIGHEST, preferred_element_type=jnp.float32
        )
        for k in range(4):
            for s in range(2):
                start = (((col ^ (k % 2)) * 2 + (sub ^ s)) * 2 + (group ^ (k // 2))) * height
                outs[k][s, j * height : (j + 1) * height] = scratch[j, pl.ds(pl.multiple_of(start, height), height)]


def pack_kernel(*refs):
    kept, got_ref, out_ref = refs[:-2], refs[-2], refs[-1]
    lanes = got_ref.shape[-1]
    parts = jnp.concatenate([ref[0] for ref in kept] + [got_ref[...].reshape(-1, lanes)], 0)
    k = exponents(parts)
    out_ref[: parts.shape[0]] = scaled(parts, k)
    out_ref[parts.shape[0] :] = jnp.broadcast_to(k, (PAD, lanes))


def pack_scores_kernel(scores_ref, out_ref):
    scores = scores_ref[...]
    k = exponents(scores)
    out_ref[: scores.shape[0]] = scaled(scores, k)
    out_ref[scores.shape[0] :] = jnp.broadcast_to(k, (PAD, scores.shape[1]))


def sum_scores_kernel(*refs):
    out_ref = refs[-1]
    count = out_ref.shape[0]
    out_ref[...] = tree_sum([restored(ref[:count], ref[count : count + 1]) for ref in refs[:-1]])


def split(block):
    high = block.astype(jnp.bfloat16)
    return high, (block - high.astype(jnp.float32)).astype(jnp.bfloat16)


def gram_split_kernel(place_ref, gram_ref, high_ref, low_ref, mark_ref, buffer, sems):
    slots, tile, width = buffer.shape
    steps = high_ref.shape[0] // tile
    column = pl.multiple_of(place_ref[0] * width, width)

    def copy(i):
        rows = pl.ds(pl.multiple_of(i * tile, tile), tile)
        slot = lax.rem(i, slots)
        return pltpu.make_async_copy(gram_ref.at[rows, pl.ds(column, width)], buffer.at[slot], sems.at[slot])

    for i in range(slots - 1):
        copy(i).start()

    @pl.loop(0, steps)
    def _(i):
        @pl.when(i + slots - 1 < steps)
        def _():
            copy(i + slots - 1).start()

        copy(i).wait()
        rows = pl.ds(pl.multiple_of(i * tile, tile), tile)
        high, low = split(buffer[lax.rem(i, slots)])
        high_ref[rows] = high
        low_ref[rows] = low

    mark_ref[...] = jnp.zeros_like(mark_ref)


def gram_split(inverse_gram, place, tile=256, slots=4):
    rows, width = inverse_gram.shape
    half = width // 2
    tile = min(tile, rows)
    terms = pltpu.VMEM((rows, half), jnp.bfloat16)
    return pl.pallas_call(
        gram_split_kernel,
        in_specs=[pl.BlockSpec(memory_space=pltpu.SMEM), pl.BlockSpec(memory_space=pltpu.HBM)],
        out_specs=[WHOLE, WHOLE, WHOLE],
        out_shape=[terms, terms, jax.ShapeDtypeStruct((8, 128), jnp.float32)],
        scratch_shapes=[pltpu.VMEM((slots, tile, half), jnp.float32), pltpu.SemaphoreType.DMA((slots,))],
        compiler_params=pltpu.CompilerParams(vmem_limit_bytes=SPLIT_LIMIT),
        cost_estimate=pl.CostEstimate(flops=0, bytes_accessed=4 * rows * half, transcendentals=0),
        name="gram_split",
    )(place, inverse_gram)


def gram_rows(half, group, high_ref, low_ref, terms, out_ref):
    queries, width = 2 * out_ref.shape[1], out_ref.shape[2]
    tile = min(TILE, width)
    dims = (((1,), (1,)), ((), ()))

    @pl.loop(0, width // tile)
    def _(i):
        rows = pl.ds(pl.multiple_of(half * width + i * tile, tile), tile)
        part = lax.dot_general(high_ref[rows], terms[...], dims, preferred_element_type=jnp.float32)
        part += lax.dot_general(low_ref[rows], terms[...], dims, preferred_element_type=jnp.float32)
        done = (part[:, :queries] + part[:, queries:]).T
        columns = pl.ds(pl.multiple_of(i * tile, tile), tile)
        for g in range(2):
            out_ref[g ^ group, :, columns] = done[g * (queries // 2) : (g + 1) * (queries // 2)]


def away_kernel(place_ref, high_ref, low_ref, *refs, row_count, own):
    sources, (out_ref, terms, natural) = refs[:row_count], refs[row_count:]
    group, row, col, sub = (place_ref[i] for i in range(4))
    height, queries, lanes = natural.shape
    for z in range(row_count):
        count = sources[z].shape[0] - PAD
        piece = restored(sources[z][:count], sources[z][count : count + 1])
        for place in range(8):
            s, g, c = place // 4, place // 2 % 2, place % 2
            first = ((((g ^ group) * 2 + (c ^ col)) * 2 + (s ^ sub)) * row_count + (z ^ row)) * own
            for j in range(own):
                start = (place * own + j) * height
                natural[:, pl.ds(first + j, 1), :] = piece[start : start + height].reshape(height, 1, lanes)
    for a in range(height):
        high, low = split(natural[a])
        terms[:queries, a * lanes : (a + 1) * lanes] = high
        terms[queries:, a * lanes : (a + 1) * lanes] = low
    gram_rows(1 - sub, group, high_ref, low_ref, terms, out_ref)


def home_kernel(place_ref, high_ref, low_ref, terms_ref, out_ref):
    gram_rows(place_ref[3], place_ref[0], high_ref, low_ref, terms_ref, out_ref)


TILE = 512
SPLIT_LIMIT = 12 * MIB


def gram_product(place, high, low, sources, own, lanes):
    rows, half = high.shape
    row_count = len(sources)
    queries = 8 * row_count * own
    part = jax.ShapeDtypeStruct((2, queries // 2, rows // 2), jnp.float32)
    terms = jax.ShapeDtypeStruct((2 * queries, half), jnp.bfloat16)
    common = dict(
        compiler_params=pltpu.CompilerParams(vmem_limit_bytes=8 * MIB),
        cost_estimate=pl.CostEstimate(flops=4 * queries * rows * half, bytes_accessed=2 * rows * half, transcendentals=0),
    )
    index = pl.BlockSpec(memory_space=pltpu.SMEM)
    high, low = (pltpu.with_memory_space_constraint(x, pltpu.VMEM) for x in (high, low))
    away, terms = pl.pallas_call(
        functools.partial(away_kernel, row_count=row_count, own=own),
        in_specs=[index] + [WHOLE] * (2 + row_count),
        out_specs=[WHOLE, WHOLE],
        out_shape=[part, terms],
        scratch_shapes=[pltpu.VMEM((half // lanes, queries, lanes), jnp.float32)],
        name="away",
        **common,
    )(place, high, low, *sources)
    got = swapped(away, "sub")
    home = pl.pallas_call(
        home_kernel, in_specs=[index] + [WHOLE] * 3, out_specs=WHOLE, out_shape=part, name="home", **common
    )(place, high, low, terms)
    return home + got


def others(pick, axis):
    size = lax.axis_size(axis)
    index = lax.axis_index(axis)
    return [lax.ppermute(pick(index ^ k), axis, [(i, i ^ k) for i in range(size)]) for k in range(1, size)]


def tree_sum(terms):
    while len(terms) > 1:
        terms = [terms[i] + terms[i + 1] for i in range(0, len(terms), 2)]
    return terms[0]


def swapped(array, axis):
    return others(lambda d: array, axis)[0]


def peers(pick):
    return [lax.ppermute(pick(k), ("groups", "col"), [(i, i ^ k) for i in range(4)]) for k in (1, 2, 3)]


def call(kernel, shapes, name, *args, specs=None, scratch=()):
    specs = specs or [pl.BlockSpec(memory_space=pltpu.SMEM) if a.dtype == jnp.int32 else WHOLE for a in args]
    many = isinstance(shapes, list)
    shapes = [jax.ShapeDtypeStruct(shape, jnp.float32) for shape in (shapes if many else [shapes])]
    outs = pl.pallas_call(
        kernel,
        in_specs=specs,
        out_specs=[WHOLE] * len(shapes),
        out_shape=shapes,
        scratch_shapes=list(scratch),
        compiler_params=pltpu.CompilerParams(vmem_limit_bytes=4 * MIB),
        name=name,
    )(*args)
    return outs if many else outs[0]


def body(query_acts, query_grads, proj_in, proj_out, inverse_gram, store_slab):
    row_count = lax.axis_size("row")
    place = jnp.stack([lax.axis_index(axis) for axis in ("groups", "row", "col", "sub")])
    queries, tokens = query_acts.shape[:2]
    own = queries // row_count
    in_width, out_width = proj_in.shape[1], proj_out.shape[1]
    parts = project(place, query_acts, query_grads, proj_in, proj_out, row_count)
    got = [
        lax.ppermute(parts[k].astype(jnp.float16), "row", [(i, i ^ k) for i in range(row_count)])
        for k in range(1, row_count)
    ]
    high, low, mark = gram_split(inverse_gram, place)
    height = own * in_width // 8
    near = call(
        functools.partial(kron_kernel, tokens=tokens),
        [(2, height, out_width)] * 4,
        "kron",
        place,
        mark,
        parts[0],
        *[x.astype(jnp.float32) for x in got],
        scratch=[pltpu.VMEM((own, in_width, out_width), jnp.float32)],
    )
    near = [near[0]] + peers(lambda k: near[k])
    got = swapped(jnp.stack([x[1] for x in near]), "sub")
    packed = call(pack_kernel, (8 * height + PAD, out_width), "pack", *near, got)
    wire = packed.astype(jnp.float16)
    sources = [packed] + [got.astype(jnp.float32) for got in others(lambda d: wire, "row")]
    total = gram_product(place, high, low, sources, own, out_width)
    wire = total.astype(jnp.bfloat16)
    total = total[0]
    for got in peers(lambda k: wire[k // 2]):
        total = total + got.astype(jnp.float32)
    high = lax.reduce_precision(total, 8, 7)
    terms = jnp.concatenate([high, total - high], 0).astype(jnp.bfloat16)
    scores = lax.dot_general(
        terms, store_slab, (((1,), (1,)), ((), ())), preferred_element_type=jnp.float32
    )
    scores = scores[: total.shape[0]] + scores[total.shape[0] :]
    scores = scores + swapped(scores, "sub")
    packed = call(pack_scores_kernel, (scores.shape[0] + PAD, scores.shape[1]), "pack_scores", scores)
    packed = lax.reduce_precision(packed, 5, 10)
    wire = packed.astype(jnp.float16)
    sources = [packed] + [got.astype(jnp.float32) for got in others(lambda d: wire, "row")]
    return call(sum_scores_kernel, scores.shape, "sum_scores", *sources)


def solution(mesh):
    shape = mesh.shape
    rows = shape["row"]
    paired = shape["groups"] == shape["col"] == shape["sub"] == 2 and rows & (rows - 1) == 0

    def chosen(query_acts, query_grads, proj_in, proj_out, *rest):
        queries = query_acts.shape[0] // (shape["groups"] * shape["col"] * shape["sub"])
        square = proj_in.shape[1] == proj_out.shape[1] == 128
        chosen_body = body if paired and square and queries % rows == 0 else plain_body
        return jax.shard_map(
            chosen_body,
            mesh=mesh,
            in_specs=(
                P(("groups", "col", "sub"), None, "row"),
                P(("groups", "col", "sub"), None, "row"),
                P("row", None),
                P("row", None),
                P("row", ("col", "sub")),
                P(("groups", "col"), ("row", "sub")),
            ),
            out_specs=P("groups", "col"),
            check_vma=False,
        )(query_acts, query_grads, proj_in, proj_out, *rest)

    return chosen
```

```python
import functools

import jax
import jax.numpy as jnp
from jax import lax
from jax.experimental import pallas as pl
from jax.experimental.pallas import tpu as pltpu
from jax.sharding import PartitionSpec as P

HIGHEST = lax.Precision.HIGHEST


def plain_body(query_acts, query_grads, proj_in, proj_out, inverse_gram, store_slab):
    row_count = lax.axis_size("row")
    row_index = lax.axis_index("row")
    sub_index = lax.axis_index("sub")
    in_width = proj_in.shape[1]
    act_part = jnp.einsum("qtd,dk->qtk", query_acts, proj_in, preferred_element_type=jnp.float32)
    grad_part = jnp.einsum("qtd,dk->qtk", query_grads, proj_out, preferred_element_type=jnp.float32)
    store_width = store_slab.shape[1]
    row_block = in_width // row_count
    act_whole, grad_proj = lax.psum((act_part, grad_part), "row")
    act_proj = lax.dynamic_slice_in_dim(act_whole, row_index * row_block, row_block, 2)
    kron_part = jnp.einsum("qta,qtb->qab", act_proj, grad_proj, precision=HIGHEST)
    kron_feats = lax.all_gather(kron_part, ("col", "sub"), axis=0, tiled=True)
    features_flat = kron_feats.reshape(kron_feats.shape[0], -1)
    precond_part = jnp.dot(features_flat, inverse_gram, precision=HIGHEST)
    precond_block = lax.psum(precond_part, "row").astype(jnp.bfloat16)
    precond_full = lax.all_gather(precond_block, ("col", "sub"), axis=1, tiled=True)
    store_start = (row_index * lax.axis_size("sub") + sub_index) * store_width
    precond_mine = lax.dynamic_slice_in_dim(precond_full, store_start, store_width, 1)
    score_part = lax.dot_general(
        precond_mine, store_slab, (((1,), (1,)), ((), ())), preferred_element_type=jnp.float32
    )
    return lax.psum(score_part, ("row", "sub"))


PAD = 8
SHIFT = 13.0
LOG2E = 1.4426950408889634
WHOLE = pl.BlockSpec(memory_space=pltpu.VMEM)
MIB = 2**20


def exponents(part):
    top = jnp.max(jnp.abs(part), axis=0, keepdims=True)
    return jnp.ceil(jnp.log(jnp.clip(top, 1e-30, 1e30)) * LOG2E)


def scaled(part, k):
    return part * jnp.exp2(SHIFT - k)


def restored(part, k):
    return part * jnp.exp2(k - SHIFT)


def project_kernel(place_ref, *refs, targets):
    inputs, outs, (inputs_buf, weights_buf, sems, weights_sems) = refs[:4], refs[4:-4], refs[-4:]
    own, tokens, width = inputs_buf.shape[2:]
    count = own * tokens
    row = place_ref[1]
    weights = [pltpu.make_async_copy(inputs[2 + i], weights_buf.at[i], weights_sems.at[i]) for i in range(2)]
    copies = {}
    for k in range(len(targets)):
        for i in range(2):
            if k == 0:
                weights[i].start()
            rows = pl.ds((row ^ targets[k]) * own, own)
            copies[k, i] = pltpu.make_async_copy(inputs[i].at[rows], inputs_buf.at[i, k], sems.at[i, k])
            copies[k, i].start()
    for k in range(len(targets)):
        for i in range(2):
            if k == 0:
                weights[i].wait()
            copies[k, i].wait()
            x = inputs_buf[i, k].reshape(count, width)
            part = jnp.dot(x, weights_buf[i], preferred_element_type=jnp.float32)
            e = exponents(part)
            outs[k][i * count : (i + 1) * count] = scaled(part, e)
            outs[k][2 * count + i * PAD : 2 * count + (i + 1) * PAD] = jnp.broadcast_to(e, (PAD, e.shape[1]))


def project(targets, row_count, place, query_acts, query_grads, proj_in, proj_out):
    queries, tokens, width = query_acts.shape
    own = queries // row_count
    out_width = proj_in.shape[1]
    height = 2 * own * tokens + 2 * PAD
    far = pl.BlockSpec(memory_space=pltpu.HBM)
    return pl.pallas_call(
        functools.partial(project_kernel, targets=targets),
        in_specs=[pl.BlockSpec(memory_space=pltpu.SMEM)] + [far] * 4,
        out_specs=[WHOLE] * len(targets),
        out_shape=[jax.ShapeDtypeStruct((height, out_width), jnp.float32)] * len(targets),
        scratch_shapes=[
            pltpu.VMEM((2, len(targets), own, tokens, width), query_acts.dtype),
            pltpu.VMEM((2,) + proj_in.shape, proj_in.dtype),
            pltpu.SemaphoreType.DMA((2, len(targets))),
            pltpu.SemaphoreType.DMA((2,)),
        ],
        compiler_params=pltpu.CompilerParams(vmem_limit_bytes=8 * MIB),
        name="project",
    )(place, *[pltpu.with_memory_space_constraint(x, pltpu.HBM) for x in (query_acts, query_grads, proj_in, proj_out)])


def kron_kernel(place_ref, after_ref, own_ref, *refs, tokens):
    del after_ref
    refs, outs, scratch = refs[:-5], refs[-5:-1], refs[-1]
    count = (own_ref.shape[0] - 2 * PAD) // 2
    sums = []
    for i in range(2):
        total = None
        for ref in (own_ref,) + refs:
            k = 2 * count + i * PAD
            part = restored(ref[i * count : (i + 1) * count], ref[k : k + 1])
            total = part if total is None else total + part
        sums.append(total)
    acts, grads = sums
    height = acts.shape[1] // 8
    group, col, sub = place_ref[0], place_ref[2], place_ref[3]
    for j in range(count // tokens):
        rows = slice(j * tokens, (j + 1) * tokens)
        scratch[j] = lax.dot_general(
            acts[rows], grads[rows], (((0,), (0,)), ((), ())), precision=HIGHEST, preferred_element_type=jnp.float32
        )
        for k in range(4):
            for s in range(2):
                start = (((col ^ (k % 2)) * 2 + (sub ^ s)) * 2 + (group ^ (k // 2))) * height
                outs[k][s, j * height : (j + 1) * height] = scratch[j, pl.ds(pl.multiple_of(start, height), height)]


def pack_kernel(*refs):
    kept, got_ref, out_ref = refs[:-2], refs[-2], refs[-1]
    lanes = got_ref.shape[-1]
    parts = jnp.concatenate([ref[0] for ref in kept] + [got_ref[...].reshape(-1, lanes)], 0)
    k = exponents(parts)
    out_ref[: parts.shape[0]] = scaled(parts, k)
    out_ref[parts.shape[0] :] = jnp.broadcast_to(k, (PAD, lanes))


def pack_scores_kernel(scores_ref, out_ref):
    scores = scores_ref[...]
    k = exponents(scores)
    out_ref[: scores.shape[0]] = scaled(scores, k)
    out_ref[scores.shape[0] :] = jnp.broadcast_to(k, (PAD, scores.shape[1]))


def sum_scores_kernel(*refs):
    out_ref = refs[-1]
    count = out_ref.shape[0]
    out_ref[...] = tree_sum([restored(ref[:count], ref[count : count + 1]) for ref in refs[:-1]])


def split(block):
    high = block.astype(jnp.bfloat16)
    return high, (block - high.astype(jnp.float32)).astype(jnp.bfloat16)


def gram_split_kernel(place_ref, gram_ref, away_ref, home_ref, mark_ref, buffer, sems, *, group):
    slots, tile, width = buffer.shape
    steps = away_ref.shape[0] // (2 * tile)
    column = pl.multiple_of(place_ref[0] * width, width)
    sub = place_ref[3]

    def copy(i):
        half = lax.rem(i // steps + 1 + sub, 2)
        rows = pl.ds(pl.multiple_of((half * steps + lax.rem(i, steps)) * tile, tile), tile)
        slot = lax.rem(i, slots)
        return pltpu.make_async_copy(gram_ref.at[rows, pl.ds(column, width)], buffer.at[slot], sems.at[slot])

    for i in range(slots - 1):
        copy(i).start()

    for part, out_ref in enumerate((away_ref, home_ref)):

        @pl.loop(0, steps)
        def _(j):
            i = part * steps + j

            @pl.when(i + slots - 1 < 2 * steps)
            def _():
                copy(i + slots - 1).start()

            copy(i).wait()
            high, low = split(buffer[lax.rem(i, slots)])
            start = (j + j // (group // tile) * (group // tile)) * tile
            out_ref[pl.ds(pl.multiple_of(start, tile), tile)] = high
            out_ref[pl.ds(pl.multiple_of(start + group, tile), tile)] = low

    mark_ref[...] = jnp.zeros_like(mark_ref)


def gram_split(inverse_gram, place, tile=256, slots=4):
    rows, width = inverse_gram.shape
    half = width // 2
    group = min(TILE, rows // 2)
    tile = min(tile, group)
    return pl.pallas_call(
        functools.partial(gram_split_kernel, group=group),
        in_specs=[pl.BlockSpec(memory_space=pltpu.SMEM), pl.BlockSpec(memory_space=pltpu.HBM)],
        out_specs=[WHOLE] * 3,
        out_shape=[pltpu.VMEM((rows, half), jnp.bfloat16)] * 2 + [jax.ShapeDtypeStruct((8, 128), jnp.float32)],
        scratch_shapes=[pltpu.VMEM((slots, tile, half), jnp.float32), pltpu.SemaphoreType.DMA((slots,))],
        compiler_params=pltpu.CompilerParams(vmem_limit_bytes=SPLIT_LIMIT),
        cost_estimate=pl.CostEstimate(flops=0, bytes_accessed=4 * rows * half, transcendentals=0),
        name="gram_split",
    )(place, inverse_gram)


def gram_rows(group, gram_ref, terms, out_ref):
    queries, width = 2 * out_ref.shape[1], out_ref.shape[2]
    tile = min(TILE, width)

    @pl.loop(0, width // tile)
    def _(i):
        rows = pl.ds(pl.multiple_of(2 * i * tile, 2 * tile), 2 * tile)
        part = jnp.dot(gram_ref[rows], terms[...], preferred_element_type=jnp.float32)
        part = part[:tile] + part[tile:]
        done = (part[:, :queries] + part[:, queries:]).T
        columns = pl.ds(pl.multiple_of(i * tile, tile), tile)
        for g in range(2):
            out_ref[g ^ group, :, columns] = done[g * (queries // 2) : (g + 1) * (queries // 2)]


def away_kernel(place_ref, gram_ref, *refs, row_count, own):
    sources, (out_ref, terms, natural) = refs[:row_count], refs[row_count:]
    group, row, col, sub = (place_ref[i] for i in range(4))
    height, queries, lanes = natural.shape
    for z in range(row_count):
        count = sources[z].shape[0] - PAD
        piece = restored(sources[z][:count], sources[z][count : count + 1])
        for place in range(8):
            s, g, c = place // 4, place // 2 % 2, place % 2
            first = ((((g ^ group) * 2 + (c ^ col)) * 2 + (s ^ sub)) * row_count + (z ^ row)) * own
            for j in range(own):
                start = (place * own + j) * height
                natural[:, pl.ds(first + j, 1), :] = piece[start : start + height].reshape(height, 1, lanes)
    for a in range(height):
        block = natural[a]
        high = block.astype(jnp.bfloat16).astype(jnp.float32)
        both = jnp.concatenate([high, block - high], 0).T
        terms[a * lanes : (a + 1) * lanes] = both.astype(jnp.bfloat16)
    gram_rows(group, gram_ref, terms, out_ref)


def home_kernel(place_ref, gram_ref, terms_ref, out_ref):
    gram_rows(place_ref[0], gram_ref, terms_ref, out_ref)


TILE = 1024
SPLIT_LIMIT = 12 * MIB


def gram_product(place, away_gram, home_gram, sources, own, lanes):
    rows, half = away_gram.shape
    row_count = len(sources)
    queries = 8 * row_count * own
    part = jax.ShapeDtypeStruct((2, queries // 2, rows // 2), jnp.float32)
    terms = jax.ShapeDtypeStruct((half, 2 * queries), jnp.bfloat16)
    common = dict(
        compiler_params=pltpu.CompilerParams(vmem_limit_bytes=8 * MIB),
        cost_estimate=pl.CostEstimate(flops=4 * queries * rows * half, bytes_accessed=2 * rows * half, transcendentals=0),
    )
    index = pl.BlockSpec(memory_space=pltpu.SMEM)
    away_gram = pltpu.with_memory_space_constraint(away_gram, pltpu.VMEM)
    home_gram = pltpu.with_memory_space_constraint(home_gram, pltpu.VMEM)
    away, terms = pl.pallas_call(
        functools.partial(away_kernel, row_count=row_count, own=own),
        in_specs=[index] + [WHOLE] * (1 + row_count),
        out_specs=[WHOLE, WHOLE],
        out_shape=[part, terms],
        scratch_shapes=[pltpu.VMEM((half // lanes, queries, lanes), jnp.float32)],
        name="away",
        **common,
    )(place, away_gram, *sources)
    got = swapped(away, "sub")
    home = pl.pallas_call(
        home_kernel, in_specs=[index] + [WHOLE] * 2, out_specs=WHOLE, out_shape=part, name="home", **common
    )(place, home_gram, terms)
    return home + got


def others(pick, axis):
    size = lax.axis_size(axis)
    index = lax.axis_index(axis)
    return [lax.ppermute(pick(index ^ k), axis, [(i, i ^ k) for i in range(size)]) for k in range(1, size)]


def tree_sum(terms):
    while len(terms) > 1:
        terms = [terms[i] + terms[i + 1] for i in range(0, len(terms), 2)]
    return terms[0]


def swapped(array, axis):
    return others(lambda d: array, axis)[0]


def peers(pick):
    return [lax.ppermute(pick(k), ("groups", "col"), [(i, i ^ k) for i in range(4)]) for k in (1, 2, 3)]


def call(kernel, shapes, name, *args, specs=None, scratch=()):
    specs = specs or [pl.BlockSpec(memory_space=pltpu.SMEM) if a.dtype == jnp.int32 else WHOLE for a in args]
    many = isinstance(shapes, list)
    shapes = [jax.ShapeDtypeStruct(shape, jnp.float32) for shape in (shapes if many else [shapes])]
    outs = pl.pallas_call(
        kernel,
        in_specs=specs,
        out_specs=[WHOLE] * len(shapes),
        out_shape=shapes,
        scratch_shapes=list(scratch),
        compiler_params=pltpu.CompilerParams(vmem_limit_bytes=4 * MIB),
        name=name,
    )(*args)
    return outs if many else outs[0]


def body(query_acts, query_grads, proj_in, proj_out, inverse_gram, store_slab):
    row_count = lax.axis_size("row")
    place = jnp.stack([lax.axis_index(axis) for axis in ("groups", "row", "col", "sub")])
    queries, tokens = query_acts.shape[:2]
    own = queries // row_count
    in_width, out_width = proj_in.shape[1], proj_out.shape[1]
    got = []
    for targets in (range(row_count)[: row_count // 2 - 1 : -1], range(row_count)[: row_count // 2][::-1]):
        parts = project(targets, row_count, place, query_acts, query_grads, proj_in, proj_out)
        for k, part in zip(targets, parts):
            if k:
                got.append(lax.ppermute(part.astype(jnp.float16), "row", [(i, i ^ k) for i in range(row_count)]))
    away_gram, home_gram, mark = gram_split(inverse_gram, place)
    height = own * in_width // 8
    near = call(
        functools.partial(kron_kernel, tokens=tokens),
        [(2, height, out_width)] * 4,
        "kron",
        place,
        mark,
        parts[-1],
        *[x.astype(jnp.float32) for x in got],
        scratch=[pltpu.VMEM((own, in_width, out_width), jnp.float32)],
    )
    near = [near[0]] + peers(lambda k: near[k])
    got = swapped(jnp.stack([x[1] for x in near]), "sub")
    packed = call(pack_kernel, (8 * height + PAD, out_width), "pack", *near, got)
    wire = packed.astype(jnp.float16)
    sources = [packed] + [got.astype(jnp.float32) for got in others(lambda d: wire, "row")]
    total = gram_product(place, away_gram, home_gram, sources, own, out_width)
    wire = total.astype(jnp.bfloat16)
    total = total[0]
    for got in peers(lambda k: wire[k // 2]):
        total = total + got.astype(jnp.float32)
    high = lax.reduce_precision(total, 8, 7)
    terms = jnp.concatenate([high, total - high], 0).astype(jnp.bfloat16)
    scores = lax.dot_general(
        terms, store_slab, (((1,), (1,)), ((), ())), preferred_element_type=jnp.float32
    )
    scores = scores[: total.shape[0]] + scores[total.shape[0] :]
    scores = scores + swapped(scores, "sub")
    packed = call(pack_scores_kernel, (scores.shape[0] + PAD, scores.shape[1]), "pack_scores", scores)
    packed = lax.reduce_precision(packed, 5, 10)
    wire = packed.astype(jnp.float16)
    sources = [packed] + [got.astype(jnp.float32) for got in others(lambda d: wire, "row")]
    return call(sum_scores_kernel, scores.shape, "sum_scores", *sources)


def solution(mesh):
    shape = mesh.shape
    rows = shape["row"]
    paired = shape["groups"] == shape["col"] == shape["sub"] == 2 and rows & (rows - 1) == 0

    def chosen(query_acts, query_grads, proj_in, proj_out, *rest):
        queries = query_acts.shape[0] // (shape["groups"] * shape["col"] * shape["sub"])
        square = proj_in.shape[1] == proj_out.shape[1] == 128
        chosen_body = body if paired and square and queries % rows == 0 else plain_body
        return jax.shard_map(
            chosen_body,
            mesh=mesh,
            in_specs=(
                P(("groups", "col", "sub"), None, "row"),
                P(("groups", "col", "sub"), None, "row"),
                P("row", None),
                P("row", None),
                P("row", ("col", "sub")),
                P(("groups", "col"), ("row", "sub")),
            ),
            out_specs=P("groups", "col"),
            check_vma=False,
        )(query_acts, query_grads, proj_in, proj_out, *rest)

    return chosen
```

```python
import functools

import jax
import jax.numpy as jnp
from jax import lax
from jax.experimental import pallas as pl
from jax.experimental.pallas import tpu as pltpu
from jax.sharding import PartitionSpec as P

HIGHEST = lax.Precision.HIGHEST


def plain_body(query_acts, query_grads, proj_in, proj_out, inverse_gram, store_slab):
    row_count = lax.axis_size("row")
    row_index = lax.axis_index("row")
    sub_index = lax.axis_index("sub")
    in_width = proj_in.shape[1]
    act_part = jnp.einsum("qtd,dk->qtk", query_acts, proj_in, preferred_element_type=jnp.float32)
    grad_part = jnp.einsum("qtd,dk->qtk", query_grads, proj_out, preferred_element_type=jnp.float32)
    store_width = store_slab.shape[1]
    row_block = in_width // row_count
    act_whole, grad_proj = lax.psum((act_part, grad_part), "row")
    act_proj = lax.dynamic_slice_in_dim(act_whole, row_index * row_block, row_block, 2)
    kron_part = jnp.einsum("qta,qtb->qab", act_proj, grad_proj, precision=HIGHEST)
    kron_feats = lax.all_gather(kron_part, ("col", "sub"), axis=0, tiled=True)
    features_flat = kron_feats.reshape(kron_feats.shape[0], -1)
    precond_part = jnp.dot(features_flat, inverse_gram, precision=HIGHEST)
    precond_block = lax.psum(precond_part, "row").astype(jnp.bfloat16)
    precond_full = lax.all_gather(precond_block, ("col", "sub"), axis=1, tiled=True)
    store_start = (row_index * lax.axis_size("sub") + sub_index) * store_width
    precond_mine = lax.dynamic_slice_in_dim(precond_full, store_start, store_width, 1)
    score_part = lax.dot_general(
        precond_mine, store_slab, (((1,), (1,)), ((), ())), preferred_element_type=jnp.float32
    )
    return lax.psum(score_part, ("row", "sub"))


PAD = 8
SHIFT = 13.0
LOG2E = 1.4426950408889634
WHOLE = pl.BlockSpec(memory_space=pltpu.VMEM)
MIB = 2**20


def exponents(part):
    top = jnp.max(jnp.abs(part), axis=0, keepdims=True)
    return jnp.ceil(jnp.log(jnp.clip(top, 1e-30, 1e30)) * LOG2E)


def scaled(part, k):
    return part * jnp.exp2(SHIFT - k)


def restored(part, k):
    return part * jnp.exp2(k - SHIFT)


def project_kernel(place_ref, *refs, targets):
    inputs, outs, (inputs_buf, weights_buf, sems, weights_sems) = refs[:4], refs[4:-4], refs[-4:]
    own, tokens, width = inputs_buf.shape[2:]
    count = own * tokens
    row = place_ref[1]
    weights = [pltpu.make_async_copy(inputs[2 + i], weights_buf.at[i], weights_sems.at[i]) for i in range(2)]
    copies = {}
    for k in range(len(targets)):
        for i in range(2):
            if k == 0:
                weights[i].start()
            rows = pl.ds((row ^ targets[k]) * own, own)
            copies[k, i] = pltpu.make_async_copy(inputs[i].at[rows], inputs_buf.at[i, k], sems.at[i, k])
            copies[k, i].start()
    for k in range(len(targets)):
        for i in range(2):
            if k == 0:
                weights[i].wait()
            copies[k, i].wait()
            x = inputs_buf[i, k].reshape(count, width)
            part = jnp.dot(x, weights_buf[i], preferred_element_type=jnp.float32)
            e = exponents(part)
            outs[k][i * count : (i + 1) * count] = scaled(part, e)
            outs[k][2 * count + i * PAD : 2 * count + (i + 1) * PAD] = jnp.broadcast_to(e, (PAD, e.shape[1]))


def project(targets, row_count, place, query_acts, query_grads, proj_in, proj_out):
    queries, tokens, width = query_acts.shape
    own = queries // row_count
    out_width = proj_in.shape[1]
    height = 2 * own * tokens + 2 * PAD
    far = pl.BlockSpec(memory_space=pltpu.HBM)
    return pl.pallas_call(
        functools.partial(project_kernel, targets=targets),
        in_specs=[pl.BlockSpec(memory_space=pltpu.SMEM)] + [far] * 4,
        out_specs=[WHOLE] * len(targets),
        out_shape=[jax.ShapeDtypeStruct((height, out_width), jnp.float32)] * len(targets),
        scratch_shapes=[
            pltpu.VMEM((2, len(targets), own, tokens, width), query_acts.dtype),
            pltpu.VMEM((2,) + proj_in.shape, proj_in.dtype),
            pltpu.SemaphoreType.DMA((2, len(targets))),
            pltpu.SemaphoreType.DMA((2,)),
        ],
        compiler_params=pltpu.CompilerParams(vmem_limit_bytes=8 * MIB),
        name="project",
    )(place, *[pltpu.with_memory_space_constraint(x, pltpu.HBM) for x in (query_acts, query_grads, proj_in, proj_out)])


def kron_kernel(place_ref, after_ref, own_ref, *refs, tokens):
    del after_ref
    refs, outs, scratch = refs[:-5], refs[-5:-1], refs[-1]
    count = (own_ref.shape[0] - 2 * PAD) // 2
    sums = []
    for i in range(2):
        total = None
        for ref in (own_ref,) + refs:
            k = 2 * count + i * PAD
            part = restored(ref[i * count : (i + 1) * count], ref[k : k + 1])
            total = part if total is None else total + part
        sums.append(total)
    acts, grads = sums
    height = acts.shape[1] // 8
    group, col, sub = place_ref[0], place_ref[2], place_ref[3]
    for j in range(count // tokens):
        rows = slice(j * tokens, (j + 1) * tokens)
        scratch[j] = lax.dot_general(
            acts[rows], grads[rows], (((0,), (0,)), ((), ())), precision=HIGHEST, preferred_element_type=jnp.float32
        )
        for k in range(4):
            for s in range(2):
                start = (((col ^ (k % 2)) * 2 + (sub ^ s)) * 2 + (group ^ (k // 2))) * height
                outs[k][s, j * height : (j + 1) * height] = scratch[j, pl.ds(pl.multiple_of(start, height), height)]


def pack_kernel(*refs):
    kept, got_ref, out_ref = refs[:-2], refs[-2], refs[-1]
    lanes = got_ref.shape[-1]
    parts = jnp.concatenate([ref[0] for ref in kept] + [got_ref[...].reshape(-1, lanes)], 0)
    k = exponents(parts)
    out_ref[: parts.shape[0]] = scaled(parts, k)
    out_ref[parts.shape[0] :] = jnp.broadcast_to(k, (PAD, lanes))


def pack_scores_kernel(scores_ref, out_ref):
    scores = scores_ref[...]
    k = exponents(scores)
    out_ref[: scores.shape[0]] = scaled(scores, k)
    out_ref[scores.shape[0] :] = jnp.broadcast_to(k, (PAD, scores.shape[1]))


def sum_scores_kernel(*refs):
    out_ref = refs[-1]
    count = out_ref.shape[0]
    out_ref[...] = tree_sum([restored(ref[:count], ref[count : count + 1]) for ref in refs[:-1]])


def split(block):
    high = block.astype(jnp.bfloat16)
    return high, (block - high.astype(jnp.float32)).astype(jnp.bfloat16)


def gram_split_kernel(place_ref, after_ref, gram_ref, *refs, first):
    del after_ref
    outs, (mark_ref, buffer, sems) = refs[:-3], refs[-3:]
    slots, tile, width = buffer.shape
    quarter = outs[0].shape[0] // 2
    steps = quarter // tile
    total = steps * len(outs)
    column = pl.multiple_of(place_ref[0] * width, width)
    sub = place_ref[3]

    def copy(i):
        part = first + i // steps
        start = (lax.rem(part // 2 + 1 + sub, 2) * 2 + lax.rem(part, 2)) * quarter + lax.rem(i, steps) * tile
        rows = pl.ds(pl.multiple_of(start, tile), tile)
        slot = lax.rem(i, slots)
        return pltpu.make_async_copy(gram_ref.at[rows, pl.ds(column, width)], buffer.at[slot], sems.at[slot])

    for i in range(min(slots - 1, total)):
        copy(i).start()

    for part, out_ref in enumerate(outs):

        @pl.loop(0, steps)
        def _(j):
            i = part * steps + j

            @pl.when(i + slots - 1 < total)
            def _():
                copy(i + slots - 1).start()

            copy(i).wait()
            high, low = split(buffer[lax.rem(i, slots)])
            start = pl.multiple_of(j * tile, tile)
            out_ref[pl.ds(start, tile)] = high
            out_ref[pl.ds(start + quarter, tile)] = low

    mark_ref[...] = jnp.zeros_like(mark_ref)


def gram_split(place, after, inverse_gram, first, count, tile=256, slots=4):
    rows, width = inverse_gram.shape
    half, quarter = width // 2, rows // 4
    tile = min(tile, quarter)
    *quarters, mark = pl.pallas_call(
        functools.partial(gram_split_kernel, first=first),
        in_specs=[pl.BlockSpec(memory_space=pltpu.SMEM), WHOLE, pl.BlockSpec(memory_space=pltpu.HBM)],
        out_specs=[WHOLE] * (count + 1),
        out_shape=[pltpu.VMEM((2 * quarter, half), jnp.bfloat16)] * count
        + [jax.ShapeDtypeStruct((8, 128), jnp.float32)],
        scratch_shapes=[pltpu.VMEM((slots, tile, half), jnp.float32), pltpu.SemaphoreType.DMA((slots,))],
        compiler_params=pltpu.CompilerParams(vmem_limit_bytes=12 * MIB),
        cost_estimate=pl.CostEstimate(flops=0, bytes_accessed=count * 4 * quarter * half, transcendentals=0),
        name="gram_split",
    )(place, after, inverse_gram)
    return [pltpu.with_memory_space_constraint(x, pltpu.VMEM) for x in quarters], mark


def gram_rows(group, gram_ref, terms, write):
    quarter = gram_ref.shape[0] // 2
    queries = terms.shape[1] // 2
    part = jnp.dot(gram_ref[...], terms[...], preferred_element_type=jnp.float32)
    part = part[:quarter] + part[quarter:]
    done = (part[:, :queries] + part[:, queries:]).T
    for g in range(2):
        write(g ^ group, done[g * (queries // 2) : (g + 1) * (queries // 2)])


def away_kernel(place_ref, after_ref, *refs, row_count, own):
    del after_ref
    grams, sources, (out_ref, terms, natural) = refs[:2], refs[2 : 2 + row_count], refs[2 + row_count :]
    group, row, col, sub = (place_ref[i] for i in range(4))
    height, queries, lanes = natural.shape
    for z in range(row_count):
        count = sources[z].shape[0] - PAD
        piece = restored(sources[z][:count], sources[z][count : count + 1])
        for place in range(8):
            s, g, c = place // 4, place // 2 % 2, place % 2
            first = ((((g ^ group) * 2 + (c ^ col)) * 2 + (s ^ sub)) * row_count + (z ^ row)) * own
            for j in range(own):
                start = (place * own + j) * height
                natural[:, pl.ds(first + j, 1), :] = piece[start : start + height].reshape(height, 1, lanes)
    for a in range(height):
        block = natural[a]
        high = block.astype(jnp.bfloat16).astype(jnp.float32)
        both = jnp.concatenate([high, block - high], 0).T
        terms[a * lanes : (a + 1) * lanes] = both.astype(jnp.bfloat16)
    for i in range(2):

        def write(g, value):
            out_ref[i, g] = value

        gram_rows(group, grams[i], terms, write)


def home_kernel(place_ref, gram_ref, terms_ref, *refs):
    out_ref = refs[-1]

    def write(g, value):
        out_ref[g] = value

    gram_rows(place_ref[0], gram_ref, terms_ref, write)


def join_kernel(early_ref, early_got_ref, late_ref, late_got_ref, early_out, early_wire, late_out, late_wire):
    early = early_ref[...] + early_got_ref[...].astype(jnp.float32)
    early_out[...] = early
    early_wire[...] = early.astype(jnp.bfloat16)
    late_out[...] = late_ref[0] + late_got_ref[0]
    late_wire[...] = (late_ref[1] + late_got_ref[1]).astype(jnp.bfloat16)


def gram_product(place, after, quarters, sources, own, lanes):
    quarter, half = quarters[0].shape[0] // 2, quarters[0].shape[1]
    row_count = len(sources)
    queries = 8 * row_count * own
    index = pl.BlockSpec(memory_space=pltpu.SMEM)

    def common(count):
        return dict(
            compiler_params=pltpu.CompilerParams(vmem_limit_bytes=8 * MIB),
            cost_estimate=pl.CostEstimate(
                flops=8 * count * queries * quarter * half, bytes_accessed=count * quarter * half, transcendentals=0
            ),
        )

    away, terms = pl.pallas_call(
        functools.partial(away_kernel, row_count=row_count, own=own),
        in_specs=[index] + [WHOLE] * (3 + row_count),
        out_specs=[WHOLE, WHOLE],
        out_shape=[
            jax.ShapeDtypeStruct((2, 2, queries // 2, quarter), jnp.float32),
            jax.ShapeDtypeStruct((half, 2 * queries), jnp.bfloat16),
        ],
        scratch_shapes=[pltpu.VMEM((half // lanes, queries, lanes), jnp.float32)],
        name="away",
        **common(2),
    )(place, after, *quarters[:2], *sources)
    got = swapped(away, "sub")

    def home(i, *after):
        return pl.pallas_call(
            home_kernel,
            in_specs=[index] + [WHOLE] * (2 + len(after)),
            out_specs=WHOLE,
            out_shape=jax.ShapeDtypeStruct((2, queries // 2, quarter), jnp.float32),
            name="home",
            **common(1),
        )(place, quarters[2 + i], terms, *after)

    early = home(0) + got[0]
    wire = early[1].astype(jnp.bfloat16)
    late = home(1, wire)
    shape = (queries // 2, quarter)
    early, early_wire, late, late_wire = pl.pallas_call(
        join_kernel,
        in_specs=[WHOLE] * 4,
        out_specs=[WHOLE] * 4,
        out_shape=[jax.ShapeDtypeStruct(shape, kind) for kind in (jnp.float32, jnp.bfloat16) * 2],
        compiler_params=pltpu.CompilerParams(vmem_limit_bytes=4 * MIB),
        name="join",
    )(early[0], swapped(wire, "groups"), late, got[1])
    late = late + swapped(late_wire, "groups").astype(jnp.float32)
    early = early + swapped(early_wire, "col").astype(jnp.float32)
    late = late + swapped(late.astype(jnp.bfloat16), "col").astype(jnp.float32)
    return jnp.concatenate([early, late], 1)


def others(pick, axis):
    size = lax.axis_size(axis)
    index = lax.axis_index(axis)
    return [lax.ppermute(pick(index ^ k), axis, [(i, i ^ k) for i in range(size)]) for k in range(1, size)]


def tree_sum(terms):
    while len(terms) > 1:
        terms = [terms[i] + terms[i + 1] for i in range(0, len(terms), 2)]
    return terms[0]


def swapped(array, axis):
    return others(lambda d: array, axis)[0]


def peers(pick):
    return [lax.ppermute(pick(k), ("groups", "col"), [(i, i ^ k) for i in range(4)]) for k in (1, 2, 3)]


def call(kernel, shapes, name, *args, specs=None, scratch=()):
    specs = specs or [pl.BlockSpec(memory_space=pltpu.SMEM) if a.dtype == jnp.int32 else WHOLE for a in args]
    many = isinstance(shapes, list)
    shapes = [jax.ShapeDtypeStruct(shape, jnp.float32) for shape in (shapes if many else [shapes])]
    outs = pl.pallas_call(
        kernel,
        in_specs=specs,
        out_specs=[WHOLE] * len(shapes),
        out_shape=shapes,
        scratch_shapes=list(scratch),
        compiler_params=pltpu.CompilerParams(vmem_limit_bytes=4 * MIB),
        name=name,
    )(*args)
    return outs if many else outs[0]


def body(query_acts, query_grads, proj_in, proj_out, inverse_gram, store_slab):
    row_count = lax.axis_size("row")
    place = jnp.stack([lax.axis_index(axis) for axis in ("groups", "row", "col", "sub")])
    queries, tokens = query_acts.shape[:2]
    own = queries // row_count
    in_width, out_width = proj_in.shape[1], proj_out.shape[1]
    got = []
    for targets in (range(row_count)[: row_count // 2 - 1 : -1], range(row_count)[: row_count // 2][::-1]):
        parts = project(targets, row_count, place, query_acts, query_grads, proj_in, proj_out)
        for k, part in zip(targets, parts):
            if k:
                got.append(lax.ppermute(part.astype(jnp.float16), "row", [(i, i ^ k) for i in range(row_count)]))
    first, mark = gram_split(place, parts[-1], inverse_gram, 0, 3)
    height = own * in_width // 8
    near = call(
        functools.partial(kron_kernel, tokens=tokens),
        [(2, height, out_width)] * 4,
        "kron",
        place,
        mark,
        parts[-1],
        *[x.astype(jnp.float32) for x in got],
        scratch=[pltpu.VMEM((own, in_width, out_width), jnp.float32)],
    )
    near = [near[0]] + peers(lambda k: near[k])
    got = swapped(jnp.stack([x[1] for x in near]), "sub")
    packed = call(pack_kernel, (8 * height + PAD, out_width), "pack", *near, got)
    wire = packed.astype(jnp.float16)
    sources = [packed] + [got.astype(jnp.float32) for got in others(lambda d: wire, "row")]
    last, mark = gram_split(place, packed, inverse_gram, 3, 1)
    total = gram_product(place, mark, first + last, sources, own, out_width)
    high = lax.reduce_precision(total, 8, 7)
    terms = jnp.concatenate([high, total - high], 0).astype(jnp.bfloat16)
    scores = lax.dot_general(
        terms, store_slab, (((1,), (1,)), ((), ())), preferred_element_type=jnp.float32
    )
    scores = scores[: total.shape[0]] + scores[total.shape[0] :]
    scores = scores + swapped(scores, "sub")
    packed = call(pack_scores_kernel, (scores.shape[0] + PAD, scores.shape[1]), "pack_scores", scores)
    packed = lax.reduce_precision(packed, 5, 10)
    wire = packed.astype(jnp.float16)
    sources = [packed] + [got.astype(jnp.float32) for got in others(lambda d: wire, "row")]
    return call(sum_scores_kernel, scores.shape, "sum_scores", *sources)


def solution(mesh):
    shape = mesh.shape
    rows = shape["row"]
    paired = shape["groups"] == shape["col"] == shape["sub"] == 2 and rows & (rows - 1) == 0

    def chosen(query_acts, query_grads, proj_in, proj_out, *rest):
        queries = query_acts.shape[0] // (shape["groups"] * shape["col"] * shape["sub"])
        square = proj_in.shape[1] == proj_out.shape[1] == 128
        chosen_body = body if paired and square and queries % rows == 0 else plain_body
        return jax.shard_map(
            chosen_body,
            mesh=mesh,
            in_specs=(
                P(("groups", "col", "sub"), None, "row"),
                P(("groups", "col", "sub"), None, "row"),
                P("row", None),
                P("row", None),
                P("row", ("col", "sub")),
                P(("groups", "col"), ("row", "sub")),
            ),
            out_specs=P("groups", "col"),
            check_vma=False,
        )(query_acts, query_grads, proj_in, proj_out, *rest)

    return chosen
```

```python
import functools

import jax
import jax.numpy as jnp
from jax import lax
from jax.experimental import pallas as pl
from jax.experimental.pallas import tpu as pltpu
from jax.sharding import PartitionSpec as P

HIGHEST = lax.Precision.HIGHEST


def plain_body(query_acts, query_grads, proj_in, proj_out, inverse_gram, store_slab):
    row_count = lax.axis_size("row")
    row_index = lax.axis_index("row")
    sub_index = lax.axis_index("sub")
    in_width = proj_in.shape[1]
    act_part = jnp.einsum("qtd,dk->qtk", query_acts, proj_in, preferred_element_type=jnp.float32)
    grad_part = jnp.einsum("qtd,dk->qtk", query_grads, proj_out, preferred_element_type=jnp.float32)
    store_width = store_slab.shape[1]
    row_block = in_width // row_count
    act_whole, grad_proj = lax.psum((act_part, grad_part), "row")
    act_proj = lax.dynamic_slice_in_dim(act_whole, row_index * row_block, row_block, 2)
    kron_part = jnp.einsum("qta,qtb->qab", act_proj, grad_proj, precision=HIGHEST)
    kron_feats = lax.all_gather(kron_part, ("col", "sub"), axis=0, tiled=True)
    features_flat = kron_feats.reshape(kron_feats.shape[0], -1)
    precond_part = jnp.dot(features_flat, inverse_gram, precision=HIGHEST)
    precond_block = lax.psum(precond_part, "row").astype(jnp.bfloat16)
    precond_full = lax.all_gather(precond_block, ("col", "sub"), axis=1, tiled=True)
    store_start = (row_index * lax.axis_size("sub") + sub_index) * store_width
    precond_mine = lax.dynamic_slice_in_dim(precond_full, store_start, store_width, 1)
    score_part = lax.dot_general(
        precond_mine, store_slab, (((1,), (1,)), ((), ())), preferred_element_type=jnp.float32
    )
    return lax.psum(score_part, ("row", "sub"))


PAD = 8
SHIFT = 13.0
LOG2E = 1.4426950408889634
WHOLE = pl.BlockSpec(memory_space=pltpu.VMEM)
MIB = 2**20


def exponents(part):
    top = jnp.max(jnp.abs(part), axis=0, keepdims=True)
    return jnp.ceil(jnp.log(jnp.clip(top, 1e-30, 1e30)) * LOG2E)


def scaled(part, k):
    return part * jnp.exp2(SHIFT - k)


def restored(part, k):
    return part * jnp.exp2(k - SHIFT)


def project_kernel(place_ref, *refs, targets):
    inputs, outs, (inputs_buf, weights_buf, sems, weights_sems) = refs[:4], refs[4:-4], refs[-4:]
    own, tokens, width = inputs_buf.shape[2:]
    count = own * tokens
    row = place_ref[1]
    weights = [pltpu.make_async_copy(inputs[2 + i], weights_buf.at[i], weights_sems.at[i]) for i in range(2)]
    copies = {}
    for k in range(len(targets)):
        for i in range(2):
            if k == 0:
                weights[i].start()
            rows = pl.ds((row ^ targets[k]) * own, own)
            copies[k, i] = pltpu.make_async_copy(inputs[i].at[rows], inputs_buf.at[i, k], sems.at[i, k])
            copies[k, i].start()
    for k in range(len(targets)):
        for i in range(2):
            if k == 0:
                weights[i].wait()
            copies[k, i].wait()
            x = inputs_buf[i, k].reshape(count, width)
            part = jnp.dot(x, weights_buf[i], preferred_element_type=jnp.float32)
            e = exponents(part)
            outs[k][i * count : (i + 1) * count] = scaled(part, e)
            outs[k][2 * count + i * PAD : 2 * count + (i + 1) * PAD] = jnp.broadcast_to(e, (PAD, e.shape[1]))


def project(targets, row_count, place, query_acts, query_grads, proj_in, proj_out):
    queries, tokens, width = query_acts.shape
    own = queries // row_count
    out_width = proj_in.shape[1]
    height = 2 * own * tokens + 2 * PAD
    far = pl.BlockSpec(memory_space=pltpu.HBM)
    return pl.pallas_call(
        functools.partial(project_kernel, targets=targets),
        in_specs=[pl.BlockSpec(memory_space=pltpu.SMEM)] + [far] * 4,
        out_specs=[WHOLE] * len(targets),
        out_shape=[jax.ShapeDtypeStruct((height, out_width), jnp.float32)] * len(targets),
        scratch_shapes=[
            pltpu.VMEM((2, len(targets), own, tokens, width), query_acts.dtype),
            pltpu.VMEM((2,) + proj_in.shape, proj_in.dtype),
            pltpu.SemaphoreType.DMA((2, len(targets))),
            pltpu.SemaphoreType.DMA((2,)),
        ],
        compiler_params=pltpu.CompilerParams(vmem_limit_bytes=8 * MIB),
        name="project",
    )(place, *[pltpu.with_memory_space_constraint(x, pltpu.HBM) for x in (query_acts, query_grads, proj_in, proj_out)])


def kron_kernel(place_ref, after_ref, own_ref, *refs, tokens):
    del after_ref
    refs, outs, scratch = refs[:-5], refs[-5:-1], refs[-1]
    count = (own_ref.shape[0] - 2 * PAD) // 2
    sums = []
    for i in range(2):
        total = None
        for ref in (own_ref,) + refs:
            k = 2 * count + i * PAD
            part = restored(ref[i * count : (i + 1) * count], ref[k : k + 1])
            total = part if total is None else total + part
        sums.append(total)
    acts, grads = sums
    height = acts.shape[1] // 8
    group, col, sub = place_ref[0], place_ref[2], place_ref[3]
    for j in range(count // tokens):
        rows = slice(j * tokens, (j + 1) * tokens)
        scratch[j] = lax.dot_general(
            acts[rows], grads[rows], (((0,), (0,)), ((), ())), precision=HIGHEST, preferred_element_type=jnp.float32
        )
        for k in range(4):
            for s in range(2):
                start = (((col ^ (k % 2)) * 2 + (sub ^ s)) * 2 + (group ^ (k // 2))) * height
                outs[k][s, j * height : (j + 1) * height] = scratch[j, pl.ds(pl.multiple_of(start, height), height)]


def pack_kernel(after_ref, *refs):
    del after_ref
    kept, out_ref = refs[:-1], refs[-1]
    lanes = out_ref.shape[1]
    parts = jnp.concatenate([ref[i] for ref in kept for i in range(4 // len(kept))], 0)
    k = exponents(parts)
    out_ref[: parts.shape[0]] = scaled(parts, k)
    out_ref[parts.shape[0] :] = jnp.broadcast_to(k, (PAD, lanes))


def gather_kernel(after_ref, *refs):
    del after_ref
    for i, ref in enumerate(refs[:-1]):
        refs[-1][i] = ref[1]


def pack_scores_kernel(scores_ref, out_ref):
    scores = scores_ref[...]
    k = exponents(scores)
    out_ref[: scores.shape[0]] = scaled(scores, k)
    out_ref[scores.shape[0] :] = jnp.broadcast_to(k, (PAD, scores.shape[1]))


def sum_scores_kernel(*refs):
    out_ref = refs[-1]
    count = out_ref.shape[0]
    out_ref[...] = tree_sum([restored(ref[:count], ref[count : count + 1]) for ref in refs[:-1]])


def split(block):
    high = block.astype(jnp.bfloat16)
    return high, (block - high.astype(jnp.float32)).astype(jnp.bfloat16)


def gram_split_kernel(place_ref, after_ref, gram_ref, *refs, first):
    del after_ref
    outs, (mark_ref, buffer, sems) = refs[:-3], refs[-3:]
    slots, tile, width = buffer.shape
    quarter = outs[0].shape[0] // 2
    steps = quarter // tile
    total = steps * len(outs)
    column = pl.multiple_of(place_ref[0] * width, width)
    sub = place_ref[3]

    def copy(i):
        part = first + i // steps
        start = (lax.rem(part // 2 + 1 + sub, 2) * 2 + lax.rem(part, 2)) * quarter + lax.rem(i, steps) * tile
        rows = pl.ds(pl.multiple_of(start, tile), tile)
        slot = lax.rem(i, slots)
        return pltpu.make_async_copy(gram_ref.at[rows, pl.ds(column, width)], buffer.at[slot], sems.at[slot])

    for i in range(min(slots - 1, total)):
        copy(i).start()

    for part, out_ref in enumerate(outs):

        @pl.loop(0, steps)
        def _(j):
            i = part * steps + j

            @pl.when(i + slots - 1 < total)
            def _():
                copy(i + slots - 1).start()

            copy(i).wait()
            high, low = split(buffer[lax.rem(i, slots)])
            start = pl.multiple_of(j * tile, tile)
            out_ref[pl.ds(start, tile)] = high
            out_ref[pl.ds(start + quarter, tile)] = low

    mark_ref[...] = jnp.zeros_like(mark_ref)


def gram_split(place, after, inverse_gram, first, count, tile=128, slots=8):
    rows, width = inverse_gram.shape
    half, quarter = width // 2, rows // 4
    tile = min(tile, quarter)
    *quarters, mark = pl.pallas_call(
        functools.partial(gram_split_kernel, first=first),
        in_specs=[pl.BlockSpec(memory_space=pltpu.SMEM), WHOLE, pl.BlockSpec(memory_space=pltpu.HBM)],
        out_specs=[WHOLE] * (count + 1),
        out_shape=[pltpu.VMEM((2 * quarter, half), jnp.bfloat16)] * count
        + [jax.ShapeDtypeStruct((8, 128), jnp.float32)],
        scratch_shapes=[pltpu.VMEM((slots, tile, half), jnp.float32), pltpu.SemaphoreType.DMA((slots,))],
        compiler_params=pltpu.CompilerParams(vmem_limit_bytes=12 * MIB),
        cost_estimate=pl.CostEstimate(flops=0, bytes_accessed=count * 4 * quarter * half, transcendentals=0),
        name="gram_split",
    )(place, after, inverse_gram)
    return [pltpu.with_memory_space_constraint(x, pltpu.VMEM) for x in quarters], mark


def gram_rows(group, gram_ref, terms, write):
    quarter = gram_ref.shape[0] // 2
    queries = terms.shape[1] // 2
    part = jnp.dot(gram_ref[...], terms[...], preferred_element_type=jnp.float32)
    part = part[:quarter] + part[quarter:]
    done = (part[:, :queries] + part[:, queries:]).T
    for g in range(2):
        write(g ^ group, done[g * (queries // 2) : (g + 1) * (queries // 2)])


def away_kernel(place_ref, *refs, row_count, own):
    grams, sources, (out_ref, terms, natural) = refs[:2], refs[2:-3], refs[-3:]
    group, row, col, sub = (place_ref[i] for i in range(4))
    height, queries, lanes = natural.shape
    for i, ref in enumerate(sources):
        s, z = i // row_count, i % row_count
        count = ref.shape[0] - PAD
        piece = restored(ref[:count], ref[count : count + 1])
        for k in range(4):
            g, c = k // 2, k % 2
            first = ((((g ^ group) * 2 + (c ^ col)) * 2 + (s ^ sub)) * row_count + (z ^ row)) * own
            for j in range(own):
                start = (k * own + j) * height
                natural[:, pl.ds(first + j, 1), :] = piece[start : start + height].reshape(height, 1, lanes)
    for a in range(height):
        block = natural[a]
        high = block.astype(jnp.bfloat16).astype(jnp.float32)
        both = jnp.concatenate([high, block - high], 0).T
        terms[a * lanes : (a + 1) * lanes] = both.astype(jnp.bfloat16)
    for i in range(2):

        def write(g, value):
            out_ref[i, g] = value

        gram_rows(group, grams[i], terms, write)


def home_kernel(place_ref, gram_ref, terms_ref, *refs):
    out_ref = refs[-1]

    def write(g, value):
        out_ref[g] = value

    gram_rows(place_ref[0], gram_ref, terms_ref, write)


def join_kernel(early_ref, early_got_ref, late_ref, late_got_ref, early_out, early_wire, late_out, late_wire):
    early = early_ref[...] + early_got_ref[...].astype(jnp.float32)
    early_out[...] = early
    early_wire[...] = early.astype(jnp.bfloat16)
    late_out[...] = late_ref[0] + late_got_ref[0]
    late_wire[...] = (late_ref[1] + late_got_ref[1]).astype(jnp.bfloat16)


def gram_product(place, quarters, sources, own, lanes):
    quarter, half = quarters[0].shape[0] // 2, quarters[0].shape[1]
    row_count = len(sources) // 2
    queries = 8 * row_count * own
    index = pl.BlockSpec(memory_space=pltpu.SMEM)

    def common(count):
        return dict(
            compiler_params=pltpu.CompilerParams(vmem_limit_bytes=8 * MIB),
            cost_estimate=pl.CostEstimate(
                flops=8 * count * queries * quarter * half, bytes_accessed=count * quarter * half, transcendentals=0
            ),
        )

    away, terms = pl.pallas_call(
        functools.partial(away_kernel, row_count=row_count, own=own),
        in_specs=[index] + [WHOLE] * (2 + len(sources)),
        out_specs=[WHOLE, WHOLE],
        out_shape=[
            jax.ShapeDtypeStruct((2, 2, queries // 2, quarter), jnp.float32),
            jax.ShapeDtypeStruct((half, 2 * queries), jnp.bfloat16),
        ],
        scratch_shapes=[pltpu.VMEM((half // lanes, queries, lanes), jnp.float32)],
        name="away",
        **common(2),
    )(place, *quarters[:2], *sources)
    got = swapped(away, "sub")

    def home(i, *after):
        return pl.pallas_call(
            home_kernel,
            in_specs=[index] + [WHOLE] * (2 + len(after)),
            out_specs=WHOLE,
            out_shape=jax.ShapeDtypeStruct((2, queries // 2, quarter), jnp.float32),
            name="home",
            **common(1),
        )(place, quarters[2 + i], terms, *after)

    early = home(0) + got[0]
    wire = early[1].astype(jnp.bfloat16)
    late = home(1, wire)
    shape = (queries // 2, quarter)
    early, early_wire, late, late_wire = pl.pallas_call(
        join_kernel,
        in_specs=[WHOLE] * 4,
        out_specs=[WHOLE] * 4,
        out_shape=[jax.ShapeDtypeStruct(shape, kind) for kind in (jnp.float32, jnp.bfloat16) * 2],
        compiler_params=pltpu.CompilerParams(vmem_limit_bytes=4 * MIB),
        name="join",
    )(early[0], swapped(wire, "groups"), late, got[1])
    late = late + swapped(late_wire, "groups").astype(jnp.float32)
    early = early + swapped(early_wire, "col").astype(jnp.float32)
    late = late + swapped(late.astype(jnp.bfloat16), "col").astype(jnp.float32)
    return jnp.concatenate([early, late], 1)


def others(pick, axis):
    size = lax.axis_size(axis)
    index = lax.axis_index(axis)
    return [lax.ppermute(pick(index ^ k), axis, [(i, i ^ k) for i in range(size)]) for k in range(1, size)]


def tree_sum(terms):
    while len(terms) > 1:
        terms = [terms[i] + terms[i + 1] for i in range(0, len(terms), 2)]
    return terms[0]


def swapped(array, axis):
    return others(lambda d: array, axis)[0]


def peers(pick):
    return [lax.ppermute(pick(k), ("groups", "col"), [(i, i ^ k) for i in range(4)]) for k in (1, 2, 3)]


def call(kernel, shapes, name, *args, specs=None, scratch=()):
    specs = specs or [pl.BlockSpec(memory_space=pltpu.SMEM) if a.dtype == jnp.int32 else WHOLE for a in args]
    many = isinstance(shapes, list)
    shapes = [jax.ShapeDtypeStruct(shape, jnp.float32) for shape in (shapes if many else [shapes])]
    outs = pl.pallas_call(
        kernel,
        in_specs=specs,
        out_specs=[WHOLE] * len(shapes),
        out_shape=shapes,
        scratch_shapes=list(scratch),
        compiler_params=pltpu.CompilerParams(vmem_limit_bytes=4 * MIB),
        name=name,
    )(*args)
    return outs if many else outs[0]


def body(query_acts, query_grads, proj_in, proj_out, inverse_gram, store_slab):
    row_count = lax.axis_size("row")
    place = jnp.stack([lax.axis_index(axis) for axis in ("groups", "row", "col", "sub")])
    queries, tokens = query_acts.shape[:2]
    own = queries // row_count
    in_width, out_width = proj_in.shape[1], proj_out.shape[1]
    got = []
    for targets in [(k,) for k in range(row_count - 1, row_count // 2 - 1, -1)] + [range(row_count // 2)[::-1]]:
        parts = project(targets, row_count, place, query_acts, query_grads, proj_in, proj_out)
        for k, part in zip(targets, parts):
            if k:
                got.append(lax.ppermute(part.astype(jnp.float16), "row", [(i, i ^ k) for i in range(row_count)]))
    first, mark = gram_split(place, parts[-1], inverse_gram, 0, 3)
    height = own * in_width // 8
    near = call(
        functools.partial(kron_kernel, tokens=tokens),
        [(2, height, out_width)] * 4,
        "kron",
        place,
        mark,
        parts[-1],
        *[x.astype(jnp.float32) for x in got],
        scratch=[pltpu.VMEM((own, in_width, out_width), jnp.float32)],
    )
    last, mark = gram_split(place, near[0], inverse_gram, 3, 1)
    near = [near[0]] + peers(lambda k: near[k])
    sources = []
    away = call(gather_kernel, (4, height, out_width), "gather", mark, *near)
    for kept in (near, [swapped(away, "sub")]):
        packed = call(pack_kernel, (4 * height + PAD, out_width), "pack", mark, *kept)
        wire = packed.astype(jnp.float16)
        sources += [packed] + [got.astype(jnp.float32) for got in others(lambda d: wire, "row")]
    total = gram_product(place, first + last, sources, own, out_width)
    high = lax.reduce_precision(total, 8, 7)
    terms = jnp.concatenate([high, total - high], 0).astype(jnp.bfloat16)
    scores = lax.dot_general(
        terms, store_slab, (((1,), (1,)), ((), ())), preferred_element_type=jnp.float32
    )
    scores = scores[: total.shape[0]] + scores[total.shape[0] :]
    scores = scores + swapped(scores, "sub")
    packed = call(pack_scores_kernel, (scores.shape[0] + PAD, scores.shape[1]), "pack_scores", scores)
    packed = lax.reduce_precision(packed, 5, 10)
    wire = packed.astype(jnp.float16)
    sources = [packed] + [got.astype(jnp.float32) for got in others(lambda d: wire, "row")]
    return call(sum_scores_kernel, scores.shape, "sum_scores", *sources)


def solution(mesh):
    shape = mesh.shape
    rows = shape["row"]
    paired = shape["groups"] == shape["col"] == shape["sub"] == 2 and rows & (rows - 1) == 0

    def chosen(query_acts, query_grads, proj_in, proj_out, *rest):
        queries = query_acts.shape[0] // (shape["groups"] * shape["col"] * shape["sub"])
        square = proj_in.shape[1] == proj_out.shape[1] == 128
        chosen_body = body if paired and square and queries % rows == 0 else plain_body
        return jax.shard_map(
            chosen_body,
            mesh=mesh,
            in_specs=(
                P(("groups", "col", "sub"), None, "row"),
                P(("groups", "col", "sub"), None, "row"),
                P("row", None),
                P("row", None),
                P("row", ("col", "sub")),
                P(("groups", "col"), ("row", "sub")),
            ),
            out_specs=P("groups", "col"),
            check_vma=False,
        )(query_acts, query_grads, proj_in, proj_out, *rest)

    return chosen
```

```python
import functools

import jax
import jax.numpy as jnp
from jax import lax
from jax.experimental import pallas as pl
from jax.experimental.pallas import tpu as pltpu
from jax.sharding import PartitionSpec as P

HIGHEST = lax.Precision.HIGHEST


def plain_body(query_acts, query_grads, proj_in, proj_out, inverse_gram, store_slab):
    row_count = lax.axis_size("row")
    row_index = lax.axis_index("row")
    sub_index = lax.axis_index("sub")
    in_width = proj_in.shape[1]
    act_part = jnp.einsum("qtd,dk->qtk", query_acts, proj_in, preferred_element_type=jnp.float32)
    grad_part = jnp.einsum("qtd,dk->qtk", query_grads, proj_out, preferred_element_type=jnp.float32)
    store_width = store_slab.shape[1]
    row_block = in_width // row_count
    act_whole, grad_proj = lax.psum((act_part, grad_part), "row")
    act_proj = lax.dynamic_slice_in_dim(act_whole, row_index * row_block, row_block, 2)
    kron_part = jnp.einsum("qta,qtb->qab", act_proj, grad_proj, precision=HIGHEST)
    kron_feats = lax.all_gather(kron_part, ("col", "sub"), axis=0, tiled=True)
    features_flat = kron_feats.reshape(kron_feats.shape[0], -1)
    precond_part = jnp.dot(features_flat, inverse_gram, precision=HIGHEST)
    precond_block = lax.psum(precond_part, "row").astype(jnp.bfloat16)
    precond_full = lax.all_gather(precond_block, ("col", "sub"), axis=1, tiled=True)
    store_start = (row_index * lax.axis_size("sub") + sub_index) * store_width
    precond_mine = lax.dynamic_slice_in_dim(precond_full, store_start, store_width, 1)
    score_part = lax.dot_general(
        precond_mine, store_slab, (((1,), (1,)), ((), ())), preferred_element_type=jnp.float32
    )
    return lax.psum(score_part, ("row", "sub"))


PAD = 8
SHIFT = 13.0
LOG2E = 1.4426950408889634
WHOLE = pl.BlockSpec(memory_space=pltpu.VMEM)
MIB = 2**20


def exponents(part):
    top = jnp.max(jnp.abs(part), axis=0, keepdims=True)
    return jnp.ceil(jnp.log(jnp.clip(top, 1e-30, 1e30)) * LOG2E)


def scaled(part, k):
    return part * jnp.exp2(SHIFT - k)


def restored(part, k):
    return part * jnp.exp2(k - SHIFT)


def project_kernel(place_ref, *refs, targets):
    inputs, outs, (inputs_buf, weights_buf, sems, weights_sems) = refs[:4], refs[4:-4], refs[-4:]
    own, tokens, width = inputs_buf.shape[2:]
    count = own * tokens
    row = place_ref[1]
    weights = [pltpu.make_async_copy(inputs[2 + i], weights_buf.at[i], weights_sems.at[i]) for i in range(2)]
    copies = {}
    for k in range(len(targets)):
        for i in range(2):
            if k == 0:
                weights[i].start()
            rows = pl.ds((row ^ targets[k]) * own, own)
            copies[k, i] = pltpu.make_async_copy(inputs[i].at[rows], inputs_buf.at[i, k], sems.at[i, k])
            copies[k, i].start()
    for k in range(len(targets)):
        for i in range(2):
            if k == 0:
                weights[i].wait()
            copies[k, i].wait()
            x = inputs_buf[i, k].reshape(count, width)
            part = jnp.dot(x, weights_buf[i], preferred_element_type=jnp.float32)
            e = exponents(part)
            outs[k][i * count : (i + 1) * count] = scaled(part, e)
            outs[k][2 * count + i * PAD : 2 * count + (i + 1) * PAD] = jnp.broadcast_to(e, (PAD, e.shape[1]))


def project(targets, row_count, place, query_acts, query_grads, proj_in, proj_out):
    queries, tokens, width = query_acts.shape
    own = queries // row_count
    out_width = proj_in.shape[1]
    height = 2 * own * tokens + 2 * PAD
    far = pl.BlockSpec(memory_space=pltpu.HBM)
    return pl.pallas_call(
        functools.partial(project_kernel, targets=targets),
        in_specs=[pl.BlockSpec(memory_space=pltpu.SMEM)] + [far] * 4,
        out_specs=[WHOLE] * len(targets),
        out_shape=[jax.ShapeDtypeStruct((height, out_width), jnp.float32)] * len(targets),
        scratch_shapes=[
            pltpu.VMEM((2, len(targets), own, tokens, width), query_acts.dtype),
            pltpu.VMEM((2,) + proj_in.shape, proj_in.dtype),
            pltpu.SemaphoreType.DMA((2, len(targets))),
            pltpu.SemaphoreType.DMA((2,)),
        ],
        compiler_params=pltpu.CompilerParams(vmem_limit_bytes=8 * MIB),
        name="project",
    )(place, *[pltpu.with_memory_space_constraint(x, pltpu.HBM) for x in (query_acts, query_grads, proj_in, proj_out)])


def kron_kernel(place_ref, after_ref, own_ref, *refs, tokens):
    del after_ref
    refs, outs, scratch = refs[:-5], refs[-5:-1], refs[-1]
    count = (own_ref.shape[0] - 2 * PAD) // 2
    sums = []
    for i in range(2):
        total = None
        for ref in (own_ref,) + refs:
            k = 2 * count + i * PAD
            part = restored(ref[i * count : (i + 1) * count], ref[k : k + 1])
            total = part if total is None else total + part
        sums.append(total)
    acts, grads = sums
    height = acts.shape[1] // 8
    group, col, sub = place_ref[0], place_ref[2], place_ref[3]
    for j in range(count // tokens):
        rows = slice(j * tokens, (j + 1) * tokens)
        scratch[j] = lax.dot_general(
            acts[rows], grads[rows], (((0,), (0,)), ((), ())), precision=HIGHEST, preferred_element_type=jnp.float32
        )
        for k in range(4):
            for s in range(2):
                start = (((col ^ (k % 2)) * 2 + (sub ^ s)) * 2 + (group ^ (k // 2))) * height
                outs[k][s, j * height : (j + 1) * height] = scratch[j, pl.ds(pl.multiple_of(start, height), height)]


def pack_kernel(*refs):
    kept, got_ref, out_ref = refs[:-2], refs[-2], refs[-1]
    lanes = got_ref.shape[-1]
    parts = jnp.concatenate([ref[0] for ref in kept] + [got_ref[...].reshape(-1, lanes)], 0)
    k = exponents(parts)
    out_ref[: parts.shape[0]] = scaled(parts, k)
    out_ref[parts.shape[0] :] = jnp.broadcast_to(k, (PAD, lanes))


def gather_kernel(after_ref, *refs):
    del after_ref
    for i, ref in enumerate(refs[:-1]):
        refs[-1][i] = ref[1]


def pack_scores_kernel(scores_ref, out_ref):
    scores = scores_ref[...]
    k = exponents(scores)
    out_ref[: scores.shape[0]] = scaled(scores, k)
    out_ref[scores.shape[0] :] = jnp.broadcast_to(k, (PAD, scores.shape[1]))


def sum_scores_kernel(*refs):
    out_ref = refs[-1]
    count = out_ref.shape[0]
    out_ref[...] = tree_sum([restored(ref[:count], ref[count : count + 1]) for ref in refs[:-1]])


def split(block):
    high = block.astype(jnp.bfloat16)
    return high, (block - high.astype(jnp.float32)).astype(jnp.bfloat16)


def gram_split_kernel(place_ref, after_ref, gram_ref, *refs, first):
    del after_ref
    outs, (mark_ref, buffer, sems) = refs[:-3], refs[-3:]
    slots, tile, width = buffer.shape
    quarter = outs[0].shape[0] // 2
    steps = quarter // tile
    total = steps * len(outs)
    column = pl.multiple_of(place_ref[0] * width, width)
    sub = place_ref[3]

    def copy(i):
        part = first + i // steps
        start = (lax.rem(part // 2 + 1 + sub, 2) * 2 + lax.rem(part, 2)) * quarter + lax.rem(i, steps) * tile
        rows = pl.ds(pl.multiple_of(start, tile), tile)
        slot = lax.rem(i, slots)
        return pltpu.make_async_copy(gram_ref.at[rows, pl.ds(column, width)], buffer.at[slot], sems.at[slot])

    for i in range(min(slots - 1, total)):
        copy(i).start()

    for part, out_ref in enumerate(outs):

        @pl.loop(0, steps)
        def _(j):
            i = part * steps + j

            @pl.when(i + slots - 1 < total)
            def _():
                copy(i + slots - 1).start()

            copy(i).wait()
            high, low = split(buffer[lax.rem(i, slots)])
            start = pl.multiple_of(j * tile, tile)
            out_ref[pl.ds(start, tile)] = high
            out_ref[pl.ds(start + quarter, tile)] = low

    mark_ref[...] = jnp.zeros_like(mark_ref)


def gram_split(place, after, inverse_gram, first, count, tile=128, slots=8):
    rows, width = inverse_gram.shape
    half, quarter = width // 2, rows // 4
    tile = min(tile, quarter)
    *quarters, mark = pl.pallas_call(
        functools.partial(gram_split_kernel, first=first),
        in_specs=[pl.BlockSpec(memory_space=pltpu.SMEM), WHOLE, pl.BlockSpec(memory_space=pltpu.HBM)],
        out_specs=[WHOLE] * (count + 1),
        out_shape=[pltpu.VMEM((2 * quarter, half), jnp.bfloat16)] * count
        + [jax.ShapeDtypeStruct((8, 128), jnp.float32)],
        scratch_shapes=[pltpu.VMEM((slots, tile, half), jnp.float32), pltpu.SemaphoreType.DMA((slots,))],
        compiler_params=pltpu.CompilerParams(vmem_limit_bytes=12 * MIB),
        cost_estimate=pl.CostEstimate(flops=0, bytes_accessed=count * 4 * quarter * half, transcendentals=0),
        name="gram_split",
    )(place, after, inverse_gram)
    return [pltpu.with_memory_space_constraint(x, pltpu.VMEM) for x in quarters], mark


def gram_rows(group, gram_ref, terms, write):
    quarter = gram_ref.shape[0] // 2
    queries = terms.shape[1] // 2
    part = jnp.dot(gram_ref[...], terms[...], preferred_element_type=jnp.float32)
    part = part[:quarter] + part[quarter:]
    done = (part[:, :queries] + part[:, queries:]).T
    for g in range(2):
        write(g ^ group, done[g * (queries // 2) : (g + 1) * (queries // 2)])


def away_kernel(place_ref, after_ref, *refs, row_count, own):
    del after_ref
    grams, sources, (out_ref, terms, natural) = refs[:2], refs[2 : 2 + row_count], refs[2 + row_count :]
    group, row, col, sub = (place_ref[i] for i in range(4))
    height, queries, lanes = natural.shape
    for z in range(row_count):
        count = sources[z].shape[0] - PAD
        piece = restored(sources[z][:count], sources[z][count : count + 1])
        for place in range(8):
            s, g, c = place // 4, place // 2 % 2, place % 2
            first = ((((g ^ group) * 2 + (c ^ col)) * 2 + (s ^ sub)) * row_count + (z ^ row)) * own
            for j in range(own):
                start = (place * own + j) * height
                natural[:, pl.ds(first + j, 1), :] = piece[start : start + height].reshape(height, 1, lanes)
    for a in range(height):
        block = natural[a]
        high = block.astype(jnp.bfloat16).astype(jnp.float32)
        both = jnp.concatenate([high, block - high], 0).T
        terms[a * lanes : (a + 1) * lanes] = both.astype(jnp.bfloat16)
    for i in range(2):

        def write(g, value):
            out_ref[i, g] = value

        gram_rows(group, grams[i], terms, write)


def home_kernel(place_ref, gram_ref, terms_ref, *refs):
    out_ref = refs[-1]

    def write(g, value):
        out_ref[g] = value

    gram_rows(place_ref[0], gram_ref, terms_ref, write)


def join_kernel(early_ref, early_got_ref, late_ref, late_got_ref, early_out, early_wire, late_out, late_wire):
    early = early_ref[...] + early_got_ref[...].astype(jnp.float32)
    early_out[...] = early
    early_wire[...] = early.astype(jnp.bfloat16)
    late_out[...] = late_ref[0] + late_got_ref[0]
    late_wire[...] = (late_ref[1] + late_got_ref[1]).astype(jnp.bfloat16)


def gram_product(place, after, quarters, sources, own, lanes):
    quarter, half = quarters[0].shape[0] // 2, quarters[0].shape[1]
    row_count = len(sources)
    queries = 8 * row_count * own
    index = pl.BlockSpec(memory_space=pltpu.SMEM)

    def common(count):
        return dict(
            compiler_params=pltpu.CompilerParams(vmem_limit_bytes=8 * MIB),
            cost_estimate=pl.CostEstimate(
                flops=8 * count * queries * quarter * half, bytes_accessed=count * quarter * half, transcendentals=0
            ),
        )

    away, terms = pl.pallas_call(
        functools.partial(away_kernel, row_count=row_count, own=own),
        in_specs=[index] + [WHOLE] * (3 + row_count),
        out_specs=[WHOLE, WHOLE],
        out_shape=[
            jax.ShapeDtypeStruct((2, 2, queries // 2, quarter), jnp.float32),
            jax.ShapeDtypeStruct((half, 2 * queries), jnp.bfloat16),
        ],
        scratch_shapes=[pltpu.VMEM((half // lanes, queries, lanes), jnp.float32)],
        name="away",
        **common(2),
    )(place, after, *quarters[:2], *sources)
    got = swapped(away, "sub")

    def home(i, *after):
        return pl.pallas_call(
            home_kernel,
            in_specs=[index] + [WHOLE] * (2 + len(after)),
            out_specs=WHOLE,
            out_shape=jax.ShapeDtypeStruct((2, queries // 2, quarter), jnp.float32),
            name="home",
            **common(1),
        )(place, quarters[2 + i], terms, *after)

    early = home(0) + got[0]
    wire = early[1].astype(jnp.bfloat16)
    late = home(1, wire)
    shape = (queries // 2, quarter)
    early, early_wire, late, late_wire = pl.pallas_call(
        join_kernel,
        in_specs=[WHOLE] * 4,
        out_specs=[WHOLE] * 4,
        out_shape=[jax.ShapeDtypeStruct(shape, kind) for kind in (jnp.float32, jnp.bfloat16) * 2],
        compiler_params=pltpu.CompilerParams(vmem_limit_bytes=4 * MIB),
        name="join",
    )(early[0], swapped(wire, "groups"), late, got[1])
    late = late + swapped(late_wire, "groups").astype(jnp.float32)
    early = early + swapped(early_wire, "col").astype(jnp.float32)
    late = late + swapped(late.astype(jnp.bfloat16), "col").astype(jnp.float32)
    return jnp.concatenate([early, late], 1)


def others(pick, axis):
    size = lax.axis_size(axis)
    index = lax.axis_index(axis)
    return [lax.ppermute(pick(index ^ k), axis, [(i, i ^ k) for i in range(size)]) for k in range(1, size)]


def tree_sum(terms):
    while len(terms) > 1:
        terms = [terms[i] + terms[i + 1] for i in range(0, len(terms), 2)]
    return terms[0]


def swapped(array, axis):
    return others(lambda d: array, axis)[0]


def peers(pick):
    return [lax.ppermute(pick(k), ("groups", "col"), [(i, i ^ k) for i in range(4)]) for k in (1, 2, 3)]


def call(kernel, shapes, name, *args, specs=None, scratch=()):
    specs = specs or [pl.BlockSpec(memory_space=pltpu.SMEM) if a.dtype == jnp.int32 else WHOLE for a in args]
    many = isinstance(shapes, list)
    shapes = [jax.ShapeDtypeStruct(shape, jnp.float32) for shape in (shapes if many else [shapes])]
    outs = pl.pallas_call(
        kernel,
        in_specs=specs,
        out_specs=[WHOLE] * len(shapes),
        out_shape=shapes,
        scratch_shapes=list(scratch),
        compiler_params=pltpu.CompilerParams(vmem_limit_bytes=4 * MIB),
        name=name,
    )(*args)
    return outs if many else outs[0]


def body(query_acts, query_grads, proj_in, proj_out, inverse_gram, store_slab):
    row_count = lax.axis_size("row")
    place = jnp.stack([lax.axis_index(axis) for axis in ("groups", "row", "col", "sub")])
    queries, tokens = query_acts.shape[:2]
    own = queries // row_count
    in_width, out_width = proj_in.shape[1], proj_out.shape[1]
    got = []
    for targets in (range(row_count)[: row_count // 2 - 1 : -1], range(row_count)[: row_count // 2][::-1]):
        parts = project(targets, row_count, place, query_acts, query_grads, proj_in, proj_out)
        for k, part in zip(targets, parts):
            if k:
                got.append(lax.ppermute(part.astype(jnp.float16), "row", [(i, i ^ k) for i in range(row_count)]))
    quarters, mark = gram_split(place, parts[-1], inverse_gram, 0, 2)
    height = own * in_width // 8
    near = call(
        functools.partial(kron_kernel, tokens=tokens),
        [(2, height, out_width)] * 4,
        "kron",
        place,
        mark,
        parts[-1],
        *[x.astype(jnp.float32) for x in got],
        scratch=[pltpu.VMEM((own, in_width, out_width), jnp.float32)],
    )
    third, mark = gram_split(place, near[0], inverse_gram, 2, 1)
    near = [near[0]] + peers(lambda k: near[k])
    got = swapped(call(gather_kernel, (4, height, out_width), "gather", mark, *near), "sub")
    packed = call(pack_kernel, (8 * height + PAD, out_width), "pack", *near, got)
    wire = packed.astype(jnp.float16)
    sources = [packed] + [got.astype(jnp.float32) for got in others(lambda d: wire, "row")]
    fourth, mark = gram_split(place, packed, inverse_gram, 3, 1)
    total = gram_product(place, mark, quarters + third + fourth, sources, own, out_width)
    high = lax.reduce_precision(total, 8, 7)
    terms = jnp.concatenate([high, total - high], 0).astype(jnp.bfloat16)
    scores = lax.dot_general(
        terms, store_slab, (((1,), (1,)), ((), ())), preferred_element_type=jnp.float32
    )
    scores = scores[: total.shape[0]] + scores[total.shape[0] :]
    scores = scores + swapped(scores, "sub")
    packed = call(pack_scores_kernel, (scores.shape[0] + PAD, scores.shape[1]), "pack_scores", scores)
    packed = lax.reduce_precision(packed, 5, 10)
    wire = packed.astype(jnp.float16)
    sources = [packed] + [got.astype(jnp.float32) for got in others(lambda d: wire, "row")]
    return call(sum_scores_kernel, scores.shape, "sum_scores", *sources)


def solution(mesh):
    shape = mesh.shape
    rows = shape["row"]
    paired = shape["groups"] == shape["col"] == shape["sub"] == 2 and rows & (rows - 1) == 0

    def chosen(query_acts, query_grads, proj_in, proj_out, *rest):
        queries = query_acts.shape[0] // (shape["groups"] * shape["col"] * shape["sub"])
        square = proj_in.shape[1] == proj_out.shape[1] == 128
        chosen_body = body if paired and square and queries % rows == 0 else plain_body
        return jax.shard_map(
            chosen_body,
            mesh=mesh,
            in_specs=(
                P(("groups", "col", "sub"), None, "row"),
                P(("groups", "col", "sub"), None, "row"),
                P("row", None),
                P("row", None),
                P("row", ("col", "sub")),
                P(("groups", "col"), ("row", "sub")),
            ),
            out_specs=P("groups", "col"),
            check_vma=False,
        )(query_acts, query_grads, proj_in, proj_out, *rest)

    return chosen
```

```python
import functools

import jax
import jax.numpy as jnp
from jax import lax
from jax.experimental import pallas as pl
from jax.experimental.pallas import tpu as pltpu
from jax.sharding import PartitionSpec as P

HIGHEST = lax.Precision.HIGHEST


def plain_body(query_acts, query_grads, proj_in, proj_out, inverse_gram, store_slab):
    row_count = lax.axis_size("row")
    row_index = lax.axis_index("row")
    sub_index = lax.axis_index("sub")
    in_width = proj_in.shape[1]
    act_part = jnp.einsum("qtd,dk->qtk", query_acts, proj_in, preferred_element_type=jnp.float32)
    grad_part = jnp.einsum("qtd,dk->qtk", query_grads, proj_out, preferred_element_type=jnp.float32)
    store_width = store_slab.shape[1]
    row_block = in_width // row_count
    act_whole, grad_proj = lax.psum((act_part, grad_part), "row")
    act_proj = lax.dynamic_slice_in_dim(act_whole, row_index * row_block, row_block, 2)
    kron_part = jnp.einsum("qta,qtb->qab", act_proj, grad_proj, precision=HIGHEST)
    kron_feats = lax.all_gather(kron_part, ("col", "sub"), axis=0, tiled=True)
    features_flat = kron_feats.reshape(kron_feats.shape[0], -1)
    precond_part = jnp.dot(features_flat, inverse_gram, precision=HIGHEST)
    precond_block = lax.psum(precond_part, "row").astype(jnp.bfloat16)
    precond_full = lax.all_gather(precond_block, ("col", "sub"), axis=1, tiled=True)
    store_start = (row_index * lax.axis_size("sub") + sub_index) * store_width
    precond_mine = lax.dynamic_slice_in_dim(precond_full, store_start, store_width, 1)
    score_part = lax.dot_general(
        precond_mine, store_slab, (((1,), (1,)), ((), ())), preferred_element_type=jnp.float32
    )
    return lax.psum(score_part, ("row", "sub"))


PAD = 8
SHIFT = 13.0
LOG2E = 1.4426950408889634
WHOLE = pl.BlockSpec(memory_space=pltpu.VMEM)
MIB = 2**20


def exponents(part):
    top = jnp.max(jnp.abs(part), axis=0, keepdims=True)
    return jnp.ceil(jnp.log(jnp.clip(top, 1e-30, 1e30)) * LOG2E)


def scaled(part, k):
    return part * jnp.exp2(SHIFT - k)


def restored(part, k):
    return part * jnp.exp2(k - SHIFT)


def project_kernel(place_ref, *refs, targets):
    inputs, outs, (inputs_buf, weights_buf, sems, weights_sems) = refs[:4], refs[4:-4], refs[-4:]
    own, tokens, width = inputs_buf.shape[2:]
    count = own * tokens
    row = place_ref[1]
    weights = [pltpu.make_async_copy(inputs[2 + i], weights_buf.at[i], weights_sems.at[i]) for i in range(2)]
    copies = {}
    for k in range(len(targets)):
        for i in range(2):
            if k == 0:
                weights[i].start()
            rows = pl.ds((row ^ targets[k]) * own, own)
            copies[k, i] = pltpu.make_async_copy(inputs[i].at[rows], inputs_buf.at[i, k], sems.at[i, k])
            copies[k, i].start()
    for k in range(len(targets)):
        for i in range(2):
            if k == 0:
                weights[i].wait()
            copies[k, i].wait()
            x = inputs_buf[i, k].reshape(count, width)
            part = jnp.dot(x, weights_buf[i], preferred_element_type=jnp.float32)
            e = exponents(part)
            outs[k][i * count : (i + 1) * count] = scaled(part, e)
            outs[k][2 * count + i * PAD : 2 * count + (i + 1) * PAD] = jnp.broadcast_to(e, (PAD, e.shape[1]))


def project(targets, row_count, place, query_acts, query_grads, proj_in, proj_out):
    queries, tokens, width = query_acts.shape
    own = queries // row_count
    out_width = proj_in.shape[1]
    height = 2 * own * tokens + 2 * PAD
    far = pl.BlockSpec(memory_space=pltpu.HBM)
    return pl.pallas_call(
        functools.partial(project_kernel, targets=targets),
        in_specs=[pl.BlockSpec(memory_space=pltpu.SMEM)] + [far] * 4,
        out_specs=[WHOLE] * len(targets),
        out_shape=[jax.ShapeDtypeStruct((height, out_width), jnp.float32)] * len(targets),
        scratch_shapes=[
            pltpu.VMEM((2, len(targets), own, tokens, width), query_acts.dtype),
            pltpu.VMEM((2,) + proj_in.shape, proj_in.dtype),
            pltpu.SemaphoreType.DMA((2, len(targets))),
            pltpu.SemaphoreType.DMA((2,)),
        ],
        compiler_params=pltpu.CompilerParams(vmem_limit_bytes=8 * MIB),
        name="project",
    )(place, *[pltpu.with_memory_space_constraint(x, pltpu.HBM) for x in (query_acts, query_grads, proj_in, proj_out)])


def kron_kernel(place_ref, after_ref, own_ref, *refs, tokens):
    del after_ref
    refs, outs, scratch = refs[:-5], refs[-5:-1], refs[-1]
    count = (own_ref.shape[0] - 2 * PAD) // 2
    sums = []
    for i in range(2):
        total = None
        for ref in (own_ref,) + refs:
            k = 2 * count + i * PAD
            part = restored(ref[i * count : (i + 1) * count], ref[k : k + 1])
            total = part if total is None else total + part
        sums.append(total)
    acts, grads = sums
    height = acts.shape[1] // 8
    group, col, sub = place_ref[0], place_ref[2], place_ref[3]
    for j in range(count // tokens):
        rows = slice(j * tokens, (j + 1) * tokens)
        scratch[j] = lax.dot_general(
            acts[rows], grads[rows], (((0,), (0,)), ((), ())), precision=HIGHEST, preferred_element_type=jnp.float32
        )
        for k in range(4):
            for s in range(2):
                start = (((col ^ (k % 2)) * 2 + (sub ^ s)) * 2 + (group ^ (k // 2))) * height
                outs[k][s, j * height : (j + 1) * height] = scratch[j, pl.ds(pl.multiple_of(start, height), height)]


def pack_kernel(*refs):
    kept, got_ref, out_ref = refs[:-2], refs[-2], refs[-1]
    lanes = got_ref.shape[-1]
    parts = jnp.concatenate([ref[0] for ref in kept] + [got_ref[...].reshape(-1, lanes)], 0)
    k = exponents(parts)
    out_ref[: parts.shape[0]] = scaled(parts, k)
    out_ref[parts.shape[0] :] = jnp.broadcast_to(k, (PAD, lanes))


def gather_kernel(after_ref, *refs):
    del after_ref
    for i, ref in enumerate(refs[:-1]):
        refs[-1][i] = ref[1]


def pack_scores_kernel(scores_ref, out_ref):
    scores = scores_ref[...]
    k = exponents(scores)
    out_ref[: scores.shape[0]] = scaled(scores, k)
    out_ref[scores.shape[0] :] = jnp.broadcast_to(k, (PAD, scores.shape[1]))


def sum_scores_kernel(*refs):
    out_ref = refs[-1]
    count = out_ref.shape[0]
    out_ref[...] = tree_sum([restored(ref[:count], ref[count : count + 1]) for ref in refs[:-1]])


SMALL = jnp.float8_e5m2
SMALL_SCALE = 2.0**20


def split(block):
    high = block.astype(jnp.bfloat16)
    return high, ((block - high.astype(jnp.float32)) * SMALL_SCALE).astype(SMALL)


def gram_split_kernel(place_ref, after_ref, gram_ref, *refs, first):
    del after_ref
    outs, (mark_ref, buffer, sems) = refs[:-3], refs[-3:]
    slots, tile, width = buffer.shape
    quarter = outs[0].shape[0]
    steps = quarter // tile
    total = steps * (len(outs) // 2)
    column = pl.multiple_of(place_ref[0] * width, width)
    sub = place_ref[3]

    def copy(i):
        part = first + i // steps
        start = (lax.rem(part // 2 + 1 + sub, 2) * 2 + lax.rem(part, 2)) * quarter + lax.rem(i, steps) * tile
        rows = pl.ds(pl.multiple_of(start, tile), tile)
        slot = lax.rem(i, slots)
        return pltpu.make_async_copy(gram_ref.at[rows, pl.ds(column, width)], buffer.at[slot], sems.at[slot])

    for i in range(min(slots - 1, total)):
        copy(i).start()

    for part in range(len(outs) // 2):

        @pl.loop(0, steps)
        def _(j):
            i = part * steps + j

            @pl.when(i + slots - 1 < total)
            def _():
                copy(i + slots - 1).start()

            copy(i).wait()
            high, low = split(buffer[lax.rem(i, slots)])
            start = pl.multiple_of(j * tile, tile)
            outs[2 * part][pl.ds(start, tile)] = high
            outs[2 * part + 1][pl.ds(start, tile)] = low

    mark_ref[...] = jnp.zeros_like(mark_ref)


def gram_split(place, after, inverse_gram, first, count, tile=128, slots=8):
    rows, width = inverse_gram.shape
    half, quarter = width // 2, rows // 4
    tile = min(tile, quarter)
    *quarters, mark = pl.pallas_call(
        functools.partial(gram_split_kernel, first=first),
        in_specs=[pl.BlockSpec(memory_space=pltpu.SMEM), WHOLE, pl.BlockSpec(memory_space=pltpu.HBM)],
        out_specs=[WHOLE] * (2 * count + 1),
        out_shape=[pltpu.VMEM((quarter, half), kind) for kind in (jnp.bfloat16, SMALL)] * count
        + [jax.ShapeDtypeStruct((8, 128), jnp.float32)],
        scratch_shapes=[pltpu.VMEM((slots, tile, half), jnp.float32), pltpu.SemaphoreType.DMA((slots,))],
        compiler_params=pltpu.CompilerParams(vmem_limit_bytes=12 * MIB),
        cost_estimate=pl.CostEstimate(flops=0, bytes_accessed=count * 4 * quarter * half, transcendentals=0),
        name="gram_split",
    )(place, after, inverse_gram)
    return [pltpu.with_memory_space_constraint(x, pltpu.VMEM) for x in quarters], mark


def gram_rows(group, high_ref, low_ref, terms, small_terms, unit, write):
    queries = small_terms.shape[1]
    part = jnp.dot(high_ref[...], terms[...], preferred_element_type=jnp.float32)
    low = jnp.dot(low_ref[...], small_terms[...], preferred_element_type=jnp.float32)
    done = (part[:, :queries] + part[:, queries:] + low * unit[:1]).T
    for g in range(2):
        write(g ^ group, done[g * (queries // 2) : (g + 1) * (queries // 2)])


def away_kernel(place_ref, after_ref, *refs, row_count, own):
    del after_ref
    grams, sources = refs[:4], refs[4 : 4 + row_count]
    out_ref, terms, small_terms, unit, natural = refs[4 + row_count :]
    group, row, col, sub = (place_ref[i] for i in range(4))
    height, queries, lanes = natural.shape
    for z in range(row_count):
        count = sources[z].shape[0] - PAD
        piece = restored(sources[z][:count], sources[z][count : count + 1])
        for place in range(8):
            s, g, c = place // 4, place // 2 % 2, place % 2
            first = ((((g ^ group) * 2 + (c ^ col)) * 2 + (s ^ sub)) * row_count + (z ^ row)) * own
            for j in range(own):
                start = (place * own + j) * height
                natural[:, pl.ds(first + j, 1), :] = piece[start : start + height].reshape(height, 1, lanes)
    top = jnp.max(jnp.max(jnp.abs(natural[...]), axis=0), axis=1, keepdims=True)
    k = jnp.ceil(jnp.log(jnp.clip(top, 1e-30, 1e30)) * LOG2E)
    k = jnp.broadcast_to(k, (queries, lanes)).T[: unit.shape[0]]
    unit[...] = jnp.exp2(k - 7.0) * (1.0 / SMALL_SCALE)
    factor = jnp.exp2(7.0 - k[:1])
    for a in range(height):
        block = natural[a]
        high = block.astype(jnp.bfloat16).astype(jnp.float32)
        both = jnp.concatenate([high, block - high], 0).T
        terms[a * lanes : (a + 1) * lanes] = both.astype(jnp.bfloat16)
        small_terms[a * lanes : (a + 1) * lanes] = (both[:, :queries] * factor).astype(SMALL)
    for i in range(2):

        def write(g, value):
            out_ref[i, g] = value

        gram_rows(group, *grams[2 * i : 2 * i + 2], terms, small_terms, unit, write)


def home_kernel(place_ref, high_ref, low_ref, terms_ref, small_ref, unit_ref, *refs):
    out_ref = refs[-1]

    def write(g, value):
        out_ref[g] = value

    gram_rows(place_ref[0], high_ref, low_ref, terms_ref, small_ref, unit_ref, write)


def join_kernel(early_ref, early_got_ref, late_ref, late_got_ref, early_out, early_wire, late_out, late_wire):
    early = early_ref[...] + early_got_ref[...].astype(jnp.float32)
    early_out[...] = early
    early_wire[...] = early.astype(jnp.bfloat16)
    late_out[...] = late_ref[0] + late_got_ref[0]
    late_wire[...] = (late_ref[1] + late_got_ref[1]).astype(jnp.bfloat16)


def gram_product(place, after, quarters, sources, own, lanes):
    quarter, half = quarters[0].shape
    row_count = len(sources)
    queries = 8 * row_count * own
    index = pl.BlockSpec(memory_space=pltpu.SMEM)

    def common(count):
        return dict(
            compiler_params=pltpu.CompilerParams(vmem_limit_bytes=8 * MIB),
            cost_estimate=pl.CostEstimate(
                flops=8 * count * queries * quarter * half, bytes_accessed=count * quarter * half, transcendentals=0
            ),
        )

    away, *terms = pl.pallas_call(
        functools.partial(away_kernel, row_count=row_count, own=own),
        in_specs=[index] + [WHOLE] * (5 + row_count),
        out_specs=[WHOLE] * 4,
        out_shape=[
            jax.ShapeDtypeStruct((2, 2, queries // 2, quarter), jnp.float32),
            jax.ShapeDtypeStruct((half, 2 * queries), jnp.bfloat16),
            jax.ShapeDtypeStruct((half, queries), SMALL),
            jax.ShapeDtypeStruct((PAD, queries), jnp.float32),
        ],
        scratch_shapes=[pltpu.VMEM((half // lanes, queries, lanes), jnp.float32)],
        name="away",
        **common(2),
    )(place, after, *quarters[:4], *sources)
    got = swapped(away, "sub")

    def home(i, *after):
        return pl.pallas_call(
            home_kernel,
            in_specs=[index] + [WHOLE] * (5 + len(after)),
            out_specs=WHOLE,
            out_shape=jax.ShapeDtypeStruct((2, queries // 2, quarter), jnp.float32),
            name="home",
            **common(1),
        )(place, *quarters[4 + 2 * i : 6 + 2 * i], *terms, *after)

    early = home(0) + got[0]
    wire = early[1].astype(jnp.bfloat16)
    late = home(1, wire)
    shape = (queries // 2, quarter)
    early, early_wire, late, late_wire = pl.pallas_call(
        join_kernel,
        in_specs=[WHOLE] * 4,
        out_specs=[WHOLE] * 4,
        out_shape=[jax.ShapeDtypeStruct(shape, kind) for kind in (jnp.float32, jnp.bfloat16) * 2],
        compiler_params=pltpu.CompilerParams(vmem_limit_bytes=4 * MIB),
        name="join",
    )(early[0], swapped(wire, "groups"), late, got[1])
    late = late + swapped(late_wire, "groups").astype(jnp.float32)
    early = early + swapped(early_wire, "col").astype(jnp.float32)
    late = late + swapped(late.astype(jnp.bfloat16), "col").astype(jnp.float32)
    return jnp.concatenate([early, late], 1)


def others(pick, axis):
    size = lax.axis_size(axis)
    index = lax.axis_index(axis)
    return [lax.ppermute(pick(index ^ k), axis, [(i, i ^ k) for i in range(size)]) for k in range(1, size)]


def tree_sum(terms):
    while len(terms) > 1:
        terms = [terms[i] + terms[i + 1] for i in range(0, len(terms), 2)]
    return terms[0]


def swapped(array, axis):
    return others(lambda d: array, axis)[0]


def peers(pick):
    return [lax.ppermute(pick(k), ("groups", "col"), [(i, i ^ k) for i in range(4)]) for k in (1, 2, 3)]


def call(kernel, shapes, name, *args, specs=None, scratch=()):
    specs = specs or [pl.BlockSpec(memory_space=pltpu.SMEM) if a.dtype == jnp.int32 else WHOLE for a in args]
    many = isinstance(shapes, list)
    shapes = [jax.ShapeDtypeStruct(shape, jnp.float32) for shape in (shapes if many else [shapes])]
    outs = pl.pallas_call(
        kernel,
        in_specs=specs,
        out_specs=[WHOLE] * len(shapes),
        out_shape=shapes,
        scratch_shapes=list(scratch),
        compiler_params=pltpu.CompilerParams(vmem_limit_bytes=4 * MIB),
        name=name,
    )(*args)
    return outs if many else outs[0]


def body(query_acts, query_grads, proj_in, proj_out, inverse_gram, store_slab):
    row_count = lax.axis_size("row")
    place = jnp.stack([lax.axis_index(axis) for axis in ("groups", "row", "col", "sub")])
    queries, tokens = query_acts.shape[:2]
    own = queries // row_count
    in_width, out_width = proj_in.shape[1], proj_out.shape[1]
    got = []
    for targets in (range(row_count)[: row_count // 2 - 1 : -1], range(row_count)[: row_count // 2][::-1]):
        parts = project(targets, row_count, place, query_acts, query_grads, proj_in, proj_out)
        for k, part in zip(targets, parts):
            if k:
                got.append(lax.ppermute(part.astype(jnp.float16), "row", [(i, i ^ k) for i in range(row_count)]))
    quarters, mark = gram_split(place, parts[-1], inverse_gram, 0, 2)
    height = own * in_width // 8
    near = call(
        functools.partial(kron_kernel, tokens=tokens),
        [(2, height, out_width)] * 4,
        "kron",
        place,
        mark,
        parts[-1],
        *[x.astype(jnp.float32) for x in got],
        scratch=[pltpu.VMEM((own, in_width, out_width), jnp.float32)],
    )
    third, mark = gram_split(place, near[0], inverse_gram, 2, 1)
    near = [near[0]] + peers(lambda k: near[k])
    got = swapped(call(gather_kernel, (4, height, out_width), "gather", mark, *near), "sub")
    packed = call(pack_kernel, (8 * height + PAD, out_width), "pack", *near, got)
    wire = packed.astype(jnp.float16)
    sources = [packed] + [got.astype(jnp.float32) for got in others(lambda d: wire, "row")]
    fourth, mark = gram_split(place, packed, inverse_gram, 3, 1)
    total = gram_product(place, mark, quarters + third + fourth, sources, own, out_width)
    high = lax.reduce_precision(total, 8, 7)
    terms = jnp.concatenate([high, total - high], 0).astype(jnp.bfloat16)
    scores = lax.dot_general(
        terms, store_slab, (((1,), (1,)), ((), ())), preferred_element_type=jnp.float32
    )
    scores = scores[: total.shape[0]] + scores[total.shape[0] :]
    scores = scores + swapped(scores, "sub")
    packed = call(pack_scores_kernel, (scores.shape[0] + PAD, scores.shape[1]), "pack_scores", scores)
    packed = lax.reduce_precision(packed, 5, 10)
    wire = packed.astype(jnp.float16)
    sources = [packed] + [got.astype(jnp.float32) for got in others(lambda d: wire, "row")]
    return call(sum_scores_kernel, scores.shape, "sum_scores", *sources)


def solution(mesh):
    shape = mesh.shape
    rows = shape["row"]
    paired = shape["groups"] == shape["col"] == shape["sub"] == 2 and rows & (rows - 1) == 0

    def chosen(query_acts, query_grads, proj_in, proj_out, *rest):
        queries = query_acts.shape[0] // (shape["groups"] * shape["col"] * shape["sub"])
        square = proj_in.shape[1] == proj_out.shape[1] == 128
        chosen_body = body if paired and square and queries % rows == 0 else plain_body
        return jax.shard_map(
            chosen_body,
            mesh=mesh,
            in_specs=(
                P(("groups", "col", "sub"), None, "row"),
                P(("groups", "col", "sub"), None, "row"),
                P("row", None),
                P("row", None),
                P("row", ("col", "sub")),
                P(("groups", "col"), ("row", "sub")),
            ),
            out_specs=P("groups", "col"),
            check_vma=False,
        )(query_acts, query_grads, proj_in, proj_out, *rest)

    return chosen
```

```python
import functools

import jax
import jax.numpy as jnp
from jax import lax
from jax.experimental import pallas as pl
from jax.experimental.pallas import tpu as pltpu
from jax.sharding import PartitionSpec as P

HIGHEST = lax.Precision.HIGHEST


def plain_body(query_acts, query_grads, proj_in, proj_out, inverse_gram, store_slab):
    row_count = lax.axis_size("row")
    row_index = lax.axis_index("row")
    sub_index = lax.axis_index("sub")
    in_width = proj_in.shape[1]
    act_part = jnp.einsum("qtd,dk->qtk", query_acts, proj_in, preferred_element_type=jnp.float32)
    grad_part = jnp.einsum("qtd,dk->qtk", query_grads, proj_out, preferred_element_type=jnp.float32)
    store_width = store_slab.shape[1]
    row_block = in_width // row_count
    act_whole, grad_proj = lax.psum((act_part, grad_part), "row")
    act_proj = lax.dynamic_slice_in_dim(act_whole, row_index * row_block, row_block, 2)
    kron_part = jnp.einsum("qta,qtb->qab", act_proj, grad_proj, precision=HIGHEST)
    kron_feats = lax.all_gather(kron_part, ("col", "sub"), axis=0, tiled=True)
    features_flat = kron_feats.reshape(kron_feats.shape[0], -1)
    precond_part = jnp.dot(features_flat, inverse_gram, precision=HIGHEST)
    precond_block = lax.psum(precond_part, "row").astype(jnp.bfloat16)
    precond_full = lax.all_gather(precond_block, ("col", "sub"), axis=1, tiled=True)
    store_start = (row_index * lax.axis_size("sub") + sub_index) * store_width
    precond_mine = lax.dynamic_slice_in_dim(precond_full, store_start, store_width, 1)
    score_part = lax.dot_general(
        precond_mine, store_slab, (((1,), (1,)), ((), ())), preferred_element_type=jnp.float32
    )
    return lax.psum(score_part, ("row", "sub"))


PAD = 8
SHIFT = 13.0
LOG2E = 1.4426950408889634
WHOLE = pl.BlockSpec(memory_space=pltpu.VMEM)
MIB = 2**20


def exponents(part):
    top = jnp.max(jnp.abs(part), axis=0, keepdims=True)
    return jnp.ceil(jnp.log(jnp.clip(top, 1e-30, 1e30)) * LOG2E)


def scaled(part, k):
    return part * jnp.exp2(SHIFT - k)


def restored(part, k):
    return part * jnp.exp2(k - SHIFT)


def project_kernel(place_ref, *refs, targets):
    inputs, outs, (inputs_buf, weights_buf, sems, weights_sems) = refs[:4], refs[4:-4], refs[-4:]
    own, tokens, width = inputs_buf.shape[2:]
    count = own * tokens
    row = place_ref[1]
    weights = [pltpu.make_async_copy(inputs[2 + i], weights_buf.at[i], weights_sems.at[i]) for i in range(2)]
    copies = {}
    for k in range(len(targets)):
        for i in range(2):
            if k == 0:
                weights[i].start()
            rows = pl.ds((row ^ targets[k]) * own, own)
            copies[k, i] = pltpu.make_async_copy(inputs[i].at[rows], inputs_buf.at[i, k], sems.at[i, k])
            copies[k, i].start()
    for k in range(len(targets)):
        for i in range(2):
            if k == 0:
                weights[i].wait()
            copies[k, i].wait()
            x = inputs_buf[i, k].reshape(count, width)
            part = jnp.dot(x, weights_buf[i], preferred_element_type=jnp.float32)
            e = exponents(part)
            outs[k][i * count : (i + 1) * count] = scaled(part, e)
            outs[k][2 * count + i * PAD : 2 * count + (i + 1) * PAD] = jnp.broadcast_to(e, (PAD, e.shape[1]))


def project(targets, row_count, place, query_acts, query_grads, proj_in, proj_out):
    queries, tokens, width = query_acts.shape
    own = queries // row_count
    out_width = proj_in.shape[1]
    height = 2 * own * tokens + 2 * PAD
    far = pl.BlockSpec(memory_space=pltpu.HBM)
    return pl.pallas_call(
        functools.partial(project_kernel, targets=targets),
        in_specs=[pl.BlockSpec(memory_space=pltpu.SMEM)] + [far] * 4,
        out_specs=[WHOLE] * len(targets),
        out_shape=[jax.ShapeDtypeStruct((height, out_width), jnp.float32)] * len(targets),
        scratch_shapes=[
            pltpu.VMEM((2, len(targets), own, tokens, width), query_acts.dtype),
            pltpu.VMEM((2,) + proj_in.shape, proj_in.dtype),
            pltpu.SemaphoreType.DMA((2, len(targets))),
            pltpu.SemaphoreType.DMA((2,)),
        ],
        compiler_params=pltpu.CompilerParams(vmem_limit_bytes=8 * MIB),
        name="project",
    )(place, *[pltpu.with_memory_space_constraint(x, pltpu.HBM) for x in (query_acts, query_grads, proj_in, proj_out)])


def kron_kernel(place_ref, after_ref, own_ref, *refs, tokens):
    del after_ref
    refs, outs, scratch = refs[:-5], refs[-5:-1], refs[-1]
    count = (own_ref.shape[0] - 2 * PAD) // 2
    sums = []
    for i in range(2):
        total = None
        for ref in (own_ref,) + refs:
            k = 2 * count + i * PAD
            part = restored(ref[i * count : (i + 1) * count], ref[k : k + 1])
            total = part if total is None else total + part
        sums.append(total)
    acts, grads = sums
    height = acts.shape[1] // 8
    group, col, sub = place_ref[0], place_ref[2], place_ref[3]
    for j in range(count // tokens):
        rows = slice(j * tokens, (j + 1) * tokens)
        scratch[j] = lax.dot_general(
            acts[rows], grads[rows], (((0,), (0,)), ((), ())), precision=HIGHEST, preferred_element_type=jnp.float32
        )
        for k in range(4):
            for s in range(2):
                start = (((col ^ (k % 2)) * 2 + (sub ^ s)) * 2 + (group ^ (k // 2))) * height
                outs[k][s, j * height : (j + 1) * height] = scratch[j, pl.ds(pl.multiple_of(start, height), height)]


def pack_kernel(*refs):
    kept, got_ref, out_ref = refs[:-2], refs[-2], refs[-1]
    lanes = got_ref.shape[-1]
    parts = jnp.concatenate([ref[0] for ref in kept] + [got_ref[...].reshape(-1, lanes)], 0)
    k = exponents(parts)
    out_ref[: parts.shape[0]] = scaled(parts, k)
    out_ref[parts.shape[0] :] = jnp.broadcast_to(k, (PAD, lanes))


def gather_kernel(after_ref, *refs):
    del after_ref
    for i, ref in enumerate(refs[:-1]):
        refs[-1][i] = ref[1]


def pack_scores_kernel(scores_ref, out_ref):
    scores = scores_ref[...]
    k = exponents(scores)
    out_ref[: scores.shape[0]] = scaled(scores, k)
    out_ref[scores.shape[0] :] = jnp.broadcast_to(k, (PAD, scores.shape[1]))


def sum_scores_kernel(*refs):
    out_ref = refs[-1]
    count = out_ref.shape[0]
    out_ref[...] = tree_sum([restored(ref[:count], ref[count : count + 1]) for ref in refs[:-1]])


SMALL = jnp.float8_e5m2
SMALL_SCALE = 2.0**20


def split(block):
    high = block.astype(jnp.bfloat16)
    return high, ((block - high.astype(jnp.float32)) * SMALL_SCALE).astype(SMALL)


def gram_split_kernel(place_ref, after_ref, gram_ref, *refs, first):
    del after_ref
    outs, (mark_ref, buffer, sems) = refs[:-3], refs[-3:]
    slots, tile, width = buffer.shape
    quarter = outs[0].shape[0]
    steps = quarter // tile
    total = steps * (len(outs) // 2)
    column = pl.multiple_of(place_ref[0] * width, width)
    sub = place_ref[3]

    def copy(i):
        part = first + i // steps
        start = (lax.rem(part // 2 + 1 + sub, 2) * 2 + lax.rem(part, 2)) * quarter + lax.rem(i, steps) * tile
        rows = pl.ds(pl.multiple_of(start, tile), tile)
        slot = lax.rem(i, slots)
        return pltpu.make_async_copy(gram_ref.at[rows, pl.ds(column, width)], buffer.at[slot], sems.at[slot])

    for i in range(min(slots - 1, total)):
        copy(i).start()

    for part in range(len(outs) // 2):

        @pl.loop(0, steps)
        def _(j):
            i = part * steps + j

            @pl.when(i + slots - 1 < total)
            def _():
                copy(i + slots - 1).start()

            copy(i).wait()
            high, low = split(buffer[lax.rem(i, slots)])
            start = pl.multiple_of(j * tile, tile)
            outs[2 * part][pl.ds(start, tile)] = high
            outs[2 * part + 1][pl.ds(start, tile)] = low

    mark_ref[...] = jnp.zeros_like(mark_ref)


def gram_split(place, after, inverse_gram, first, count, tile=128, slots=8):
    rows, width = inverse_gram.shape
    half, quarter = width // 2, rows // 4
    tile = min(tile, quarter)
    *quarters, mark = pl.pallas_call(
        functools.partial(gram_split_kernel, first=first),
        in_specs=[pl.BlockSpec(memory_space=pltpu.SMEM), WHOLE, pl.BlockSpec(memory_space=pltpu.HBM)],
        out_specs=[WHOLE] * (2 * count + 1),
        out_shape=[pltpu.VMEM((quarter, half), kind) for kind in (jnp.bfloat16, SMALL)] * count
        + [jax.ShapeDtypeStruct((8, 128), jnp.float32)],
        scratch_shapes=[pltpu.VMEM((slots, tile, half), jnp.float32), pltpu.SemaphoreType.DMA((slots,))],
        compiler_params=pltpu.CompilerParams(vmem_limit_bytes=12 * MIB),
        cost_estimate=pl.CostEstimate(flops=0, bytes_accessed=count * 4 * quarter * half, transcendentals=0),
        name="gram_split",
    )(place, after, inverse_gram)
    return [pltpu.with_memory_space_constraint(x, pltpu.VMEM) for x in quarters], mark


def gram_rows(group, grams, terms, small_terms, unit, out_ref):
    queries = small_terms.shape[1]
    quarter = grams[0].shape[0]
    for i in range(len(grams) // 2):
        part = jnp.dot(grams[2 * i][...], terms[...], preferred_element_type=jnp.float32)
        low = jnp.dot(grams[2 * i + 1][...], small_terms[...], preferred_element_type=jnp.float32)
        done = (part[:, :queries] + part[:, queries:] + low * unit[:1]).T
        for g in range(2):
            rows = slice(i * quarter, (i + 1) * quarter)
            out_ref[g ^ group, :, rows] = done[g * (queries // 2) : (g + 1) * (queries // 2)]


def away_kernel(place_ref, after_ref, *refs, row_count, own):
    del after_ref
    grams, sources = refs[:4], refs[4 : 4 + row_count]
    out_ref, terms, small_terms, unit, natural = refs[4 + row_count :]
    group, row, col, sub = (place_ref[i] for i in range(4))
    height, queries, lanes = natural.shape
    for z in range(row_count):
        count = sources[z].shape[0] - PAD
        piece = restored(sources[z][:count], sources[z][count : count + 1])
        for place in range(8):
            s, g, c = place // 4, place // 2 % 2, place % 2
            first = ((((g ^ group) * 2 + (c ^ col)) * 2 + (s ^ sub)) * row_count + (z ^ row)) * own
            for j in range(own):
                start = (place * own + j) * height
                natural[:, pl.ds(first + j, 1), :] = piece[start : start + height].reshape(height, 1, lanes)
    top = jnp.max(jnp.max(jnp.abs(natural[...]), axis=0), axis=1, keepdims=True)
    k = jnp.ceil(jnp.log(jnp.clip(top, 1e-30, 1e30)) * LOG2E)
    k = jnp.broadcast_to(k, (queries, lanes)).T[: unit.shape[0]]
    unit[...] = jnp.exp2(k - 7.0) * (1.0 / SMALL_SCALE)
    factor = jnp.exp2(7.0 - k[:1])
    for a in range(height):
        block = natural[a]
        high = block.astype(jnp.bfloat16).astype(jnp.float32)
        both = jnp.concatenate([high, block - high], 0).T
        terms[a * lanes : (a + 1) * lanes] = both.astype(jnp.bfloat16)
        small_terms[a * lanes : (a + 1) * lanes] = (both[:, :queries] * factor).astype(SMALL)
    gram_rows(group, grams, terms, small_terms, unit, out_ref)


def home_kernel(place_ref, *refs):
    gram_rows(place_ref[0], refs[:4], *refs[4:])


def gram_product(place, after, quarters, sources, own, lanes):
    quarter, half = quarters[0].shape
    row_count = len(sources)
    queries = 8 * row_count * own
    index = pl.BlockSpec(memory_space=pltpu.SMEM)

    out = jax.ShapeDtypeStruct((2, queries // 2, 2 * quarter), jnp.float32)
    common = dict(
        compiler_params=pltpu.CompilerParams(vmem_limit_bytes=8 * MIB),
        cost_estimate=pl.CostEstimate(
            flops=16 * queries * quarter * half, bytes_accessed=6 * quarter * half, transcendentals=0
        ),
    )
    away, *terms = pl.pallas_call(
        functools.partial(away_kernel, row_count=row_count, own=own),
        in_specs=[index] + [WHOLE] * (5 + row_count),
        out_specs=[WHOLE] * 4,
        out_shape=[
            out,
            jax.ShapeDtypeStruct((half, 2 * queries), jnp.bfloat16),
            jax.ShapeDtypeStruct((half, queries), SMALL),
            jax.ShapeDtypeStruct((PAD, queries), jnp.float32),
        ],
        scratch_shapes=[pltpu.VMEM((half // lanes, queries, lanes), jnp.float32)],
        name="away",
        **common,
    )(place, after, *quarters[:4], *sources)
    got = swapped(away, "sub")
    home = pl.pallas_call(
        home_kernel, in_specs=[index] + [WHOLE] * 7, out_specs=WHOLE, out_shape=out, name="home", **common
    )(place, *quarters[4:], *terms)
    total = home + got
    total = total[0] + swapped(total[1].astype(jnp.bfloat16), "groups").astype(jnp.float32)
    return total + swapped(total.astype(jnp.bfloat16), "col").astype(jnp.float32)


def others(pick, axis):
    size = lax.axis_size(axis)
    index = lax.axis_index(axis)
    return [lax.ppermute(pick(index ^ k), axis, [(i, i ^ k) for i in range(size)]) for k in range(1, size)]


def tree_sum(terms):
    while len(terms) > 1:
        terms = [terms[i] + terms[i + 1] for i in range(0, len(terms), 2)]
    return terms[0]


def swapped(array, axis):
    return others(lambda d: array, axis)[0]


def peers(pick):
    return [lax.ppermute(pick(k), ("groups", "col"), [(i, i ^ k) for i in range(4)]) for k in (1, 2, 3)]


def call(kernel, shapes, name, *args, specs=None, scratch=()):
    specs = specs or [pl.BlockSpec(memory_space=pltpu.SMEM) if a.dtype == jnp.int32 else WHOLE for a in args]
    many = isinstance(shapes, list)
    shapes = [jax.ShapeDtypeStruct(shape, jnp.float32) for shape in (shapes if many else [shapes])]
    outs = pl.pallas_call(
        kernel,
        in_specs=specs,
        out_specs=[WHOLE] * len(shapes),
        out_shape=shapes,
        scratch_shapes=list(scratch),
        compiler_params=pltpu.CompilerParams(vmem_limit_bytes=4 * MIB),
        name=name,
    )(*args)
    return outs if many else outs[0]


def body(query_acts, query_grads, proj_in, proj_out, inverse_gram, store_slab):
    row_count = lax.axis_size("row")
    place = jnp.stack([lax.axis_index(axis) for axis in ("groups", "row", "col", "sub")])
    queries, tokens = query_acts.shape[:2]
    own = queries // row_count
    in_width, out_width = proj_in.shape[1], proj_out.shape[1]
    got = []
    for targets in (range(row_count)[: row_count // 2 - 1 : -1], range(row_count)[: row_count // 2][::-1]):
        parts = project(targets, row_count, place, query_acts, query_grads, proj_in, proj_out)
        for k, part in zip(targets, parts):
            if k:
                got.append(lax.ppermute(part.astype(jnp.float16), "row", [(i, i ^ k) for i in range(row_count)]))
    quarters, mark = gram_split(place, parts[-1], inverse_gram, 0, 2)
    height = own * in_width // 8
    near = call(
        functools.partial(kron_kernel, tokens=tokens),
        [(2, height, out_width)] * 4,
        "kron",
        place,
        mark,
        parts[-1],
        *[x.astype(jnp.float32) for x in got],
        scratch=[pltpu.VMEM((own, in_width, out_width), jnp.float32)],
    )
    third, mark = gram_split(place, near[0], inverse_gram, 2, 1)
    near = [near[0]] + peers(lambda k: near[k])
    got = swapped(call(gather_kernel, (4, height, out_width), "gather", mark, *near), "sub")
    packed = call(pack_kernel, (8 * height + PAD, out_width), "pack", *near, got)
    wire = packed.astype(jnp.float16)
    sources = [packed] + [got.astype(jnp.float32) for got in others(lambda d: wire, "row")]
    fourth, mark = gram_split(place, packed, inverse_gram, 3, 1)
    total = gram_product(place, mark, quarters + third + fourth, sources, own, out_width)
    high = lax.reduce_precision(total, 8, 7)
    terms = jnp.concatenate([high, total - high], 0).astype(jnp.bfloat16)
    scores = lax.dot_general(
        terms, store_slab, (((1,), (1,)), ((), ())), preferred_element_type=jnp.float32
    )
    scores = scores[: total.shape[0]] + scores[total.shape[0] :]
    scores = scores + swapped(scores, "sub")
    packed = call(pack_scores_kernel, (scores.shape[0] + PAD, scores.shape[1]), "pack_scores", scores)
    packed = lax.reduce_precision(packed, 5, 10)
    wire = packed.astype(jnp.float16)
    sources = [packed] + [got.astype(jnp.float32) for got in others(lambda d: wire, "row")]
    return call(sum_scores_kernel, scores.shape, "sum_scores", *sources)


def solution(mesh):
    shape = mesh.shape
    rows = shape["row"]
    paired = shape["groups"] == shape["col"] == shape["sub"] == 2 and rows & (rows - 1) == 0

    def chosen(query_acts, query_grads, proj_in, proj_out, *rest):
        queries = query_acts.shape[0] // (shape["groups"] * shape["col"] * shape["sub"])
        square = proj_in.shape[1] == proj_out.shape[1] == 128
        chosen_body = body if paired and square and queries % rows == 0 else plain_body
        return jax.shard_map(
            chosen_body,
            mesh=mesh,
            in_specs=(
                P(("groups", "col", "sub"), None, "row"),
                P(("groups", "col", "sub"), None, "row"),
                P("row", None),
                P("row", None),
                P("row", ("col", "sub")),
                P(("groups", "col"), ("row", "sub")),
            ),
            out_specs=P("groups", "col"),
            check_vma=False,
        )(query_acts, query_grads, proj_in, proj_out, *rest)

    return chosen
```

```python
import functools

import jax
import jax.numpy as jnp
from jax import lax
from jax.experimental import pallas as pl
from jax.experimental.pallas import tpu as pltpu
from jax.sharding import PartitionSpec as P

HIGHEST = lax.Precision.HIGHEST


def plain_body(query_acts, query_grads, proj_in, proj_out, inverse_gram, store_slab):
    row_count = lax.axis_size("row")
    row_index = lax.axis_index("row")
    sub_index = lax.axis_index("sub")
    in_width = proj_in.shape[1]
    act_part = jnp.einsum("qtd,dk->qtk", query_acts, proj_in, preferred_element_type=jnp.float32)
    grad_part = jnp.einsum("qtd,dk->qtk", query_grads, proj_out, preferred_element_type=jnp.float32)
    store_width = store_slab.shape[1]
    row_block = in_width // row_count
    act_whole, grad_proj = lax.psum((act_part, grad_part), "row")
    act_proj = lax.dynamic_slice_in_dim(act_whole, row_index * row_block, row_block, 2)
    kron_part = jnp.einsum("qta,qtb->qab", act_proj, grad_proj, precision=HIGHEST)
    kron_feats = lax.all_gather(kron_part, ("col", "sub"), axis=0, tiled=True)
    features_flat = kron_feats.reshape(kron_feats.shape[0], -1)
    precond_part = jnp.dot(features_flat, inverse_gram, precision=HIGHEST)
    precond_block = lax.psum(precond_part, "row").astype(jnp.bfloat16)
    precond_full = lax.all_gather(precond_block, ("col", "sub"), axis=1, tiled=True)
    store_start = (row_index * lax.axis_size("sub") + sub_index) * store_width
    precond_mine = lax.dynamic_slice_in_dim(precond_full, store_start, store_width, 1)
    score_part = lax.dot_general(
        precond_mine, store_slab, (((1,), (1,)), ((), ())), preferred_element_type=jnp.float32
    )
    return lax.psum(score_part, ("row", "sub"))


PAD = 8
SHIFT = 13.0
LOG2E = 1.4426950408889634
WHOLE = pl.BlockSpec(memory_space=pltpu.VMEM)
MIB = 2**20


def exponents(part):
    top = jnp.max(jnp.abs(part), axis=0, keepdims=True)
    return jnp.ceil(jnp.log(jnp.clip(top, 1e-30, 1e30)) * LOG2E)


def scaled(part, k):
    return part * jnp.exp2(SHIFT - k)


def restored(part, k):
    return part * jnp.exp2(k - SHIFT)


def project_kernel(place_ref, *refs, targets):
    inputs, outs, (inputs_buf, weights_buf, sems, weights_sems) = refs[:4], refs[4:-4], refs[-4:]
    own, tokens, width = inputs_buf.shape[2:]
    count = own * tokens
    row = place_ref[1]
    weights = [pltpu.make_async_copy(inputs[2 + i], weights_buf.at[i], weights_sems.at[i]) for i in range(2)]
    copies = {}
    for k in range(len(targets)):
        for i in range(2):
            if k == 0:
                weights[i].start()
            rows = pl.ds((row ^ targets[k]) * own, own)
            copies[k, i] = pltpu.make_async_copy(inputs[i].at[rows], inputs_buf.at[i, k], sems.at[i, k])
            copies[k, i].start()
    for k in range(len(targets)):
        for i in range(2):
            if k == 0:
                weights[i].wait()
            copies[k, i].wait()
            x = inputs_buf[i, k].reshape(count, width)
            part = jnp.dot(x, weights_buf[i], preferred_element_type=jnp.float32)
            e = exponents(part)
            outs[k][i * count : (i + 1) * count] = scaled(part, e)
            outs[k][2 * count + i * PAD : 2 * count + (i + 1) * PAD] = jnp.broadcast_to(e, (PAD, e.shape[1]))


def project(targets, row_count, place, query_acts, query_grads, proj_in, proj_out):
    queries, tokens, width = query_acts.shape
    own = queries // row_count
    out_width = proj_in.shape[1]
    height = 2 * own * tokens + 2 * PAD
    far = pl.BlockSpec(memory_space=pltpu.HBM)
    return pl.pallas_call(
        functools.partial(project_kernel, targets=targets),
        in_specs=[pl.BlockSpec(memory_space=pltpu.SMEM)] + [far] * 4,
        out_specs=[WHOLE] * len(targets),
        out_shape=[jax.ShapeDtypeStruct((height, out_width), jnp.float32)] * len(targets),
        scratch_shapes=[
            pltpu.VMEM((2, len(targets), own, tokens, width), query_acts.dtype),
            pltpu.VMEM((2,) + proj_in.shape, proj_in.dtype),
            pltpu.SemaphoreType.DMA((2, len(targets))),
            pltpu.SemaphoreType.DMA((2,)),
        ],
        compiler_params=pltpu.CompilerParams(vmem_limit_bytes=8 * MIB),
        name="project",
    )(place, *[pltpu.with_memory_space_constraint(x, pltpu.HBM) for x in (query_acts, query_grads, proj_in, proj_out)])


def kron_kernel(place_ref, after_ref, own_ref, *refs, tokens):
    del after_ref
    refs, outs, scratch = refs[:-5], refs[-5:-1], refs[-1]
    count = (own_ref.shape[0] - 2 * PAD) // 2
    sums = []
    for i in range(2):
        total = None
        for ref in (own_ref,) + refs:
            k = 2 * count + i * PAD
            part = restored(ref[i * count : (i + 1) * count], ref[k : k + 1])
            total = part if total is None else total + part
        sums.append(total)
    acts, grads = sums
    height = acts.shape[1] // 8
    group, col, sub = place_ref[0], place_ref[2], place_ref[3]
    for j in range(count // tokens):
        rows = slice(j * tokens, (j + 1) * tokens)
        scratch[j] = lax.dot_general(
            acts[rows], grads[rows], (((0,), (0,)), ((), ())), precision=HIGHEST, preferred_element_type=jnp.float32
        )
        for k in range(4):
            for s in range(2):
                start = (((col ^ (k % 2)) * 2 + (sub ^ s)) * 2 + (group ^ (k // 2))) * height
                outs[k][s, j * height : (j + 1) * height] = scratch[j, pl.ds(pl.multiple_of(start, height), height)]


def pack_kernel(*refs):
    kept, got_ref, out_ref = refs[:-2], refs[-2], refs[-1]
    lanes = got_ref.shape[-1]
    parts = jnp.concatenate([ref[0] for ref in kept] + [got_ref[...].reshape(-1, lanes)], 0)
    k = exponents(parts)
    out_ref[: parts.shape[0]] = scaled(parts, k)
    out_ref[parts.shape[0] :] = jnp.broadcast_to(k, (PAD, lanes))


def gather_kernel(after_ref, *refs):
    del after_ref
    for i, ref in enumerate(refs[:-1]):
        refs[-1][i] = ref[1]


def pack_scores_kernel(scores_ref, out_ref):
    scores = scores_ref[...]
    k = exponents(scores)
    out_ref[: scores.shape[0]] = scaled(scores, k)
    out_ref[scores.shape[0] :] = jnp.broadcast_to(k, (PAD, scores.shape[1]))


def sum_scores_kernel(parts_ref, out_ref):
    count = out_ref.shape[0]
    out_ref[...] = tree_sum([restored(parts_ref[i, :count], parts_ref[i, count : count + 1]) for i in range(parts_ref.shape[0])])


SMALL = jnp.float8_e5m2
SMALL_SCALE = 2.0**20


def split(block):
    high = block.astype(jnp.bfloat16)
    return high, ((block - high.astype(jnp.float32)) * SMALL_SCALE).astype(SMALL)


def gram_split_kernel(place_ref, after_ref, gram_ref, *refs, first):
    del after_ref
    outs, (mark_ref, buffer, sems) = refs[:-3], refs[-3:]
    slots, tile, width = buffer.shape
    quarter = outs[0].shape[0]
    steps = quarter // tile
    total = steps * (len(outs) // 2)
    column = pl.multiple_of(place_ref[0] * width, width)
    sub = place_ref[3]

    def copy(i):
        part = first + i // steps
        start = (lax.rem(part // 2 + 1 + sub, 2) * 2 + lax.rem(part, 2)) * quarter + lax.rem(i, steps) * tile
        rows = pl.ds(pl.multiple_of(start, tile), tile)
        slot = lax.rem(i, slots)
        return pltpu.make_async_copy(gram_ref.at[rows, pl.ds(column, width)], buffer.at[slot], sems.at[slot])

    for i in range(min(slots - 1, total)):
        copy(i).start()

    for part in range(len(outs) // 2):

        @pl.loop(0, steps)
        def _(j):
            i = part * steps + j

            @pl.when(i + slots - 1 < total)
            def _():
                copy(i + slots - 1).start()

            copy(i).wait()
            high, low = split(buffer[lax.rem(i, slots)])
            start = pl.multiple_of(j * tile, tile)
            outs[2 * part][pl.ds(start, tile)] = high
            outs[2 * part + 1][pl.ds(start, tile)] = low

    mark_ref[...] = jnp.zeros_like(mark_ref)


def gram_split(place, after, inverse_gram, first, count, tile=128, slots=8):
    rows, width = inverse_gram.shape
    half, quarter = width // 2, rows // 4
    tile = min(tile, quarter)
    *quarters, mark = pl.pallas_call(
        functools.partial(gram_split_kernel, first=first),
        in_specs=[pl.BlockSpec(memory_space=pltpu.SMEM), WHOLE, pl.BlockSpec(memory_space=pltpu.HBM)],
        out_specs=[WHOLE] * (2 * count + 1),
        out_shape=[pltpu.VMEM((quarter, half), kind) for kind in (jnp.bfloat16, SMALL)] * count
        + [jax.ShapeDtypeStruct((8, 128), jnp.float32)],
        scratch_shapes=[pltpu.VMEM((slots, tile, half), jnp.float32), pltpu.SemaphoreType.DMA((slots,))],
        compiler_params=pltpu.CompilerParams(vmem_limit_bytes=12 * MIB),
        cost_estimate=pl.CostEstimate(flops=0, bytes_accessed=count * 4 * quarter * half, transcendentals=0),
        name="gram_split",
    )(place, after, inverse_gram)
    return [pltpu.with_memory_space_constraint(x, pltpu.VMEM) for x in quarters], mark


def gram_rows(group, high_ref, low_ref, terms, small_terms, unit, write):
    queries = small_terms.shape[1]
    part = jnp.dot(high_ref[...], terms[...], preferred_element_type=jnp.float32)
    low = jnp.dot(low_ref[...], small_terms[...], preferred_element_type=jnp.float32)
    done = (part[:, :queries] + part[:, queries:] + low * unit[:1]).T
    for g in range(2):
        write(g ^ group, done[g * (queries // 2) : (g + 1) * (queries // 2)])


def away_kernel(place_ref, after_ref, *refs, row_count, own):
    del after_ref
    grams, sources = refs[:4], refs[4 : 4 + row_count]
    out_ref, terms, small_terms, unit, natural = refs[4 + row_count :]
    group, row, col, sub = (place_ref[i] for i in range(4))
    height, queries, lanes = natural.shape
    for z in range(row_count):
        count = sources[z].shape[0] - PAD
        piece = restored(sources[z][:count], sources[z][count : count + 1])
        for place in range(8):
            s, g, c = place // 4, place // 2 % 2, place % 2
            first = ((((g ^ group) * 2 + (c ^ col)) * 2 + (s ^ sub)) * row_count + (z ^ row)) * own
            for j in range(own):
                start = (place * own + j) * height
                natural[:, pl.ds(first + j, 1), :] = piece[start : start + height].reshape(height, 1, lanes)
    top = jnp.max(jnp.max(jnp.abs(natural[...]), axis=0), axis=1, keepdims=True)
    k = jnp.ceil(jnp.log(jnp.clip(top, 1e-30, 1e30)) * LOG2E)
    k = jnp.broadcast_to(k, (queries, lanes)).T[: unit.shape[0]]
    unit[...] = jnp.exp2(k - 7.0) * (1.0 / SMALL_SCALE)
    factor = jnp.exp2(7.0 - k[:1])
    for a in range(height):
        block = natural[a]
        high = block.astype(jnp.bfloat16).astype(jnp.float32)
        both = jnp.concatenate([high, block - high], 0).T
        terms[a * lanes : (a + 1) * lanes] = both.astype(jnp.bfloat16)
        small_terms[a * lanes : (a + 1) * lanes] = (both[:, :queries] * factor).astype(SMALL)
    for i in range(2):

        def write(g, value):
            out_ref[i, g] = value

        gram_rows(group, *grams[2 * i : 2 * i + 2], terms, small_terms, unit, write)


def home_kernel(place_ref, high_ref, low_ref, terms_ref, small_ref, unit_ref, *refs):
    out_ref = refs[-1]

    def write(g, value):
        out_ref[g] = value

    gram_rows(place_ref[0], high_ref, low_ref, terms_ref, small_ref, unit_ref, write)


def join_kernel(early_ref, early_got_ref, late_ref, late_got_ref, early_out, early_wire, late_out, late_wire):
    early = early_ref[...] + early_got_ref[...].astype(jnp.float32)
    early_out[...] = early
    early_wire[...] = early.astype(jnp.bfloat16)
    late_out[...] = late_ref[0] + late_got_ref[0]
    late_wire[...] = (late_ref[1] + late_got_ref[1]).astype(jnp.bfloat16)


def gram_product(place, after, quarters, sources, own, lanes):
    quarter, half = quarters[0].shape
    row_count = len(sources)
    queries = 8 * row_count * own
    index = pl.BlockSpec(memory_space=pltpu.SMEM)

    def common(count):
        return dict(
            compiler_params=pltpu.CompilerParams(vmem_limit_bytes=8 * MIB),
            cost_estimate=pl.CostEstimate(
                flops=8 * count * queries * quarter * half, bytes_accessed=count * quarter * half, transcendentals=0
            ),
        )

    away, *terms = pl.pallas_call(
        functools.partial(away_kernel, row_count=row_count, own=own),
        in_specs=[index] + [WHOLE] * (5 + row_count),
        out_specs=[WHOLE] * 4,
        out_shape=[
            jax.ShapeDtypeStruct((2, 2, queries // 2, quarter), jnp.float32),
            jax.ShapeDtypeStruct((half, 2 * queries), jnp.bfloat16),
            jax.ShapeDtypeStruct((half, queries), SMALL),
            jax.ShapeDtypeStruct((PAD, queries), jnp.float32),
        ],
        scratch_shapes=[pltpu.VMEM((half // lanes, queries, lanes), jnp.float32)],
        name="away",
        **common(2),
    )(place, after, *quarters[:4], *sources)
    got = swapped(away, "sub")

    def home(i, *after):
        return pl.pallas_call(
            home_kernel,
            in_specs=[index] + [WHOLE] * (5 + len(after)),
            out_specs=WHOLE,
            out_shape=jax.ShapeDtypeStruct((2, queries // 2, quarter), jnp.float32),
            name="home",
            **common(1),
        )(place, *quarters[4 + 2 * i : 6 + 2 * i], *terms, *after)

    early = home(0) + got[0]
    wire = early[1].astype(jnp.bfloat16)
    late = home(1, wire)
    shape = (queries // 2, quarter)
    early, early_wire, late, late_wire = pl.pallas_call(
        join_kernel,
        in_specs=[WHOLE] * 4,
        out_specs=[WHOLE] * 4,
        out_shape=[jax.ShapeDtypeStruct(shape, kind) for kind in (jnp.float32, jnp.bfloat16) * 2],
        compiler_params=pltpu.CompilerParams(vmem_limit_bytes=4 * MIB),
        name="join",
    )(early[0], swapped(wire, "groups"), late, got[1])
    late = late + swapped(late_wire, "groups").astype(jnp.float32)
    early = early + swapped(early_wire, "col").astype(jnp.float32)
    late = late + swapped(late.astype(jnp.bfloat16), "col").astype(jnp.float32)
    return jnp.concatenate([early, late], 1)


def others(pick, axis):
    size = lax.axis_size(axis)
    index = lax.axis_index(axis)
    return [lax.ppermute(pick(index ^ k), axis, [(i, i ^ k) for i in range(size)]) for k in range(1, size)]


def tree_sum(terms):
    while len(terms) > 1:
        terms = [terms[i] + terms[i + 1] for i in range(0, len(terms), 2)]
    return terms[0]


def swapped(array, axis):
    return others(lambda d: array, axis)[0]


def peers(pick):
    return [lax.ppermute(pick(k), ("groups", "col"), [(i, i ^ k) for i in range(4)]) for k in (1, 2, 3)]


def call(kernel, shapes, name, *args, specs=None, scratch=()):
    specs = specs or [pl.BlockSpec(memory_space=pltpu.SMEM) if a.dtype == jnp.int32 else WHOLE for a in args]
    many = isinstance(shapes, list)
    shapes = [jax.ShapeDtypeStruct(shape, jnp.float32) for shape in (shapes if many else [shapes])]
    outs = pl.pallas_call(
        kernel,
        in_specs=specs,
        out_specs=[WHOLE] * len(shapes),
        out_shape=shapes,
        scratch_shapes=list(scratch),
        compiler_params=pltpu.CompilerParams(vmem_limit_bytes=4 * MIB),
        name=name,
    )(*args)
    return outs if many else outs[0]


def body(query_acts, query_grads, proj_in, proj_out, inverse_gram, store_slab):
    row_count = lax.axis_size("row")
    place = jnp.stack([lax.axis_index(axis) for axis in ("groups", "row", "col", "sub")])
    queries, tokens = query_acts.shape[:2]
    own = queries // row_count
    in_width, out_width = proj_in.shape[1], proj_out.shape[1]
    got = []
    for targets in (range(row_count)[: row_count // 2 - 1 : -1], range(row_count)[: row_count // 2][::-1]):
        parts = project(targets, row_count, place, query_acts, query_grads, proj_in, proj_out)
        for k, part in zip(targets, parts):
            if k:
                got.append(lax.ppermute(part.astype(jnp.float16), "row", [(i, i ^ k) for i in range(row_count)]))
    quarters, mark = gram_split(place, parts[-1], inverse_gram, 0, 2)
    height = own * in_width // 8
    near = call(
        functools.partial(kron_kernel, tokens=tokens),
        [(2, height, out_width)] * 4,
        "kron",
        place,
        mark,
        parts[-1],
        *[x.astype(jnp.float32) for x in got],
        scratch=[pltpu.VMEM((own, in_width, out_width), jnp.float32)],
    )
    third, mark = gram_split(place, near[0], inverse_gram, 2, 1)
    near = [near[0]] + peers(lambda k: near[k])
    got = swapped(call(gather_kernel, (4, height, out_width), "gather", mark, *near), "sub")
    packed = call(pack_kernel, (8 * height + PAD, out_width), "pack", *near, got)
    wire = packed.astype(jnp.float16)
    sources = [packed] + [got.astype(jnp.float32) for got in others(lambda d: wire, "row")]
    fourth, mark = gram_split(place, packed, inverse_gram, 3, 1)
    total = gram_product(place, mark, quarters + third + fourth, sources, own, out_width)
    high = lax.reduce_precision(total, 8, 7)
    terms = jnp.concatenate([high, total - high], 0).astype(jnp.bfloat16)
    scores = lax.dot_general(
        terms, store_slab, (((1,), (1,)), ((), ())), preferred_element_type=jnp.float32
    )
    scores = scores[: total.shape[0]] + scores[total.shape[0] :]
    packed = call(pack_scores_kernel, (scores.shape[0] + PAD, scores.shape[1]), "pack_scores", scores)
    whole = lax.all_gather(packed.astype(jnp.float16), ("row", "sub")).astype(jnp.float32)
    return call(sum_scores_kernel, scores.shape, "sum_scores", whole)


def solution(mesh):
    shape = mesh.shape
    rows = shape["row"]
    paired = shape["groups"] == shape["col"] == shape["sub"] == 2 and rows & (rows - 1) == 0

    def chosen(query_acts, query_grads, proj_in, proj_out, *rest):
        queries = query_acts.shape[0] // (shape["groups"] * shape["col"] * shape["sub"])
        square = proj_in.shape[1] == proj_out.shape[1] == 128
        chosen_body = body if paired and square and queries % rows == 0 else plain_body
        return jax.shard_map(
            chosen_body,
            mesh=mesh,
            in_specs=(
                P(("groups", "col", "sub"), None, "row"),
                P(("groups", "col", "sub"), None, "row"),
                P("row", None),
                P("row", None),
                P("row", ("col", "sub")),
                P(("groups", "col"), ("row", "sub")),
            ),
            out_specs=P("groups", "col"),
            check_vma=False,
        )(query_acts, query_grads, proj_in, proj_out, *rest)

    return chosen
```

```python
import functools

import jax
import jax.numpy as jnp
from jax import lax
from jax.experimental import pallas as pl
from jax.experimental.pallas import tpu as pltpu
from jax.sharding import PartitionSpec as P

HIGHEST = lax.Precision.HIGHEST


def plain_body(query_acts, query_grads, proj_in, proj_out, inverse_gram, store_slab):
    row_count = lax.axis_size("row")
    row_index = lax.axis_index("row")
    sub_index = lax.axis_index("sub")
    in_width = proj_in.shape[1]
    act_part = jnp.einsum("qtd,dk->qtk", query_acts, proj_in, preferred_element_type=jnp.float32)
    grad_part = jnp.einsum("qtd,dk->qtk", query_grads, proj_out, preferred_element_type=jnp.float32)
    store_width = store_slab.shape[1]
    row_block = in_width // row_count
    act_whole, grad_proj = lax.psum((act_part, grad_part), "row")
    act_proj = lax.dynamic_slice_in_dim(act_whole, row_index * row_block, row_block, 2)
    kron_part = jnp.einsum("qta,qtb->qab", act_proj, grad_proj, precision=HIGHEST)
    kron_feats = lax.all_gather(kron_part, ("col", "sub"), axis=0, tiled=True)
    features_flat = kron_feats.reshape(kron_feats.shape[0], -1)
    precond_part = jnp.dot(features_flat, inverse_gram, precision=HIGHEST)
    precond_block = lax.psum(precond_part, "row").astype(jnp.bfloat16)
    precond_full = lax.all_gather(precond_block, ("col", "sub"), axis=1, tiled=True)
    store_start = (row_index * lax.axis_size("sub") + sub_index) * store_width
    precond_mine = lax.dynamic_slice_in_dim(precond_full, store_start, store_width, 1)
    score_part = lax.dot_general(
        precond_mine, store_slab, (((1,), (1,)), ((), ())), preferred_element_type=jnp.float32
    )
    return lax.psum(score_part, ("row", "sub"))


PAD = 8
SHIFT = 13.0
LOG2E = 1.4426950408889634
WHOLE = pl.BlockSpec(memory_space=pltpu.VMEM)
MIB = 2**20


def exponents(part):
    top = jnp.max(jnp.abs(part), axis=0, keepdims=True)
    return jnp.ceil(jnp.log(jnp.clip(top, 1e-30, 1e30)) * LOG2E)


def scaled(part, k):
    return part * jnp.exp2(SHIFT - k)


def restored(part, k):
    return part * jnp.exp2(k - SHIFT)


def project_kernel(place_ref, *refs, targets):
    inputs, outs, (inputs_buf, weights_buf, sems, weights_sems) = refs[:4], refs[4:-4], refs[-4:]
    own, tokens, width = inputs_buf.shape[2:]
    count = own * tokens
    row = place_ref[1]
    weights = [pltpu.make_async_copy(inputs[2 + i], weights_buf.at[i], weights_sems.at[i]) for i in range(2)]
    copies = {}
    for k in range(len(targets)):
        for i in range(2):
            if k == 0:
                weights[i].start()
            rows = pl.ds((row ^ targets[k]) * own, own)
            copies[k, i] = pltpu.make_async_copy(inputs[i].at[rows], inputs_buf.at[i, k], sems.at[i, k])
            copies[k, i].start()
    for k in range(len(targets)):
        for i in range(2):
            if k == 0:
                weights[i].wait()
            copies[k, i].wait()
            x = inputs_buf[i, k].reshape(count, width)
            part = jnp.dot(x, weights_buf[i], preferred_element_type=jnp.float32)
            e = exponents(part)
            outs[k][i * count : (i + 1) * count] = scaled(part, e)
            outs[k][2 * count + i * PAD : 2 * count + (i + 1) * PAD] = jnp.broadcast_to(e, (PAD, e.shape[1]))


def project(targets, row_count, place, query_acts, query_grads, proj_in, proj_out):
    queries, tokens, width = query_acts.shape
    own = queries // row_count
    out_width = proj_in.shape[1]
    height = 2 * own * tokens + 2 * PAD
    far = pl.BlockSpec(memory_space=pltpu.HBM)
    return pl.pallas_call(
        functools.partial(project_kernel, targets=targets),
        in_specs=[pl.BlockSpec(memory_space=pltpu.SMEM)] + [far] * 4,
        out_specs=[WHOLE] * len(targets),
        out_shape=[jax.ShapeDtypeStruct((height, out_width), jnp.float32)] * len(targets),
        scratch_shapes=[
            pltpu.VMEM((2, len(targets), own, tokens, width), query_acts.dtype),
            pltpu.VMEM((2,) + proj_in.shape, proj_in.dtype),
            pltpu.SemaphoreType.DMA((2, len(targets))),
            pltpu.SemaphoreType.DMA((2,)),
        ],
        compiler_params=pltpu.CompilerParams(vmem_limit_bytes=8 * MIB),
        name="project",
    )(place, *[pltpu.with_memory_space_constraint(x, pltpu.HBM) for x in (query_acts, query_grads, proj_in, proj_out)])


def kron_kernel(place_ref, after_ref, own_ref, *refs, tokens):
    del after_ref
    refs, outs, scratch = refs[:-5], refs[-5:-1], refs[-1]
    count = (own_ref.shape[0] - 2 * PAD) // 2
    sums = []
    for i in range(2):
        total = None
        for ref in (own_ref,) + refs:
            k = 2 * count + i * PAD
            part = restored(ref[i * count : (i + 1) * count], ref[k : k + 1])
            total = part if total is None else total + part
        sums.append(total)
    acts, grads = sums
    height = acts.shape[1] // 8
    group, col, sub = place_ref[0], place_ref[2], place_ref[3]
    for j in range(count // tokens):
        rows = slice(j * tokens, (j + 1) * tokens)
        scratch[j] = lax.dot_general(
            acts[rows], grads[rows], (((0,), (0,)), ((), ())), precision=HIGHEST, preferred_element_type=jnp.float32
        )
        for k in range(4):
            for s in range(2):
                start = (((col ^ (k % 2)) * 2 + (sub ^ s)) * 2 + (group ^ (k // 2))) * height
                outs[k][s, j * height : (j + 1) * height] = scratch[j, pl.ds(pl.multiple_of(start, height), height)]


def pack_kernel(*refs):
    kept, got_ref, out_ref = refs[:-2], refs[-2], refs[-1]
    lanes = got_ref.shape[-1]
    parts = jnp.concatenate([ref[0] for ref in kept] + [got_ref[...].reshape(-1, lanes)], 0)
    k = exponents(parts)
    out_ref[: parts.shape[0]] = scaled(parts, k)
    out_ref[parts.shape[0] :] = jnp.broadcast_to(k, (PAD, lanes))


def gather_kernel(after_ref, *refs):
    del after_ref
    for i, ref in enumerate(refs[:-1]):
        refs[-1][i] = ref[1]


def pack_scores_kernel(scores_ref, out_ref):
    scores = scores_ref[...]
    k = exponents(scores)
    out_ref[: scores.shape[0]] = scaled(scores, k)
    out_ref[scores.shape[0] :] = jnp.broadcast_to(k, (PAD, scores.shape[1]))


def sum_scores_kernel(*refs):
    out_ref = refs[-1]
    count = out_ref.shape[0]
    out_ref[...] = tree_sum([restored(ref[:count], ref[count : count + 1]) for ref in refs[:-1]])


SMALL = jnp.float8_e5m2
SMALL_SCALE = 2.0**20


def split(block):
    high = block.astype(jnp.bfloat16)
    return high, ((block - high.astype(jnp.float32)) * SMALL_SCALE).astype(SMALL)


def gram_split_kernel(place_ref, after_ref, gram_ref, *refs, first):
    del after_ref
    outs, (mark_ref, buffer, sems) = refs[:-3], refs[-3:]
    slots, tile, width = buffer.shape
    quarter = outs[0].shape[0]
    steps = quarter // tile
    total = steps * (len(outs) // 2)
    column = pl.multiple_of(place_ref[0] * width, width)
    sub = place_ref[3]

    def copy(i):
        part = first + i // steps
        start = (lax.rem(part // 2 + 1 + sub, 2) * 2 + lax.rem(part, 2)) * quarter + lax.rem(i, steps) * tile
        rows = pl.ds(pl.multiple_of(start, tile), tile)
        slot = lax.rem(i, slots)
        return pltpu.make_async_copy(gram_ref.at[rows, pl.ds(column, width)], buffer.at[slot], sems.at[slot])

    for i in range(min(slots - 1, total)):
        copy(i).start()

    for part in range(len(outs) // 2):

        @pl.loop(0, steps)
        def _(j):
            i = part * steps + j

            @pl.when(i + slots - 1 < total)
            def _():
                copy(i + slots - 1).start()

            copy(i).wait()
            high, low = split(buffer[lax.rem(i, slots)])
            start = pl.multiple_of(j * tile, tile)
            outs[2 * part][pl.ds(start, tile)] = high
            outs[2 * part + 1][pl.ds(start, tile)] = low

    mark_ref[...] = jnp.zeros_like(mark_ref)


def gram_split(place, after, inverse_gram, first, count, tile=128, slots=8):
    rows, width = inverse_gram.shape
    half, quarter = width // 2, rows // 4
    tile = min(tile, quarter)
    *quarters, mark = pl.pallas_call(
        functools.partial(gram_split_kernel, first=first),
        in_specs=[pl.BlockSpec(memory_space=pltpu.SMEM), WHOLE, pl.BlockSpec(memory_space=pltpu.HBM)],
        out_specs=[WHOLE] * (2 * count + 1),
        out_shape=[pltpu.VMEM((quarter, half), kind) for kind in (jnp.bfloat16, SMALL)] * count
        + [jax.ShapeDtypeStruct((8, 128), jnp.float32)],
        scratch_shapes=[pltpu.VMEM((slots, tile, half), jnp.float32), pltpu.SemaphoreType.DMA((slots,))],
        compiler_params=pltpu.CompilerParams(vmem_limit_bytes=12 * MIB),
        cost_estimate=pl.CostEstimate(flops=0, bytes_accessed=count * 4 * quarter * half, transcendentals=0),
        name="gram_split",
    )(place, after, inverse_gram)
    return [pltpu.with_memory_space_constraint(x, pltpu.VMEM) for x in quarters], mark


def gram_rows(group, high_ref, low_ref, terms, small_terms, unit, write):
    queries = small_terms.shape[1]
    part = jnp.dot(high_ref[...], terms[...], preferred_element_type=jnp.float32)
    low = jnp.dot(low_ref[...], small_terms[...], preferred_element_type=jnp.float32)
    done = (part[:, :queries] + part[:, queries:] + low * unit[:1]).T
    for g in range(2):
        write(g ^ group, done[g * (queries // 2) : (g + 1) * (queries // 2)])


def away_kernel(place_ref, after_ref, *refs, row_count, own):
    del after_ref
    grams, sources = refs[:4], refs[4 : 4 + row_count]
    out_ref, terms, small_terms, unit, natural = refs[4 + row_count :]
    group, row, col, sub = (place_ref[i] for i in range(4))
    height, queries, lanes = natural.shape
    for z in range(row_count):
        count = sources[z].shape[0] - PAD
        piece = restored(sources[z][:count], sources[z][count : count + 1])
        for place in range(8):
            s, g, c = place // 4, place // 2 % 2, place % 2
            first = ((((g ^ group) * 2 + (c ^ col)) * 2 + (s ^ sub)) * row_count + (z ^ row)) * own
            for j in range(own):
                start = (place * own + j) * height
                natural[:, pl.ds(first + j, 1), :] = piece[start : start + height].reshape(height, 1, lanes)
    top = jnp.max(jnp.max(jnp.abs(natural[...]), axis=0), axis=1, keepdims=True)
    k = jnp.ceil(jnp.log(jnp.clip(top, 1e-30, 1e30)) * LOG2E)
    k = jnp.broadcast_to(k, (queries, lanes)).T[: unit.shape[0]]
    unit[...] = jnp.exp2(k - 7.0) * (1.0 / SMALL_SCALE)
    factor = jnp.exp2(7.0 - k[:1])
    for a in range(height):
        block = natural[a]
        high = block.astype(jnp.bfloat16).astype(jnp.float32)
        both = jnp.concatenate([high, block - high], 0).T
        terms[a * lanes : (a + 1) * lanes] = both.astype(jnp.bfloat16)
        small_terms[a * lanes : (a + 1) * lanes] = (both[:, :queries] * factor).astype(SMALL)
    for i in range(2):

        def write(g, value):
            out_ref[i, g] = value

        gram_rows(group, *grams[2 * i : 2 * i + 2], terms, small_terms, unit, write)


def home_kernel(place_ref, high_ref, low_ref, terms_ref, small_ref, unit_ref, *refs):
    out_ref = refs[-1]

    def write(g, value):
        out_ref[g] = value

    gram_rows(place_ref[0], high_ref, low_ref, terms_ref, small_ref, unit_ref, write)


def join_kernel(early_ref, early_got_ref, late_ref, late_got_ref, early_out, early_wire, late_out, late_wire):
    early = early_ref[...] + early_got_ref[...].astype(jnp.float32)
    early_out[...] = early
    early_wire[...] = early.astype(jnp.bfloat16)
    late_out[...] = late_ref[0] + late_got_ref[0]
    late_wire[...] = (late_ref[1] + late_got_ref[1]).astype(jnp.bfloat16)


def gram_product(place, after, quarters, sources, own, lanes):
    quarter, half = quarters[0].shape
    row_count = len(sources)
    queries = 8 * row_count * own
    index = pl.BlockSpec(memory_space=pltpu.SMEM)

    def common(count):
        return dict(
            compiler_params=pltpu.CompilerParams(vmem_limit_bytes=8 * MIB),
            cost_estimate=pl.CostEstimate(
                flops=8 * count * queries * quarter * half, bytes_accessed=count * quarter * half, transcendentals=0
            ),
        )

    away, *terms = pl.pallas_call(
        functools.partial(away_kernel, row_count=row_count, own=own),
        in_specs=[index] + [WHOLE] * (5 + row_count),
        out_specs=[WHOLE] * 4,
        out_shape=[
            jax.ShapeDtypeStruct((2, 2, queries // 2, quarter), jnp.float32),
            jax.ShapeDtypeStruct((half, 2 * queries), jnp.bfloat16),
            jax.ShapeDtypeStruct((half, queries), SMALL),
            jax.ShapeDtypeStruct((PAD, queries), jnp.float32),
        ],
        scratch_shapes=[pltpu.VMEM((half // lanes, queries, lanes), jnp.float32)],
        name="away",
        **common(2),
    )(place, after, *quarters[:4], *sources)
    got = swapped(away, "sub")

    def home(i, *after):
        return pl.pallas_call(
            home_kernel,
            in_specs=[index] + [WHOLE] * (5 + len(after)),
            out_specs=WHOLE,
            out_shape=jax.ShapeDtypeStruct((2, queries // 2, quarter), jnp.float32),
            name="home",
            **common(1),
        )(place, *quarters[4 + 2 * i : 6 + 2 * i], *terms, *after)

    early = home(0) + got[0]
    wire = early[1].astype(jnp.bfloat16)
    late = home(1, wire)
    shape = (queries // 2, quarter)
    early, early_wire, late, late_wire = pl.pallas_call(
        join_kernel,
        in_specs=[WHOLE] * 4,
        out_specs=[WHOLE] * 4,
        out_shape=[jax.ShapeDtypeStruct(shape, kind) for kind in (jnp.float32, jnp.bfloat16) * 2],
        compiler_params=pltpu.CompilerParams(vmem_limit_bytes=4 * MIB),
        name="join",
    )(early[0], swapped(wire, "groups"), late, got[1])
    late = late + swapped(late_wire, "groups").astype(jnp.float32)
    early = early + swapped(early_wire, "col").astype(jnp.float32)
    late = late + swapped(late.astype(jnp.bfloat16), "col").astype(jnp.float32)
    return jnp.concatenate([early, late], 1)


def others(pick, axis):
    size = lax.axis_size(axis)
    index = lax.axis_index(axis)
    return [lax.ppermute(pick(index ^ k), axis, [(i, i ^ k) for i in range(size)]) for k in range(1, size)]


def tree_sum(terms):
    while len(terms) > 1:
        terms = [terms[i] + terms[i + 1] for i in range(0, len(terms), 2)]
    return terms[0]


def swapped(array, axis):
    return others(lambda d: array, axis)[0]


def peers(pick):
    return [lax.ppermute(pick(k), ("groups", "col"), [(i, i ^ k) for i in range(4)]) for k in (1, 2, 3)]


def call(kernel, shapes, name, *args, specs=None, scratch=()):
    specs = specs or [pl.BlockSpec(memory_space=pltpu.SMEM) if a.dtype == jnp.int32 else WHOLE for a in args]
    many = isinstance(shapes, list)
    shapes = [jax.ShapeDtypeStruct(shape, jnp.float32) for shape in (shapes if many else [shapes])]
    outs = pl.pallas_call(
        kernel,
        in_specs=specs,
        out_specs=[WHOLE] * len(shapes),
        out_shape=shapes,
        scratch_shapes=list(scratch),
        compiler_params=pltpu.CompilerParams(vmem_limit_bytes=4 * MIB),
        name=name,
    )(*args)
    return outs if many else outs[0]


def body(query_acts, query_grads, proj_in, proj_out, inverse_gram, store_slab):
    row_count = lax.axis_size("row")
    place = jnp.stack([lax.axis_index(axis) for axis in ("groups", "row", "col", "sub")])
    queries, tokens = query_acts.shape[:2]
    own = queries // row_count
    in_width, out_width = proj_in.shape[1], proj_out.shape[1]
    got = []
    order = range(row_count)[::-1]
    for targets in (order[:1], order[1:]) if row_count > 1 else (order,):
        parts = project(targets, row_count, place, query_acts, query_grads, proj_in, proj_out)
        for k, part in zip(targets, parts):
            if k:
                got.append(lax.ppermute(part.astype(jnp.float16), "row", [(i, i ^ k) for i in range(row_count)]))
    quarters, mark = gram_split(place, parts[-1], inverse_gram, 0, 2)
    height = own * in_width // 8
    near = call(
        functools.partial(kron_kernel, tokens=tokens),
        [(2, height, out_width)] * 4,
        "kron",
        place,
        mark,
        parts[-1],
        *[x.astype(jnp.float32) for x in got],
        scratch=[pltpu.VMEM((own, in_width, out_width), jnp.float32)],
    )
    third, mark = gram_split(place, near[0], inverse_gram, 2, 1)
    near = [near[0]] + peers(lambda k: near[k])
    got = swapped(call(gather_kernel, (4, height, out_width), "gather", mark, *near), "sub")
    packed = call(pack_kernel, (8 * height + PAD, out_width), "pack", *near, got)
    wire = packed.astype(jnp.float16)
    sources = [packed] + [got.astype(jnp.float32) for got in others(lambda d: wire, "row")]
    fourth, mark = gram_split(place, packed, inverse_gram, 3, 1)
    total = gram_product(place, mark, quarters + third + fourth, sources, own, out_width)
    high = lax.reduce_precision(total, 8, 7)
    terms = jnp.concatenate([high, total - high], 0).astype(jnp.bfloat16)
    scores = lax.dot_general(
        terms, store_slab, (((1,), (1,)), ((), ())), preferred_element_type=jnp.float32
    )
    scores = scores[: total.shape[0]] + scores[total.shape[0] :]
    scores = scores + swapped(scores, "sub")
    packed = call(pack_scores_kernel, (scores.shape[0] + PAD, scores.shape[1]), "pack_scores", scores)
    packed = lax.reduce_precision(packed, 5, 10)
    wire = packed.astype(jnp.float16)
    sources = [packed] + [got.astype(jnp.float32) for got in others(lambda d: wire, "row")]
    return call(sum_scores_kernel, scores.shape, "sum_scores", *sources)


def solution(mesh):
    shape = mesh.shape
    rows = shape["row"]
    paired = shape["groups"] == shape["col"] == shape["sub"] == 2 and rows & (rows - 1) == 0

    def chosen(query_acts, query_grads, proj_in, proj_out, *rest):
        queries = query_acts.shape[0] // (shape["groups"] * shape["col"] * shape["sub"])
        square = proj_in.shape[1] == proj_out.shape[1] == 128
        chosen_body = body if paired and square and queries % rows == 0 else plain_body
        return jax.shard_map(
            chosen_body,
            mesh=mesh,
            in_specs=(
                P(("groups", "col", "sub"), None, "row"),
                P(("groups", "col", "sub"), None, "row"),
                P("row", None),
                P("row", None),
                P("row", ("col", "sub")),
                P(("groups", "col"), ("row", "sub")),
            ),
            out_specs=P("groups", "col"),
            check_vma=False,
        )(query_acts, query_grads, proj_in, proj_out, *rest)

    return chosen
```

```python
import functools

import jax
import jax.numpy as jnp
from jax import lax
from jax.experimental import pallas as pl
from jax.experimental.pallas import tpu as pltpu
from jax.sharding import PartitionSpec as P

HIGHEST = lax.Precision.HIGHEST


def plain_body(query_acts, query_grads, proj_in, proj_out, inverse_gram, store_slab):
    row_count = lax.axis_size("row")
    row_index = lax.axis_index("row")
    sub_index = lax.axis_index("sub")
    in_width = proj_in.shape[1]
    act_part = jnp.einsum("qtd,dk->qtk", query_acts, proj_in, preferred_element_type=jnp.float32)
    grad_part = jnp.einsum("qtd,dk->qtk", query_grads, proj_out, preferred_element_type=jnp.float32)
    store_width = store_slab.shape[1]
    row_block = in_width // row_count
    act_whole, grad_proj = lax.psum((act_part, grad_part), "row")
    act_proj = lax.dynamic_slice_in_dim(act_whole, row_index * row_block, row_block, 2)
    kron_part = jnp.einsum("qta,qtb->qab", act_proj, grad_proj, precision=HIGHEST)
    kron_feats = lax.all_gather(kron_part, ("col", "sub"), axis=0, tiled=True)
    features_flat = kron_feats.reshape(kron_feats.shape[0], -1)
    precond_part = jnp.dot(features_flat, inverse_gram, precision=HIGHEST)
    precond_block = lax.psum(precond_part, "row").astype(jnp.bfloat16)
    precond_full = lax.all_gather(precond_block, ("col", "sub"), axis=1, tiled=True)
    store_start = (row_index * lax.axis_size("sub") + sub_index) * store_width
    precond_mine = lax.dynamic_slice_in_dim(precond_full, store_start, store_width, 1)
    score_part = lax.dot_general(
        precond_mine, store_slab, (((1,), (1,)), ((), ())), preferred_element_type=jnp.float32
    )
    return lax.psum(score_part, ("row", "sub"))


PAD = 8
SHIFT = 13.0
LOG2E = 1.4426950408889634
WHOLE = pl.BlockSpec(memory_space=pltpu.VMEM)
MIB = 2**20


def exponents(part):
    top = jnp.max(jnp.abs(part), axis=0, keepdims=True)
    return jnp.ceil(jnp.log(jnp.clip(top, 1e-30, 1e30)) * LOG2E)


def scaled(part, k):
    return part * jnp.exp2(SHIFT - k)


def restored(part, k):
    return part * jnp.exp2(k - SHIFT)


def project_kernel(place_ref, *refs, targets):
    inputs, outs, (inputs_buf, weights_buf, sems, weights_sems) = refs[:4], refs[4:-4], refs[-4:]
    own, tokens, width = inputs_buf.shape[2:]
    count = own * tokens
    row = place_ref[1]
    weights = [pltpu.make_async_copy(inputs[2 + i], weights_buf.at[i], weights_sems.at[i]) for i in range(2)]
    copies = {}
    for k in range(len(targets)):
        for i in range(2):
            if k == 0:
                weights[i].start()
            rows = pl.ds((row ^ targets[k]) * own, own)
            copies[k, i] = pltpu.make_async_copy(inputs[i].at[rows], inputs_buf.at[i, k], sems.at[i, k])
            copies[k, i].start()
    for k in range(len(targets)):
        for i in range(2):
            if k == 0:
                weights[i].wait()
            copies[k, i].wait()
            x = inputs_buf[i, k].reshape(count, width)
            part = jnp.dot(x, weights_buf[i], preferred_element_type=jnp.float32)
            e = exponents(part)
            outs[k][i * count : (i + 1) * count] = scaled(part, e)
            outs[k][2 * count + i * PAD : 2 * count + (i + 1) * PAD] = jnp.broadcast_to(e, (PAD, e.shape[1]))


def project(targets, row_count, place, query_acts, query_grads, proj_in, proj_out):
    queries, tokens, width = query_acts.shape
    own = queries // row_count
    out_width = proj_in.shape[1]
    height = 2 * own * tokens + 2 * PAD
    far = pl.BlockSpec(memory_space=pltpu.HBM)
    return pl.pallas_call(
        functools.partial(project_kernel, targets=targets),
        in_specs=[pl.BlockSpec(memory_space=pltpu.SMEM)] + [far] * 4,
        out_specs=[WHOLE] * len(targets),
        out_shape=[jax.ShapeDtypeStruct((height, out_width), jnp.float32)] * len(targets),
        scratch_shapes=[
            pltpu.VMEM((2, len(targets), own, tokens, width), query_acts.dtype),
            pltpu.VMEM((2,) + proj_in.shape, proj_in.dtype),
            pltpu.SemaphoreType.DMA((2, len(targets))),
            pltpu.SemaphoreType.DMA((2,)),
        ],
        compiler_params=pltpu.CompilerParams(vmem_limit_bytes=8 * MIB),
        name="project",
    )(place, *[pltpu.with_memory_space_constraint(x, pltpu.HBM) for x in (query_acts, query_grads, proj_in, proj_out)])


def kron_kernel(place_ref, after_ref, own_ref, *refs, tokens):
    del after_ref
    refs, outs, scratch = refs[:-5], refs[-5:-1], refs[-1]
    count = (own_ref.shape[0] - 2 * PAD) // 2
    sums = []
    for i in range(2):
        total = None
        for ref in (own_ref,) + refs:
            k = 2 * count + i * PAD
            part = restored(ref[i * count : (i + 1) * count], ref[k : k + 1])
            total = part if total is None else total + part
        sums.append(total)
    acts, grads = sums
    height = acts.shape[1] // 8
    group, col, sub = place_ref[0], place_ref[2], place_ref[3]
    for j in range(count // tokens):
        rows = slice(j * tokens, (j + 1) * tokens)
        scratch[j] = lax.dot_general(
            acts[rows], grads[rows], (((0,), (0,)), ((), ())), precision=HIGHEST, preferred_element_type=jnp.float32
        )
        for k in range(4):
            for s in range(2):
                start = (((col ^ (k % 2)) * 2 + (sub ^ s)) * 2 + (group ^ (k // 2))) * height
                outs[k][s, j * height : (j + 1) * height] = scratch[j, pl.ds(pl.multiple_of(start, height), height)]


def pack_kernel(*refs):
    kept, got_ref, out_ref = refs[:-2], refs[-2], refs[-1]
    lanes = got_ref.shape[-1]
    parts = jnp.concatenate([ref[0] for ref in kept] + [got_ref[...].reshape(-1, lanes)], 0)
    k = exponents(parts)
    out_ref[: parts.shape[0]] = scaled(parts, k)
    out_ref[parts.shape[0] :] = jnp.broadcast_to(k, (PAD, lanes))


def gather_kernel(after_ref, *refs):
    del after_ref
    for i, ref in enumerate(refs[:-1]):
        refs[-1][i] = ref[1]


def pack_scores_kernel(scores_ref, out_ref):
    scores = scores_ref[...]
    k = exponents(scores)
    out_ref[: scores.shape[0]] = scaled(scores, k)
    out_ref[scores.shape[0] :] = jnp.broadcast_to(k, (PAD, scores.shape[1]))


def sum_scores_kernel(*refs):
    out_ref = refs[-1]
    count = out_ref.shape[0]
    out_ref[...] = tree_sum([restored(ref[:count], ref[count : count + 1]) for ref in refs[:-1]])


SMALL = jnp.float8_e5m2
SMALL_SCALE = 2.0**20


def split(block):
    high = block.astype(jnp.bfloat16)
    return high, ((block - high.astype(jnp.float32)) * SMALL_SCALE).astype(SMALL)


def gram_split_kernel(place_ref, after_ref, gram_ref, *refs, first):
    del after_ref
    outs, (mark_ref, buffer, sems) = refs[:-3], refs[-3:]
    slots, tile, width = buffer.shape
    quarter = outs[0].shape[0]
    steps = quarter // tile
    total = steps * (len(outs) // 2)
    column = pl.multiple_of(place_ref[0] * width, width)
    sub = place_ref[3]

    def copy(i):
        part = first + i // steps
        start = (lax.rem(part // 2 + 1 + sub, 2) * 2 + lax.rem(part, 2)) * quarter + lax.rem(i, steps) * tile
        rows = pl.ds(pl.multiple_of(start, tile), tile)
        slot = lax.rem(i, slots)
        return pltpu.make_async_copy(gram_ref.at[rows, pl.ds(column, width)], buffer.at[slot], sems.at[slot])

    for i in range(min(slots - 1, total)):
        copy(i).start()

    for part in range(len(outs) // 2):

        @pl.loop(0, steps)
        def _(j):
            i = part * steps + j

            @pl.when(i + slots - 1 < total)
            def _():
                copy(i + slots - 1).start()

            copy(i).wait()
            high, low = split(buffer[lax.rem(i, slots)])
            start = pl.multiple_of(j * tile, tile)
            outs[2 * part][pl.ds(start, tile)] = high
            outs[2 * part + 1][pl.ds(start, tile)] = low

    mark_ref[...] = jnp.zeros_like(mark_ref)


def gram_split(place, after, inverse_gram, first, count, tile=128, slots=8):
    rows, width = inverse_gram.shape
    half, quarter = width // 2, rows // 4
    tile = min(tile, quarter)
    *quarters, mark = pl.pallas_call(
        functools.partial(gram_split_kernel, first=first),
        in_specs=[pl.BlockSpec(memory_space=pltpu.SMEM), WHOLE, pl.BlockSpec(memory_space=pltpu.HBM)],
        out_specs=[WHOLE] * (2 * count + 1),
        out_shape=[pltpu.VMEM((quarter, half), kind) for kind in (jnp.bfloat16, SMALL)] * count
        + [jax.ShapeDtypeStruct((8, 128), jnp.float32)],
        scratch_shapes=[pltpu.VMEM((slots, tile, half), jnp.float32), pltpu.SemaphoreType.DMA((slots,))],
        compiler_params=pltpu.CompilerParams(vmem_limit_bytes=12 * MIB),
        cost_estimate=pl.CostEstimate(flops=0, bytes_accessed=count * 4 * quarter * half, transcendentals=0),
        name="gram_split",
    )(place, after, inverse_gram)
    return [pltpu.with_memory_space_constraint(x, pltpu.VMEM) for x in quarters], mark


def gram_rows(group, high_ref, low_ref, terms, small_terms, unit, write):
    queries = small_terms.shape[1]
    part = jnp.dot(high_ref[...], terms[...], preferred_element_type=jnp.float32)
    low = jnp.dot(low_ref[...], small_terms[...], preferred_element_type=jnp.float32)
    done = (part[:, :queries] + part[:, queries:] + low * unit[:1]).T
    for g in range(2):
        write(g ^ group, done[g * (queries // 2) : (g + 1) * (queries // 2)])


def away_kernel(place_ref, after_ref, *refs, row_count, own):
    del after_ref
    grams, sources = refs[:4], refs[4 : 4 + row_count]
    out_ref, terms, small_terms, unit, natural = refs[4 + row_count :]
    group, row, col, sub = (place_ref[i] for i in range(4))
    height, queries, lanes = natural.shape
    for z in range(row_count):
        count = sources[z].shape[0] - PAD
        piece = restored(sources[z][:count], sources[z][count : count + 1])
        for place in range(8):
            s, g, c = place // 4, place // 2 % 2, place % 2
            first = ((((g ^ group) * 2 + (c ^ col)) * 2 + (s ^ sub)) * row_count + (z ^ row)) * own
            for j in range(own):
                start = (place * own + j) * height
                natural[:, pl.ds(first + j, 1), :] = piece[start : start + height].reshape(height, 1, lanes)
    top = jnp.max(jnp.max(jnp.abs(natural[...]), axis=0), axis=1, keepdims=True)
    k = jnp.ceil(jnp.log(jnp.clip(top, 1e-30, 1e30)) * LOG2E)
    k = jnp.broadcast_to(k, (queries, lanes)).T[: unit.shape[0]]
    unit[...] = jnp.exp2(k - 7.0) * (1.0 / SMALL_SCALE)
    factor = jnp.exp2(7.0 - k[:1])
    for a in range(height):
        block = natural[a]
        high = block.astype(jnp.bfloat16).astype(jnp.float32)
        both = jnp.concatenate([high, block - high], 0).T
        terms[a * lanes : (a + 1) * lanes] = both.astype(jnp.bfloat16)
        small_terms[a * lanes : (a + 1) * lanes] = (both[:, :queries] * factor).astype(SMALL)
    for i in range(2):

        def write(g, value):
            out_ref[i, g] = value

        gram_rows(group, *grams[2 * i : 2 * i + 2], terms, small_terms, unit, write)


def home_kernel(place_ref, high_ref, low_ref, terms_ref, small_ref, unit_ref, *refs):
    out_ref = refs[-1]

    def write(g, value):
        out_ref[g] = value

    gram_rows(place_ref[0], high_ref, low_ref, terms_ref, small_ref, unit_ref, write)


def join_kernel(early_ref, early_got_ref, late_ref, late_got_ref, early_out, early_wire, late_out, late_wire):
    early = early_ref[...] + early_got_ref[...].astype(jnp.float32)
    early_out[...] = early
    early_wire[...] = early.astype(jnp.bfloat16)
    late_out[...] = late_ref[0] + late_got_ref[0]
    late_wire[...] = (late_ref[1] + late_got_ref[1]).astype(jnp.bfloat16)


def gram_product(place, after, quarters, sources, own, lanes):
    quarter, half = quarters[0].shape
    row_count = len(sources)
    queries = 8 * row_count * own
    index = pl.BlockSpec(memory_space=pltpu.SMEM)

    def common(count):
        return dict(
            compiler_params=pltpu.CompilerParams(vmem_limit_bytes=8 * MIB),
            cost_estimate=pl.CostEstimate(
                flops=8 * count * queries * quarter * half, bytes_accessed=count * quarter * half, transcendentals=0
            ),
        )

    away, *terms = pl.pallas_call(
        functools.partial(away_kernel, row_count=row_count, own=own),
        in_specs=[index] + [WHOLE] * (5 + row_count),
        out_specs=[WHOLE] * 4,
        out_shape=[
            jax.ShapeDtypeStruct((2, 2, queries // 2, quarter), jnp.float32),
            jax.ShapeDtypeStruct((half, 2 * queries), jnp.bfloat16),
            jax.ShapeDtypeStruct((half, queries), SMALL),
            jax.ShapeDtypeStruct((PAD, queries), jnp.float32),
        ],
        scratch_shapes=[pltpu.VMEM((half // lanes, queries, lanes), jnp.float32)],
        name="away",
        **common(2),
    )(place, after, *quarters[:4], *sources)
    got = swapped(away, "sub")

    def home(i, *after):
        return pl.pallas_call(
            home_kernel,
            in_specs=[index] + [WHOLE] * (5 + len(after)),
            out_specs=WHOLE,
            out_shape=jax.ShapeDtypeStruct((2, queries // 2, quarter), jnp.float32),
            name="home",
            **common(1),
        )(place, *quarters[4 + 2 * i : 6 + 2 * i], *terms, *after)

    early = home(0) + got[0]
    wire = early[1].astype(jnp.bfloat16)
    late = home(1, wire)
    shape = (queries // 2, quarter)
    early, early_wire, late, late_wire = pl.pallas_call(
        join_kernel,
        in_specs=[WHOLE] * 4,
        out_specs=[WHOLE] * 4,
        out_shape=[jax.ShapeDtypeStruct(shape, kind) for kind in (jnp.float32, jnp.bfloat16) * 2],
        compiler_params=pltpu.CompilerParams(vmem_limit_bytes=4 * MIB),
        name="join",
    )(early[0], swapped(wire, "groups"), late, got[1])
    late = late + swapped(late_wire, "groups").astype(jnp.float32)
    early = early + swapped(early_wire, "col").astype(jnp.float32)
    late = late + swapped(late.astype(jnp.bfloat16), "col").astype(jnp.float32)
    return jnp.concatenate([early, late], 1)


def others(pick, axis):
    size = lax.axis_size(axis)
    index = lax.axis_index(axis)
    return [lax.ppermute(pick(index ^ k), axis, [(i, i ^ k) for i in range(size)]) for k in range(1, size)]


def tree_sum(terms):
    while len(terms) > 1:
        terms = [terms[i] + terms[i + 1] for i in range(0, len(terms), 2)]
    return terms[0]


def swapped(array, axis):
    return others(lambda d: array, axis)[0]


def peers(pick):
    return [lax.ppermute(pick(k), ("groups", "col"), [(i, i ^ k) for i in range(4)]) for k in (1, 2, 3)]


def call(kernel, shapes, name, *args, specs=None, scratch=()):
    specs = specs or [pl.BlockSpec(memory_space=pltpu.SMEM) if a.dtype == jnp.int32 else WHOLE for a in args]
    many = isinstance(shapes, list)
    shapes = [jax.ShapeDtypeStruct(shape, jnp.float32) for shape in (shapes if many else [shapes])]
    outs = pl.pallas_call(
        kernel,
        in_specs=specs,
        out_specs=[WHOLE] * len(shapes),
        out_shape=shapes,
        scratch_shapes=list(scratch),
        compiler_params=pltpu.CompilerParams(vmem_limit_bytes=4 * MIB),
        name=name,
    )(*args)
    return outs if many else outs[0]


def body(query_acts, query_grads, proj_in, proj_out, inverse_gram, store_slab):
    row_count = lax.axis_size("row")
    place = jnp.stack([lax.axis_index(axis) for axis in ("groups", "row", "col", "sub")])
    queries, tokens = query_acts.shape[:2]
    own = queries // row_count
    in_width, out_width = proj_in.shape[1], proj_out.shape[1]
    got = []
    for targets in (range(row_count)[: row_count // 2 - 1 : -1], range(row_count)[: row_count // 2][::-1]):
        parts = project(targets, row_count, place, query_acts, query_grads, proj_in, proj_out)
        for k, part in zip(targets, parts):
            if k:
                got.append(lax.ppermute(part.astype(jnp.float16), "row", [(i, i ^ k) for i in range(row_count)]))
    quarters, mark = gram_split(place, parts[-1], inverse_gram, 0, 2)
    height = own * in_width // 8
    near = call(
        functools.partial(kron_kernel, tokens=tokens),
        [(2, height, out_width)] * 4,
        "kron",
        place,
        mark,
        parts[-1],
        *[x.astype(jnp.float32) for x in got],
        scratch=[pltpu.VMEM((own, in_width, out_width), jnp.float32)],
    )
    third, mark = gram_split(place, near[0], inverse_gram, 2, 1)
    near = [near[0]] + peers(lambda k: near[k])
    got = swapped(call(gather_kernel, (4, height, out_width), "gather", mark, *near), "sub")
    packed = call(pack_kernel, (8 * height + PAD, out_width), "pack", *near, got)
    wire = packed.astype(jnp.float16)
    sources = [packed] + [got.astype(jnp.float32) for got in others(lambda d: wire, "row")]
    fourth, mark = gram_split(place, packed, inverse_gram, 3, 1)
    total = gram_product(place, mark, quarters + third + fourth, sources, own, out_width)
    high = lax.reduce_precision(total, 8, 7)
    terms = jnp.concatenate([high, total - high], 0).astype(jnp.bfloat16)
    scores = lax.dot_general(
        terms, store_slab, (((1,), (1,)), ((), ())), preferred_element_type=jnp.float32
    )
    scores = scores[: total.shape[0]] + scores[total.shape[0] :]
    scores = scores + swapped(scores, "sub")
    packed = call(pack_scores_kernel, (scores.shape[0] + PAD, scores.shape[1]), "pack_scores", scores)
    packed = lax.reduce_precision(packed, 5, 10)
    wire = packed.astype(jnp.float16)
    if row_count == 4:
        rows, axes = range(row_count), ("row", "sub")
        near = lax.ppermute(wire, axes, [(2 * r + s, 2 * (r ^ (1 + s)) + s) for r in rows for s in range(2)])
        far = lax.ppermute(wire, axes, [(2 * r + 1, 2 * (r ^ 3) + 1) for r in rows])
        first = jnp.where(lax.axis_index("sub") == 0, packed, far.astype(jnp.float32))
        half = call(sum_scores_kernel, scores.shape, "sum_scores", first, near.astype(jnp.float32))
        return half + swapped(half, "sub")
    sources = [packed] + [got.astype(jnp.float32) for got in others(lambda d: wire, "row")]
    return call(sum_scores_kernel, scores.shape, "sum_scores", *sources)


def solution(mesh):
    shape = mesh.shape
    rows = shape["row"]
    paired = shape["groups"] == shape["col"] == shape["sub"] == 2 and rows & (rows - 1) == 0

    def chosen(query_acts, query_grads, proj_in, proj_out, *rest):
        queries = query_acts.shape[0] // (shape["groups"] * shape["col"] * shape["sub"])
        square = proj_in.shape[1] == proj_out.shape[1] == 128
        chosen_body = body if paired and square and queries % rows == 0 else plain_body
        return jax.shard_map(
            chosen_body,
            mesh=mesh,
            in_specs=(
                P(("groups", "col", "sub"), None, "row"),
                P(("groups", "col", "sub"), None, "row"),
                P("row", None),
                P("row", None),
                P("row", ("col", "sub")),
                P(("groups", "col"), ("row", "sub")),
            ),
            out_specs=P("groups", "col"),
            check_vma=False,
        )(query_acts, query_grads, proj_in, proj_out, *rest)

    return chosen
```

```python
import functools

import jax
import jax.numpy as jnp
from jax import lax
from jax.experimental import pallas as pl
from jax.experimental.pallas import tpu as pltpu
from jax.sharding import PartitionSpec as P

HIGHEST = lax.Precision.HIGHEST


def plain_body(query_acts, query_grads, proj_in, proj_out, inverse_gram, store_slab):
    row_count = lax.axis_size("row")
    row_index = lax.axis_index("row")
    sub_index = lax.axis_index("sub")
    in_width = proj_in.shape[1]
    act_part = jnp.einsum("qtd,dk->qtk", query_acts, proj_in, preferred_element_type=jnp.float32)
    grad_part = jnp.einsum("qtd,dk->qtk", query_grads, proj_out, preferred_element_type=jnp.float32)
    store_width = store_slab.shape[1]
    row_block = in_width // row_count
    act_whole, grad_proj = lax.psum((act_part, grad_part), "row")
    act_proj = lax.dynamic_slice_in_dim(act_whole, row_index * row_block, row_block, 2)
    kron_part = jnp.einsum("qta,qtb->qab", act_proj, grad_proj, precision=HIGHEST)
    kron_feats = lax.all_gather(kron_part, ("col", "sub"), axis=0, tiled=True)
    features_flat = kron_feats.reshape(kron_feats.shape[0], -1)
    precond_part = jnp.dot(features_flat, inverse_gram, precision=HIGHEST)
    precond_block = lax.psum(precond_part, "row").astype(jnp.bfloat16)
    precond_full = lax.all_gather(precond_block, ("col", "sub"), axis=1, tiled=True)
    store_start = (row_index * lax.axis_size("sub") + sub_index) * store_width
    precond_mine = lax.dynamic_slice_in_dim(precond_full, store_start, store_width, 1)
    score_part = lax.dot_general(
        precond_mine, store_slab, (((1,), (1,)), ((), ())), preferred_element_type=jnp.float32
    )
    return lax.psum(score_part, ("row", "sub"))


PAD = 8
SHIFT = 13.0
LOG2E = 1.4426950408889634
WHOLE = pl.BlockSpec(memory_space=pltpu.VMEM)
MIB = 2**20


def exponents(part):
    top = jnp.max(jnp.abs(part), axis=0, keepdims=True)
    return jnp.ceil(jnp.log(jnp.clip(top, 1e-30, 1e30)) * LOG2E)


def scaled(part, k):
    return part * jnp.exp2(SHIFT - k)


def restored(part, k):
    return part * jnp.exp2(k - SHIFT)


def project_kernel(place_ref, *refs, targets):
    inputs, outs, (inputs_buf, weights_buf, sems, weights_sems) = refs[:4], refs[4:-4], refs[-4:]
    own, tokens, width = inputs_buf.shape[2:]
    count = own * tokens
    row = place_ref[1]
    weights = [pltpu.make_async_copy(inputs[2 + i], weights_buf.at[i], weights_sems.at[i]) for i in range(2)]
    copies = {}
    for k in range(len(targets)):
        for i in range(2):
            if k == 0:
                weights[i].start()
            rows = pl.ds((row ^ targets[k]) * own, own)
            copies[k, i] = pltpu.make_async_copy(inputs[i].at[rows], inputs_buf.at[i, k], sems.at[i, k])
            copies[k, i].start()
    for k in range(len(targets)):
        for i in range(2):
            if k == 0:
                weights[i].wait()
            copies[k, i].wait()
            x = inputs_buf[i, k].reshape(count, width)
            part = jnp.dot(x, weights_buf[i], preferred_element_type=jnp.float32)
            e = exponents(part)
            outs[k][i * count : (i + 1) * count] = scaled(part, e)
            outs[k][2 * count + i * PAD : 2 * count + (i + 1) * PAD] = jnp.broadcast_to(e, (PAD, e.shape[1]))


def project(targets, row_count, place, query_acts, query_grads, proj_in, proj_out):
    queries, tokens, width = query_acts.shape
    own = queries // row_count
    out_width = proj_in.shape[1]
    height = 2 * own * tokens + 2 * PAD
    far = pl.BlockSpec(memory_space=pltpu.HBM)
    return pl.pallas_call(
        functools.partial(project_kernel, targets=targets),
        in_specs=[pl.BlockSpec(memory_space=pltpu.SMEM)] + [far] * 4,
        out_specs=[WHOLE] * len(targets),
        out_shape=[jax.ShapeDtypeStruct((height, out_width), jnp.float32)] * len(targets),
        scratch_shapes=[
            pltpu.VMEM((2, len(targets), own, tokens, width), query_acts.dtype),
            pltpu.VMEM((2,) + proj_in.shape, proj_in.dtype),
            pltpu.SemaphoreType.DMA((2, len(targets))),
            pltpu.SemaphoreType.DMA((2,)),
        ],
        compiler_params=pltpu.CompilerParams(vmem_limit_bytes=8 * MIB),
        name="project",
    )(place, *[pltpu.with_memory_space_constraint(x, pltpu.HBM) for x in (query_acts, query_grads, proj_in, proj_out)])


def two_terms(block):
    high = block.astype(jnp.bfloat16)
    return high, (block - high.astype(jnp.float32)).astype(jnp.bfloat16)


def kron_kernel(place_ref, after_ref, own_ref, *refs, tokens):
    del after_ref
    refs, outs, scratch = refs[:-5], refs[-5:-1], refs[-1]
    count = (own_ref.shape[0] - 2 * PAD) // 2
    sums = []
    for i in range(2):
        total = None
        for ref in (own_ref,) + refs:
            k = 2 * count + i * PAD
            part = restored(ref[i * count : (i + 1) * count], ref[k : k + 1])
            total = part if total is None else total + part
        sums.append(total)
    acts, grads = sums
    height = acts.shape[1] // 8
    group, col, sub = place_ref[0], place_ref[2], place_ref[3]
    for j in range(count // tokens):
        rows = slice(j * tokens, (j + 1) * tokens)
        act_high, act_low = two_terms(acts[rows].T)
        grad_high, grad_low = two_terms(grads[rows])
        dot = functools.partial(jnp.dot, preferred_element_type=jnp.float32)
        scratch[j] = dot(act_high, grad_high) + (dot(act_high, grad_low) + dot(act_low, grad_high))
        for k in range(4):
            for s in range(2):
                start = (((col ^ (k % 2)) * 2 + (sub ^ s)) * 2 + (group ^ (k // 2))) * height
                outs[k][s, j * height : (j + 1) * height] = scratch[j, pl.ds(pl.multiple_of(start, height), height)]


def pack_kernel(*refs):
    kept, got_ref, out_ref = refs[:-2], refs[-2], refs[-1]
    lanes = got_ref.shape[-1]
    parts = jnp.concatenate([ref[0] for ref in kept] + [got_ref[...].reshape(-1, lanes)], 0)
    k = exponents(parts)
    out_ref[: parts.shape[0]] = scaled(parts, k)
    out_ref[parts.shape[0] :] = jnp.broadcast_to(k, (PAD, lanes))


def gather_kernel(after_ref, *refs):
    del after_ref
    for i, ref in enumerate(refs[:-1]):
        refs[-1][i] = ref[1]


def pack_scores_kernel(scores_ref, out_ref):
    scores = scores_ref[...]
    k = exponents(scores)
    out_ref[: scores.shape[0]] = scaled(scores, k)
    out_ref[scores.shape[0] :] = jnp.broadcast_to(k, (PAD, scores.shape[1]))


def sum_scores_kernel(*refs):
    out_ref = refs[-1]
    count = out_ref.shape[0]
    out_ref[...] = tree_sum([restored(ref[:count], ref[count : count + 1]) for ref in refs[:-1]])


SMALL = jnp.float8_e5m2
SMALL_SCALE = 2.0**20


def split(block):
    high = block.astype(jnp.bfloat16)
    return high, ((block - high.astype(jnp.float32)) * SMALL_SCALE).astype(SMALL)


def gram_split_kernel(place_ref, after_ref, gram_ref, *refs, first):
    del after_ref
    outs, (mark_ref, buffer, sems) = refs[:-3], refs[-3:]
    slots, tile, width = buffer.shape
    quarter = outs[0].shape[0]
    steps = quarter // tile
    total = steps * (len(outs) // 2)
    column = pl.multiple_of(place_ref[0] * width, width)
    sub = place_ref[3]

    def copy(i):
        part = first + i // steps
        start = (lax.rem(part // 2 + 1 + sub, 2) * 2 + lax.rem(part, 2)) * quarter + lax.rem(i, steps) * tile
        rows = pl.ds(pl.multiple_of(start, tile), tile)
        slot = lax.rem(i, slots)
        return pltpu.make_async_copy(gram_ref.at[rows, pl.ds(column, width)], buffer.at[slot], sems.at[slot])

    for i in range(min(slots - 1, total)):
        copy(i).start()

    for part in range(len(outs) // 2):

        @pl.loop(0, steps)
        def _(j):
            i = part * steps + j

            @pl.when(i + slots - 1 < total)
            def _():
                copy(i + slots - 1).start()

            copy(i).wait()
            high, low = split(buffer[lax.rem(i, slots)])
            start = pl.multiple_of(j * tile, tile)
            outs[2 * part][pl.ds(start, tile)] = high
            outs[2 * part + 1][pl.ds(start, tile)] = low

    mark_ref[...] = jnp.zeros_like(mark_ref)


def gram_split(place, after, inverse_gram, first, count, tile=128, slots=8):
    rows, width = inverse_gram.shape
    half, quarter = width // 2, rows // 4
    tile = min(tile, quarter)
    *quarters, mark = pl.pallas_call(
        functools.partial(gram_split_kernel, first=first),
        in_specs=[pl.BlockSpec(memory_space=pltpu.SMEM), WHOLE, pl.BlockSpec(memory_space=pltpu.HBM)],
        out_specs=[WHOLE] * (2 * count + 1),
        out_shape=[pltpu.VMEM((quarter, half), kind) for kind in (jnp.bfloat16, SMALL)] * count
        + [jax.ShapeDtypeStruct((8, 128), jnp.float32)],
        scratch_shapes=[pltpu.VMEM((slots, tile, half), jnp.float32), pltpu.SemaphoreType.DMA((slots,))],
        compiler_params=pltpu.CompilerParams(vmem_limit_bytes=12 * MIB),
        cost_estimate=pl.CostEstimate(flops=0, bytes_accessed=count * 4 * quarter * half, transcendentals=0),
        name="gram_split",
    )(place, after, inverse_gram)
    return [pltpu.with_memory_space_constraint(x, pltpu.VMEM) for x in quarters], mark


def gram_rows(group, high_ref, low_ref, terms, small_terms, unit, write):
    queries = small_terms.shape[1]
    part = jnp.dot(high_ref[...], terms[...], preferred_element_type=jnp.float32)
    low = jnp.dot(low_ref[...], small_terms[...], preferred_element_type=jnp.float32)
    done = (part[:, :queries] + part[:, queries:] + low * unit[:1]).T
    for g in range(2):
        write(g ^ group, done[g * (queries // 2) : (g + 1) * (queries // 2)])


def away_kernel(place_ref, after_ref, *refs, row_count, own):
    del after_ref
    grams, sources = refs[:4], refs[4 : 4 + row_count]
    out_ref, terms, small_terms, unit, natural = refs[4 + row_count :]
    group, row, col, sub = (place_ref[i] for i in range(4))
    height, queries, lanes = natural.shape
    for z in range(row_count):
        count = sources[z].shape[0] - PAD
        piece = restored(sources[z][:count], sources[z][count : count + 1])
        for place in range(8):
            s, g, c = place // 4, place // 2 % 2, place % 2
            first = ((((g ^ group) * 2 + (c ^ col)) * 2 + (s ^ sub)) * row_count + (z ^ row)) * own
            for j in range(own):
                start = (place * own + j) * height
                natural[:, pl.ds(first + j, 1), :] = piece[start : start + height].reshape(height, 1, lanes)
    top = jnp.max(jnp.max(jnp.abs(natural[...]), axis=0), axis=1, keepdims=True)
    k = jnp.ceil(jnp.log(jnp.clip(top, 1e-30, 1e30)) * LOG2E)
    k = jnp.broadcast_to(k, (queries, lanes)).T[: unit.shape[0]]
    unit[...] = jnp.exp2(k - 7.0) * (1.0 / SMALL_SCALE)
    factor = jnp.exp2(7.0 - k[:1])
    for a in range(height):
        block = natural[a]
        high = block.astype(jnp.bfloat16).astype(jnp.float32)
        both = jnp.concatenate([high, block - high], 0).T
        terms[a * lanes : (a + 1) * lanes] = both.astype(jnp.bfloat16)
        small_terms[a * lanes : (a + 1) * lanes] = (both[:, :queries] * factor).astype(SMALL)
    for i in range(2):

        def write(g, value):
            out_ref[i, g] = value

        gram_rows(group, *grams[2 * i : 2 * i + 2], terms, small_terms, unit, write)


def home_kernel(place_ref, high_ref, low_ref, terms_ref, small_ref, unit_ref, *refs):
    out_ref = refs[-1]

    def write(g, value):
        out_ref[g] = value

    gram_rows(place_ref[0], high_ref, low_ref, terms_ref, small_ref, unit_ref, write)


def join_kernel(early_ref, early_got_ref, late_ref, late_got_ref, early_out, early_wire, late_out, late_wire):
    early = early_ref[...] + early_got_ref[...].astype(jnp.float32)
    early_out[...] = early
    early_wire[...] = early.astype(jnp.bfloat16)
    late_out[...] = late_ref[0] + late_got_ref[0]
    late_wire[...] = (late_ref[1] + late_got_ref[1]).astype(jnp.bfloat16)


def gram_product(place, after, quarters, sources, own, lanes):
    quarter, half = quarters[0].shape
    row_count = len(sources)
    queries = 8 * row_count * own
    index = pl.BlockSpec(memory_space=pltpu.SMEM)

    def common(count):
        return dict(
            compiler_params=pltpu.CompilerParams(vmem_limit_bytes=8 * MIB),
            cost_estimate=pl.CostEstimate(
                flops=8 * count * queries * quarter * half, bytes_accessed=count * quarter * half, transcendentals=0
            ),
        )

    away, *terms = pl.pallas_call(
        functools.partial(away_kernel, row_count=row_count, own=own),
        in_specs=[index] + [WHOLE] * (5 + row_count),
        out_specs=[WHOLE] * 4,
        out_shape=[
            jax.ShapeDtypeStruct((2, 2, queries // 2, quarter), jnp.float32),
            jax.ShapeDtypeStruct((half, 2 * queries), jnp.bfloat16),
            jax.ShapeDtypeStruct((half, queries), SMALL),
            jax.ShapeDtypeStruct((PAD, queries), jnp.float32),
        ],
        scratch_shapes=[pltpu.VMEM((half // lanes, queries, lanes), jnp.float32)],
        name="away",
        **common(2),
    )(place, after, *quarters[:4], *sources)
    got = swapped(away, "sub")

    def home(i, *after):
        return pl.pallas_call(
            home_kernel,
            in_specs=[index] + [WHOLE] * (5 + len(after)),
            out_specs=WHOLE,
            out_shape=jax.ShapeDtypeStruct((2, queries // 2, quarter), jnp.float32),
            name="home",
            **common(1),
        )(place, *quarters[4 + 2 * i : 6 + 2 * i], *terms, *after)

    early = home(0) + got[0]
    wire = early[1].astype(jnp.bfloat16)
    late = home(1, wire)
    shape = (queries // 2, quarter)
    early, early_wire, late, late_wire = pl.pallas_call(
        join_kernel,
        in_specs=[WHOLE] * 4,
        out_specs=[WHOLE] * 4,
        out_shape=[jax.ShapeDtypeStruct(shape, kind) for kind in (jnp.float32, jnp.bfloat16) * 2],
        compiler_params=pltpu.CompilerParams(vmem_limit_bytes=4 * MIB),
        name="join",
    )(early[0], swapped(wire, "groups"), late, got[1])
    late = late + swapped(late_wire, "groups").astype(jnp.float32)
    early = early + swapped(early_wire, "col").astype(jnp.float32)
    late = late + swapped(late.astype(jnp.bfloat16), "col").astype(jnp.float32)
    return jnp.concatenate([early, late], 1)


def others(pick, axis):
    size = lax.axis_size(axis)
    index = lax.axis_index(axis)
    return [lax.ppermute(pick(index ^ k), axis, [(i, i ^ k) for i in range(size)]) for k in range(1, size)]


def tree_sum(terms):
    while len(terms) > 1:
        terms = [terms[i] + terms[i + 1] for i in range(0, len(terms), 2)]
    return terms[0]


def swapped(array, axis):
    return others(lambda d: array, axis)[0]


def peers(pick):
    return [lax.ppermute(pick(k), ("groups", "col"), [(i, i ^ k) for i in range(4)]) for k in (1, 2, 3)]


def call(kernel, shapes, name, *args, specs=None, scratch=()):
    specs = specs or [pl.BlockSpec(memory_space=pltpu.SMEM) if a.dtype == jnp.int32 else WHOLE for a in args]
    many = isinstance(shapes, list)
    shapes = [jax.ShapeDtypeStruct(shape, jnp.float32) for shape in (shapes if many else [shapes])]
    outs = pl.pallas_call(
        kernel,
        in_specs=specs,
        out_specs=[WHOLE] * len(shapes),
        out_shape=shapes,
        scratch_shapes=list(scratch),
        compiler_params=pltpu.CompilerParams(vmem_limit_bytes=4 * MIB),
        name=name,
    )(*args)
    return outs if many else outs[0]


def body(query_acts, query_grads, proj_in, proj_out, inverse_gram, store_slab):
    row_count = lax.axis_size("row")
    place = jnp.stack([lax.axis_index(axis) for axis in ("groups", "row", "col", "sub")])
    queries, tokens = query_acts.shape[:2]
    own = queries // row_count
    in_width, out_width = proj_in.shape[1], proj_out.shape[1]
    got = []
    for targets in (range(row_count)[: row_count // 2 - 1 : -1], range(row_count)[: row_count // 2][::-1]):
        parts = project(targets, row_count, place, query_acts, query_grads, proj_in, proj_out)
        for k, part in zip(targets, parts):
            if k:
                got.append(lax.ppermute(part.astype(jnp.float16), "row", [(i, i ^ k) for i in range(row_count)]))
    quarters, mark = gram_split(place, parts[-1], inverse_gram, 0, 2)
    height = own * in_width // 8
    near = call(
        functools.partial(kron_kernel, tokens=tokens),
        [(2, height, out_width)] * 4,
        "kron",
        place,
        mark,
        parts[-1],
        *[x.astype(jnp.float32) for x in got],
        scratch=[pltpu.VMEM((own, in_width, out_width), jnp.float32)],
    )
    third, mark = gram_split(place, near[0], inverse_gram, 2, 1)
    near = [near[0]] + peers(lambda k: near[k])
    got = swapped(call(gather_kernel, (4, height, out_width), "gather", mark, *near), "sub")
    packed = call(pack_kernel, (8 * height + PAD, out_width), "pack", *near, got)
    wire = packed.astype(jnp.float16)
    sources = [packed] + [got.astype(jnp.float32) for got in others(lambda d: wire, "row")]
    fourth, mark = gram_split(place, packed, inverse_gram, 3, 1)
    total = gram_product(place, mark, quarters + third + fourth, sources, own, out_width)
    high = lax.reduce_precision(total, 8, 7)
    terms = jnp.concatenate([high, total - high], 0).astype(jnp.bfloat16)
    scores = lax.dot_general(
        terms, store_slab, (((1,), (1,)), ((), ())), preferred_element_type=jnp.float32
    )
    scores = scores[: total.shape[0]] + scores[total.shape[0] :]
    scores = scores + swapped(scores, "sub")
    packed = call(pack_scores_kernel, (scores.shape[0] + PAD, scores.shape[1]), "pack_scores", scores)
    packed = lax.reduce_precision(packed, 5, 10)
    wire = packed.astype(jnp.float16)
    sources = [packed] + [got.astype(jnp.float32) for got in others(lambda d: wire, "row")]
    return call(sum_scores_kernel, scores.shape, "sum_scores", *sources)


def solution(mesh):
    shape = mesh.shape
    rows = shape["row"]
    paired = shape["groups"] == shape["col"] == shape["sub"] == 2 and rows & (rows - 1) == 0

    def chosen(query_acts, query_grads, proj_in, proj_out, *rest):
        queries = query_acts.shape[0] // (shape["groups"] * shape["col"] * shape["sub"])
        square = proj_in.shape[1] == proj_out.shape[1] == 128
        chosen_body = body if paired and square and queries % rows == 0 else plain_body
        return jax.shard_map(
            chosen_body,
            mesh=mesh,
            in_specs=(
                P(("groups", "col", "sub"), None, "row"),
                P(("groups", "col", "sub"), None, "row"),
                P("row", None),
                P("row", None),
                P("row", ("col", "sub")),
                P(("groups", "col"), ("row", "sub")),
            ),
            out_specs=P("groups", "col"),
            check_vma=False,
        )(query_acts, query_grads, proj_in, proj_out, *rest)

    return chosen
```
